32 devices in a mesh: dp: 8 (over z, x), tensor: 4 (over y, core).
Axes of the slice: x: 2, y: 2, z: 4, core: 2. Of those that a mesh axis runs over, the one named last changes fastest.
Arguments:
- layer_input_stream: float32 [16, 736, 1152], P('dp', 'tensor'), may hold values from -70 to 70
- cotangent: float32 [16, 736, 1152], P('dp', 'tensor'), may hold values from -6 to 6
- valid_len: int32 [16], P('dp'), may hold values from 589 to 736
- attention_norm_pair: float32 [2, 1152], replicated, may hold values from -2 to 2
- qkv_weight: float32 [1152, 3, 1152], P('dp', None, 'tensor'), may hold values from -0.1875 to 0.1875
- qv_bias: float32 [2, 1152], P(None, 'tensor'), may hold values from -3 to 3
- out_weight: float32 [1152, 1152], P('tensor', 'dp'), may hold values from -0.5 to 0.5
- out_bias: float32 [1152], replicated, may hold values from -2 to 2
- feedforward_norm_pair: float32 [2, 1152], replicated, may hold values from -2 to 2
- up_weight: float32 [1152, 4304], P('dp', 'tensor'), may hold values from -0.1875 to 0.1875
- up_bias: float32 [4304], P('tensor'), may hold values from -3 to 3
- down_weight: float32 [4304, 1152], P('tensor', 'dp'), may hold values from -0.1875 to 0.1875
- down_bias: float32 [1152], replicated, may hold values from -2 to 2
- mom_attn_norm: float32 [2, 1152], replicated, may hold values from -32 to 32
- mom_qkv_weight: float32 [1152, 3, 1152], P('dp', None, 'tensor'), may hold values from -14 to 14
- mom_qv_bias: float32 [2, 1152], P(None, 'tensor'), may hold values from -128 to 128
- mom_out_weight: float32 [1152, 1152], P('tensor', 'dp'), may hold values from -32 to 32
- mom_out_bias: float32 [1152], replicated, may hold values from -64 to 64
- mom_mlp_norm: float32 [2, 1152], replicated, may hold values from -96 to 96
- mom_up_weight: float32 [1152, 4304], P('dp', 'tensor'), may hold values from -40 to 40
- mom_up_bias: float32 [4304], P('tensor'), may hold values from -40 to 40
- mom_down_weight: float32 [4304, 1152], P('tensor', 'dp'), may hold values from -40 to 40
- mom_down_bias: float32 [1152], replicated, may hold values from -64 to 64
- var_attn_norm: float32 [2, 1152], replicated, may hold values from 11.776 to 588.8
- var_qkv_weight: float32 [1152, 3, 1152], P('dp', None, 'tensor'), may hold values from 1.1776 to 58.88
- var_qv_bias: float32 [2, 1152], P(None, 'tensor'), may hold values from 23.552 to 11776
- var_out_weight: float32 [1152, 1152], P('tensor', 'dp'), may hold values from 23.552 to 1177.6
- var_out_bias: float32 [1152], replicated, may hold values from 58.88 to 2355.2
- var_mlp_norm: float32 [2, 1152], replicated, may hold values from 117.76 to 5888
- var_up_weight: float32 [1152, 4304], P('dp', 'tensor'), may hold values from 23.552 to 1177.6
- var_up_bias: float32 [4304], P('tensor'), may hold values from 23.552 to 1177.6
- var_down_weight: float32 [4304, 1152], P('tensor', 'dp'), may hold values from 11.776 to 588.8
- var_down_bias: float32 [1152], replicated, may hold values from 58.88 to 2355.2
Outputs:
- block_out: float32 [16, 736, 1152], P('dp', 'tensor')
- grad_input: float32 [16, 736, 1152], P('dp', 'tensor')
- grad_attn_norm: float32 [2, 1152], replicated
- grad_qkv_weight: float32 [1152, 3, 1152], P('dp', None, 'tensor')
- grad_qv_bias: float32 [2, 1152], P(None, 'tensor')
- grad_out_weight: float32 [1152, 1152], P('tensor', 'dp')
- grad_out_bias: float32 [1152], replicated
- grad_mlp_norm: float32 [2, 1152], replicated
- grad_up_weight: float32 [1152, 4304], P('dp', 'tensor')
- grad_up_bias: float32 [4304], P('tensor')
- grad_down_weight: float32 [4304, 1152], P('tensor', 'dp')
- grad_down_bias: float32 [1152], replicated
- new_attn_norm: float32 [2, 1152], replicated
- new_qkv_weight: float32 [1152, 3, 1152], P('dp', None, 'tensor')
- new_qv_bias: float32 [2, 1152], P(None, 'tensor')
- new_out_weight: float32 [1152, 1152], P('tensor', 'dp')
- new_out_bias: float32 [1152], replicated
- new_mlp_norm: float32 [2, 1152], replicated
- new_up_weight: float32 [1152, 4304], P('dp', 'tensor')
- new_up_bias: float32 [4304], P('tensor')
- new_down_weight: float32 [4304, 1152], P('tensor', 'dp')
- new_down_bias: float32 [1152], replicated
- newmom_attn_norm: float32 [2, 1152], replicated
- newmom_qkv_weight: float32 [1152, 3, 1152], P('dp', None, 'tensor')
- newmom_qv_bias: float32 [2, 1152], P(None, 'tensor')
- newmom_out_weight: float32 [1152, 1152], P('tensor', 'dp')
- newmom_out_bias: float32 [1152], replicated
- newmom_mlp_norm: float32 [2, 1152], replicated
- newmom_up_weight: float32 [1152, 4304], P('dp', 'tensor')
- newmom_up_bias: float32 [4304], P('tensor')
- newmom_down_weight: float32 [4304, 1152], P('tensor', 'dp')
- newmom_down_bias: float32 [1152], replicated
- newvar_attn_norm: float32 [2, 1152], replicated
- newvar_qkv_weight: float32 [1152, 3, 1152], P('dp', None, 'tensor')
- newvar_qv_bias: float32 [2, 1152], P(None, 'tensor')
- newvar_out_weight: float32 [1152, 1152], P('tensor', 'dp')
- newvar_out_bias: float32 [1152], replicated
- newvar_mlp_norm: float32 [2, 1152], replicated
- newvar_up_weight: float32 [1152, 4304], P('dp', 'tensor')
- newvar_up_bias: float32 [4304], P('tensor')
- newvar_down_weight: float32 [4304, 1152], P('tensor', 'dp')
- newvar_down_bias: float32 [1152], replicated
The draws below stay inside these ranges and needn't reach their ends.
Inputs may be any that keep to these rules, and one draw needn't show every extreme that they name: Positions below an image's valid_len are real patch tokens, the others padding.
All inputs are finite; a program needn't handle non-finite values.
Results may differ from the reference program's by a relative error of at most 0.0095.
Values may be sent and summed in bfloat16 or wider, within the bound.
A program may use at most 192 MiB of HBM per device.

```python
import math
import jax
import jax.numpy as jnp
from jax import lax

D = 1152
HEADS = 16
HEAD_DIM = 72
FF = 4304
SEQ = 736
STEP = 4
IMAGES = 16


def draw_layer_input_stream(key, part):
    rows = jax.random.uniform(jax.random.fold_in(key, 21), (IMAGES, SEQ, 1), jnp.float32, 0.0, 1.0)
    cols = jax.random.uniform(jax.random.fold_in(key, 22), (1, 1, D), jnp.float32, 0.0, 1.0)
    scale = jnp.exp(math.log(3.0) * (2.0 * rows - 1.0)) * jnp.exp(math.log(10.0) * cols - math.log(3.0))
    noise = jnp.clip(jax.random.normal(jax.random.fold_in(key, 23), (IMAGES, SEQ, D), jnp.float32), -6.0, 6.0)
    return scale * noise


def norm_pair(key):
    norm_gain = 1.0 + 0.5 * jax.random.uniform(jax.random.fold_in(key, 41), (D,), jnp.float32, -1.0, 1.0)
    norm_shift = jnp.clip(0.3 * jax.random.normal(jax.random.fold_in(key, 42), (D,), jnp.float32), -2.0, 2.0)
    return jnp.stack([norm_gain, norm_shift])


def draw_attention_norm_pair(key, part):
    return norm_pair(jax.random.fold_in(key, 51))


def draw_feedforward_norm_pair(key, part):
    return norm_pair(jax.random.fold_in(key, 52))


def with_ends(values, stream_key, smallest, top_value):
    place = [jax.random.randint(jax.random.fold_in(stream_key, axis), (), 0, length) for axis, length in enumerate(values.shape)]
    longest = values.shape.index(max(values.shape))
    neighbour = place[:longest] + [(place[longest] + 1) % values.shape[longest]] + place[longest + 1:]
    return values.at[tuple(place)].set(smallest).at[tuple(neighbour)].set(top_value)


def level_of(own_key, extent, shards, smallest, high):
    gain, own = 1.0, jax.random.fold_in(own_key, 6)
    for axis_at, blocks in shards:
        heights = jnp.exp(jax.random.uniform(jax.random.fold_in(own, axis_at), (blocks,), jnp.float32, smallest / len(shards), high / len(shards)))
        gain = gain * jnp.repeat(heights, extent[axis_at] // blocks).reshape([-1 if axis == axis_at else 1 for axis in range(len(extent))])
    return gain


def centred(key, shape, scale, limit, cuts=(), kind=jnp.bfloat16):
    values = scale * jax.random.normal(key, shape, jnp.float32)
    if cuts:
        values = values * level_of(key, shape, cuts, -0.22, 0.18)
    return jnp.clip(values, -limit, limit).astype(kind)


def setup_inputs(seed: int = 0) -> dict:
    seeds = jax.random.split(jax.random.key(seed), 34)
    layer_input_stream = draw_layer_input_stream(jax.random.fold_in(seeds[33], 71), 0)
    cotangent = centred(seeds[1], (IMAGES, SEQ, D), 1.0, 6.0, ((0, 8), (1, 4)), jnp.float32)
    valid_len = with_ends(jax.random.randint(seeds[2], (IMAGES,), SEQ - SEQ // 5, SEQ + 1), jax.random.fold_in(seeds[2], 1), SEQ - SEQ // 5, SEQ).astype(jnp.int32)
    attention_norm_pair = draw_attention_norm_pair(jax.random.fold_in(seeds[33], 71), 0)
    qkv_weight = centred(seeds[4], (D, 3, D), D ** -0.5, 0.1875, ((0, 8), (2, 4)), jnp.float32)
    qv_bias = centred(seeds[5], (2, D), 0.5, 3.0, ((1, 4),), jnp.float32)
    out_weight = centred(seeds[6], (D, D), (max(1, D // 8)) ** -0.5, 0.5, ((0, 4), (1, 8)), jnp.float32)
    out_bias = centred(seeds[7], (D,), 0.3, 2.0, (), jnp.float32)
    feedforward_norm_pair = draw_feedforward_norm_pair(jax.random.fold_in(seeds[33], 71), 0)
    up_weight = centred(seeds[9], (D, FF), D ** -0.5, 0.1875, ((0, 8), (1, 4)), jnp.float32)
    up_bias = centred(seeds[10], (FF,), 0.5, 3.0, ((0, 4),), jnp.float32)
    down_weight = centred(seeds[11], (FF, D), (FF // 4) ** -0.5, 0.1875, ((0, 4), (1, 8)), jnp.float32)
    down_bias = centred(seeds[12], (D,), 0.3, 2.0, (), jnp.float32)
    mom_attn_norm = centred(seeds[13], (2, D), (0.05 * (IMAGES * SEQ) ** 0.5), 32.0, (), jnp.float32)
    mom_qkv_weight = centred(seeds[14], (D, 3, D), (0.02 * (IMAGES * SEQ) ** 0.5), 14.0, ((0, 8), (2, 4)), jnp.float32)
    mom_qv_bias = centred(seeds[15], (2, D), (0.2 * (IMAGES * SEQ) ** 0.5), 128.0, ((1, 4),), jnp.float32)
    mom_out_weight = centred(seeds[16], (D, D), (0.05 * (IMAGES * SEQ) ** 0.5), 32.0, ((0, 4), (1, 8)), jnp.float32)
    mom_out_bias = centred(seeds[17], (D,), (0.1 * (IMAGES * SEQ) ** 0.5), 64.0, (), jnp.float32)
    mom_mlp_norm = centred(seeds[18], (2, D), (0.15 * (IMAGES * SEQ) ** 0.5), 96.0, (), jnp.float32)
    mom_up_weight = centred(seeds[19], (D, FF), (0.06 * (IMAGES * SEQ) ** 0.5), 40.0, ((0, 8), (1, 4)), jnp.float32)
    mom_up_bias = centred(seeds[20], (FF,), (0.06 * (IMAGES * SEQ) ** 0.5), 40.0, ((0, 4),), jnp.float32)
    mom_down_weight = centred(seeds[21], (FF, D), (0.06 * (IMAGES * SEQ) ** 0.5), 40.0, ((0, 4), (1, 8)), jnp.float32)
    mom_down_bias = centred(seeds[22], (D,), (0.1 * (IMAGES * SEQ) ** 0.5), 64.0, (), jnp.float32)
    var_attn_norm = jnp.clip(jnp.exp(jax.random.uniform(seeds[23], (2, D), jnp.float32, math.log(11.776), math.log(588.8))), 11.776, 588.8)
    var_qkv_weight = jnp.clip(jnp.exp(math.log(58.88) - 3.912023 * jax.random.uniform(seeds[24], (D, 3, D), jnp.float32) ** level_of(seeds[24], (D, 3, D), ((0, 8), (2, 4)), -0.2, 0.2)), 1.1776, 58.88)
    var_qv_bias = jnp.clip(jnp.exp(math.log(11776.0) - 6.214608 * jax.random.uniform(seeds[25], (2, D), jnp.float32) ** level_of(seeds[25], (2, D), ((1, 4),), -0.2, 0.2)), 23.552, 11776.0)
    var_out_weight = jnp.clip(jnp.exp(math.log(1177.6) - 3.912023 * jax.random.uniform(seeds[26], (D, D), jnp.float32) ** level_of(seeds[26], (D, D), ((0, 4), (1, 8)), -0.2, 0.2)), 23.552, 1177.6)
    var_out_bias = jnp.clip(jnp.exp(jax.random.uniform(seeds[27], (D,), jnp.float32, math.log(58.88), math.log(2355.2))), 58.88, 2355.2)
    var_mlp_norm = jnp.clip(jnp.exp(jax.random.uniform(seeds[28], (2, D), jnp.float32, math.log(117.76), math.log(5888.0))), 117.76, 5888.0)
    var_up_weight = jnp.clip(jnp.exp(math.log(1177.6) - 3.912023 * jax.random.uniform(seeds[29], (D, FF), jnp.float32) ** level_of(seeds[29], (D, FF), ((0, 8), (1, 4)), -0.2, 0.2)), 23.552, 1177.6)
    var_up_bias = jnp.clip(jnp.exp(math.log(1177.6) - 3.912023 * jax.random.uniform(seeds[30], (FF,), jnp.float32) ** level_of(seeds[30], (FF,), ((0, 4),), -0.2, 0.2)), 23.552, 1177.6)
    var_down_weight = jnp.clip(jnp.exp(math.log(588.8) - 3.912023 * jax.random.uniform(seeds[31], (FF, D), jnp.float32) ** level_of(seeds[31], (FF, D), ((0, 4), (1, 8)), -0.2, 0.2)), 11.776, 588.8)
    var_down_bias = jnp.clip(jnp.exp(jax.random.uniform(seeds[32], (D,), jnp.float32, math.log(58.88), math.log(2355.2))), 58.88, 2355.2)
    return {"layer_input_stream": layer_input_stream, "cotangent": cotangent, "valid_len": valid_len, "attention_norm_pair": attention_norm_pair, "qkv_weight": qkv_weight, "qv_bias": qv_bias, "out_weight": out_weight, "out_bias": out_bias, "feedforward_norm_pair": feedforward_norm_pair, "up_weight": up_weight, "up_bias": up_bias, "down_weight": down_weight, "down_bias": down_bias, "mom_attn_norm": mom_attn_norm, "mom_qkv_weight": mom_qkv_weight, "mom_qv_bias": mom_qv_bias, "mom_out_weight": mom_out_weight, "mom_out_bias": mom_out_bias, "mom_mlp_norm": mom_mlp_norm, "mom_up_weight": mom_up_weight, "mom_up_bias": mom_up_bias, "mom_down_weight": mom_down_weight, "mom_down_bias": mom_down_bias, "var_attn_norm": var_attn_norm, "var_qkv_weight": var_qkv_weight, "var_qv_bias": var_qv_bias, "var_out_weight": var_out_weight, "var_out_bias": var_out_bias, "var_mlp_norm": var_mlp_norm, "var_up_weight": var_up_weight, "var_up_bias": var_up_bias, "var_down_weight": var_down_weight, "var_down_bias": var_down_bias}


NORM_EPS = 1e-06
NEG_FILL = -1e+30
BETA_ONE = 0.9
BETA_TWO = 0.95
ADAM_EPS = 1e-08
RATE_MATRIX = 0.01
RATE_VECTOR = 0.1
DECAY = 0.1
GELU_COEF = math.sqrt(2.0 / math.pi)
CUBIC = 0.044715

def rounded(value):
    return lax.optimization_barrier(value.astype(jnp.bfloat16))

def mult(left, right, form):
    return jnp.einsum(form, left.astype(jnp.float32), right.astype(jnp.float32))

def layer_norm_forward(value, norm_gain, norm_shift):
    centered_rows = value - lax.optimization_barrier(jnp.mean(value, axis=-1, keepdims=True))
    spread = lax.optimization_barrier(jnp.mean(centered_rows * centered_rows, axis=-1, keepdims=True))
    inverse_deviation = lax.rsqrt(spread + NORM_EPS)
    standardized_rows = centered_rows * inverse_deviation
    return (standardized_rows, inverse_deviation, standardized_rows * norm_gain + norm_shift)

def layer_norm_backward(normed_gradient, standardized_rows, inverse_deviation, norm_gain):
    standardized_gradient = normed_gradient * norm_gain
    first_average = lax.optimization_barrier(jnp.mean(standardized_gradient, axis=-1, keepdims=True))
    second_average = lax.optimization_barrier(jnp.mean(standardized_gradient * standardized_rows, axis=-1, keepdims=True))
    value_gradient = inverse_deviation * (standardized_gradient - first_average - standardized_rows * second_average)
    gain_shift_gradient = jnp.stack([lax.optimization_barrier(jnp.sum(normed_gradient * standardized_rows, axis=(0, 1))), lax.optimization_barrier(jnp.sum(normed_gradient, axis=(0, 1)))])
    return (value_gradient, gain_shift_gradient)

def gelu_pair(value):
    inner = GELU_COEF * (value + CUBIC * value * value * value)
    tangent = jnp.tanh(inner)
    result = 0.5 * value * (1.0 + tangent)
    slope = 0.5 * (1.0 + tangent) + 0.5 * value * (1.0 - tangent * tangent) * GELU_COEF * (1.0 + 3.0 * CUBIC * value * value)
    return (result, slope)

def masked_scores(query, keys, keep):
    scale = 1.0 / math.sqrt(HEAD_DIM)
    scores = mult(query, keys, 'gqhe,gkhe->ghqk') * scale
    return jnp.where(keep[:, None, None, :], scores, NEG_FILL)

def attend(query, keys, values, keep):
    scores = masked_scores(query, keys, keep)
    top = lax.optimization_barrier(jnp.max(scores, axis=-1, keepdims=True))
    lse = top + jnp.log(lax.optimization_barrier(jnp.sum(jnp.exp(scores - top), axis=-1, keepdims=True)))
    probs = rounded(jnp.exp(scores - lse))
    mixed = rounded(mult(probs, values, 'ghqk,gkhe->gqhe'))
    return (mixed, lse)

def attend_back(query, keys, values, lse, d_mixed, keep):
    scale = 1.0 / math.sqrt(HEAD_DIM)
    probs = jnp.exp(masked_scores(query, keys, keep) - lse)
    d_values = mult(rounded(probs), d_mixed, 'ghqk,gqhe->gkhe')
    d_probs = mult(d_mixed, values, 'gqhe,gkhe->ghqk')
    delta = lax.optimization_barrier(jnp.sum(probs * d_probs, axis=-1, keepdims=True))
    d_scores = rounded(probs * (d_probs - delta) * scale)
    d_query = mult(d_scores, keys, 'ghqk,gkhe->gqhe')
    d_keys = mult(d_scores, query, 'ghqk,gqhe->gkhe')
    return (d_query, d_keys, d_values)

def group_pass(layer_block, cot, lengths, attention_norm_pair, qv_bias, out_bias, feedforward_norm_pair, up_bias, down_bias, qkv16, out16, up16, down16):
    images, seq, width = layer_block.shape
    keep = jnp.arange(seq, dtype=jnp.int32)[None, :] < lengths[:, None]

    def to_heads(value):
        return value.reshape(images, seq, HEADS, HEAD_DIM)
    standardized_rows1, inverse_deviation1, normalized_rows1 = layer_norm_forward(layer_block, attention_norm_pair[0], attention_norm_pair[1])
    h_one = rounded(normalized_rows1)
    proj = mult(h_one, qkv16, 'gsd,dce->gsce')
    query = rounded(proj[:, :, 0] + qv_bias[0])
    keys = rounded(proj[:, :, 1])
    values = rounded(proj[:, :, 2] + qv_bias[1])
    mixed, lse = attend(to_heads(query), to_heads(keys), to_heads(values), keep)
    mixed = mixed.reshape(images, seq, width)
    residual_rows = layer_block + mult(mixed, out16, 'gsd,de->gse') + out_bias
    standardized_rows2, inverse_deviation2, normalized_rows2 = layer_norm_forward(residual_rows, feedforward_norm_pair[0], feedforward_norm_pair[1])
    h_two = rounded(normalized_rows2)
    pre = mult(h_two, up16, 'gsd,df->gsf') + up_bias
    act_val, act_der = gelu_pair(pre)
    act = rounded(act_val)
    block_out = residual_rows + mult(act, down16, 'gsf,fd->gsd') + down_bias
    grad = cot * keep[:, :, None].astype(jnp.float32)
    grad16 = rounded(grad)
    d_down = mult(act, grad16, 'gsf,gsd->fd')
    d_downbias = lax.optimization_barrier(jnp.sum(grad, axis=(0, 1)))
    d_pre = mult(grad16, down16, 'gsd,fd->gsf') * act_der
    d_upbias = lax.optimization_barrier(jnp.sum(d_pre, axis=(0, 1)))
    d_pre16 = rounded(d_pre)
    d_up = mult(h_two, d_pre16, 'gsd,gsf->df')
    second_gradient = mult(d_pre16, up16, 'gsf,df->gsd')
    residual_norm_gradient, feedforward_norm_gradient = layer_norm_backward(second_gradient, standardized_rows2, inverse_deviation2, feedforward_norm_pair[0])
    d_resid = grad + residual_norm_gradient
    d_outbias = lax.optimization_barrier(jnp.sum(d_resid, axis=(0, 1)))
    d_resid16 = rounded(d_resid)
    d_outw = mult(mixed, d_resid16, 'gse,gsd->ed')
    d_mixed = rounded(mult(d_resid16, out16, 'gsd,ed->gse'))
    d_query, d_keys, d_values = attend_back(to_heads(query), to_heads(keys), to_heads(values), lse, to_heads(d_mixed), keep)
    d_query = d_query.reshape(images, seq, width)
    d_keys = d_keys.reshape(images, seq, width)
    d_values = d_values.reshape(images, seq, width)
    d_qvbias = jnp.stack([lax.optimization_barrier(jnp.sum(d_query, axis=(0, 1))), lax.optimization_barrier(jnp.sum(d_values, axis=(0, 1)))])
    d_proj16 = rounded(jnp.stack([d_query, d_keys, d_values], axis=2))
    d_qkv = mult(h_one, d_proj16, 'gsd,gsce->dce')
    first_gradient = mult(d_proj16, qkv16, 'gsce,dce->gsd')
    norm_input_gradient, attention_norm_gradient = layer_norm_backward(first_gradient, standardized_rows1, inverse_deviation1, attention_norm_pair[0])
    grad_input = d_resid + norm_input_gradient
    grads = (attention_norm_gradient, d_qkv, d_qvbias, d_outw, d_outbias, feedforward_norm_gradient, d_up, d_upbias, d_down, d_downbias)
    return (block_out, grad_input, grads)

def adamw(param, grad, mom, var, rate, decay):
    mom_new = BETA_ONE * mom + (1.0 - BETA_ONE) * grad
    var_new = BETA_TWO * var + (1.0 - BETA_TWO) * grad * grad
    mom_hat = mom_new / (1.0 - BETA_ONE ** STEP)
    var_hat = var_new / (1.0 - BETA_TWO ** STEP)
    change = mom_hat / (jnp.sqrt(var_hat) + ADAM_EPS)
    return (param - rate * (change + decay * param), mom_new, var_new)

def reference(layer_input_stream, cotangent, valid_len, attention_norm_pair, qkv_weight, qv_bias, out_weight, out_bias, feedforward_norm_pair, up_weight, up_bias, down_weight, down_bias, mom_attn_norm, mom_qkv_weight, mom_qv_bias, mom_out_weight, mom_out_bias, mom_mlp_norm, mom_up_weight, mom_up_bias, mom_down_weight, mom_down_bias, var_attn_norm, var_qkv_weight, var_qv_bias, var_out_weight, var_out_bias, var_mlp_norm, var_up_weight, var_up_bias, var_down_weight, var_down_bias):
    params = (attention_norm_pair, qkv_weight, qv_bias, out_weight, out_bias, feedforward_norm_pair, up_weight, up_bias, down_weight, down_bias)
    moms = (mom_attn_norm, mom_qkv_weight, mom_qv_bias, mom_out_weight, mom_out_bias, mom_mlp_norm, mom_up_weight, mom_up_bias, mom_down_weight, mom_down_bias)
    varis = (var_attn_norm, var_qkv_weight, var_qv_bias, var_out_weight, var_out_bias, var_mlp_norm, var_up_weight, var_up_bias, var_down_weight, var_down_bias)
    qkv16 = rounded(qkv_weight)
    out16 = rounded(out_weight)
    up16 = rounded(up_weight)
    down16 = rounded(down_weight)
    images = layer_input_stream.shape[0]
    group = 4 if images % 4 == 0 else 1
    count = images // group

    def shaped(value):
        return value.reshape((count, group) + value.shape[1:])

    def scan_step(carry, item):
        layer_block, cot, lengths = item
        out_g, din_g, grads = group_pass(layer_block, cot, lengths, attention_norm_pair, qv_bias, out_bias, feedforward_norm_pair, up_bias, down_bias, qkv16, out16, up16, down16)
        carry = tuple((total + part for total, part in zip(carry, grads)))
        return (carry, (out_g, din_g))
    init = tuple((jnp.zeros(p.shape, jnp.float32) for p in params))
    grads, (outs_g, dins_g) = lax.scan(scan_step, init, (shaped(layer_input_stream), shaped(cotangent), shaped(valid_len)))
    block_out = outs_g.reshape(layer_input_stream.shape)
    grad_input = dins_g.reshape(layer_input_stream.shape)
    matrix_flags = (False, True, False, True, False, False, True, False, True, False)
    news, newmoms, newvars = ([], [], [])
    for param, grad, mom, var, flag in zip(params, grads, moms, varis, matrix_flags):
        rate = RATE_MATRIX if flag else RATE_VECTOR
        decay = DECAY if flag else 0.0
        new_p, new_m, new_v = adamw(param, grad, mom, var, rate, decay)
        news.append(new_p)
        newmoms.append(new_m)
        newvars.append(new_v)
    return (block_out, grad_input, grads[0], grads[1], grads[2], grads[3], grads[4], grads[5], grads[6], grads[7], grads[8], grads[9], news[0], news[1], news[2], news[3], news[4], news[5], news[6], news[7], news[8], news[9], newmoms[0], newmoms[1], newmoms[2], newmoms[3], newmoms[4], newmoms[5], newmoms[6], newmoms[7], newmoms[8], newmoms[9], newvars[0], newvars[1], newvars[2], newvars[3], newvars[4], newvars[5], newvars[6], newvars[7], newvars[8], newvars[9])
```

```python
import functools
import math
import types

import jax
import jax.numpy as jnp
from jax import lax
from jax.experimental import pallas as pl
from jax.experimental.pallas import tpu as pltpu
from jax.sharding import PartitionSpec as P

HEAD_DIM = 72
STEP = 4

NORM_EPS = 1e-06
NEG_FILL = -1e30
BETA_ONE = 0.9
BETA_TWO = 0.95
ADAM_EPS = 1e-08
RATE_MATRIX = 0.01
RATE_VECTOR = 0.1
DECAY = 0.1
GELU_COEF = math.sqrt(2.0 / math.pi)
CUBIC = 0.044715

NEAR = 2
FAR = 4
GROUPS = NEAR * FAR
RANKS = 4
LANES = 128
SCALE = 1.0 / math.sqrt(HEAD_DIM)
SCALE_TWO = SCALE * math.log2(math.e)
VMEM_BYTES = 63 * 2**20

MESH = pl.DeviceIdType.MESH
BF = jnp.bfloat16
F32 = jnp.float32
NN = (((1,), (0,)), ((), ()))
NT = (((1,), (1,)), ((), ()))
TN = (((0,), (0,)), ((), ()))


def dot(left, right, dims):
    return lax.dot_general(left, right, dims, preferred_element_type=F32)


def rows_at(start, size, unit=16):
    return pl.ds(pl.multiple_of(start, unit), size)


def standardize(value):
    centered_rows = value - jnp.mean(value, axis=-1, keepdims=True)
    spread = jnp.mean(centered_rows * centered_rows, axis=-1, keepdims=True)
    inverse_deviation = lax.rsqrt(spread + NORM_EPS)
    return centered_rows * inverse_deviation, inverse_deviation


def norm_backward(normed_gradient, rows, inverse_deviation, gain):
    g = normed_gradient * gain
    first_average = jnp.mean(g, axis=-1, keepdims=True)
    second_average = jnp.mean(g * rows, axis=-1, keepdims=True)
    return inverse_deviation * (g - first_average - rows * second_average)


def column_sum(value):
    return jnp.sum(value, axis=0, keepdims=True)


def gelu_pair(value):
    inner = GELU_COEF * (value + CUBIC * value * value * value)
    tangent = jnp.tanh(inner)
    result = 0.5 * value * (1.0 + tangent)
    slope = 0.5 * (1.0 + tangent) + 0.5 * value * (1.0 - tangent * tangent) * GELU_COEF * (
        1.0 + 3.0 * CUBIC * value * value
    )
    return (result, slope)


def padded_slab(value, slab):
    rows, width = value.shape
    if slab > rows:
        value = jnp.concatenate([value, jnp.zeros((slab - rows, width), value.dtype)], axis=0)
    return value.astype(BF)


class Place:
    def __init__(self, extra):
        dp, self.t = lax.axis_index("dp"), lax.axis_index("tensor")
        t = self.t
        group = dp // extra
        sub = dp - group * extra
        self.far = group // NEAR
        self.near = group - self.far * NEAR
        row = t // 2
        core = t - 2 * row
        self.t_core = t + 1 - 2 * core
        self.t_row = t + 2 - 4 * row
        self.t_both = 3 - t
        self.core_peer = (dp, self.t_core)
        self.row_peer = (dp, self.t_row)
        self.both_peer = (dp, self.t_both)

        def at(far, near):
            return ((far * NEAR + near) * extra + sub, t)

        self.near_peer = at(self.far, 1 - self.near)
        self.far_peers = [at(self.far_at(o), self.near) for o in range(1, FAR)]

    def far_at(self, offset):
        return lax.rem(self.far + (offset + FAR), FAR)

    def greet(self, both=False):
        peers = [self.core_peer, self.row_peer, self.near_peer] + self.far_peers
        if both:
            peers.append(self.both_peer)
        barrier = pltpu.get_barrier_semaphore()
        for peer in peers:
            pl.semaphore_signal(barrier, inc=1, device_id=peer, device_id_type=MESH)
        pl.semaphore_wait(barrier, len(peers))


def remote(src, dst, send, recv, peer):
    return pltpu.make_async_remote_copy(
        src_ref=src, dst_ref=dst, send_sem=send, recv_sem=recv, device_id=peer, device_id_type=MESH
    )


def slab_rows(cfg, image, rank):
    return rows_at(image * cfg.tokens + rank * cfg.slab, cfg.slab)


class TokenGather:
    def __init__(self, cfg, place, buf, send, recv, image):
        def copy(j, rank, peer):
            part = buf.at[slab_rows(cfg, image, rank)]
            return remote(part, part, send.at[image, j], recv.at[image, j], peer)

        self.core = copy(0, place.t, place.core_peer)
        self.row = copy(1, place.t, place.row_peer)
        self.relay = copy(2, place.t_row, place.core_peer)

    def start(self):
        self.row.start()
        self.core.start()

    def forward(self):
        self.row.wait_recv()
        self.relay.start()

    def wait(self):
        self.core.wait_recv()
        self.relay.wait_recv()

    def finish(self):
        self.core.wait_send()
        self.row.wait_send()
        self.relay.wait_send()


class TokenScatter:
    def __init__(self, place, image, got_core, got_row, out_row, sems):
        core_send, core_recv, row_send, row_recv = sems
        self.place, self.image = place, image
        self.got_core, self.got_row, self.out_row = got_core, got_row, out_row
        self.sems = sems

    def to_core(self, j, src):
        core_send, core_recv, _, _ = self.sems
        i = self.image
        return remote(
            src, self.got_core.at[i, j], core_send.at[i, j], core_recv.at[i, j], self.place.core_peer
        )

    def to_row(self):
        _, _, row_send, row_recv = self.sems
        i = self.image
        return remote(
            self.out_row.at[i], self.got_row.at[i], row_send.at[i], row_recv.at[i], self.place.row_peer
        )

    def run(self, calc, out_core, keep):
        place, i = self.place, self.image
        out_core[i, 0] = calc(place.t_both).astype(BF)
        self.first = self.to_core(0, out_core.at[i, 0])
        self.first.start()
        keep[0] = calc(place.t_row)
        out_core[i, 1] = calc(place.t_core).astype(BF)
        self.second = self.to_core(1, out_core.at[i, 1])
        self.second.start()
        self.first.wait_recv()
        self.out_row[i] = (keep[0] + self.got_core[i, 0].astype(F32)).astype(BF)
        self.row = self.to_row()
        self.row.start()
        keep[1 + i] = calc(place.t)

    def send_parts(self, cfg, parts):
        place, i = self.place, self.image
        self.first = self.to_core(0, parts.at[slab_rows(cfg, i, place.t_both)])
        self.second = self.to_core(1, parts.at[slab_rows(cfg, i, place.t_core)])
        self.first.start()
        self.second.start()

    def pass_parts(self, cfg, parts):
        i = self.image
        self.first.wait_recv()
        mine = parts[slab_rows(cfg, i, self.place.t_row), :].astype(F32)
        self.out_row[i] = (mine + self.got_core[i, 0].astype(F32)).astype(BF)
        self.row = self.to_row()
        self.row.start()

    def total(self, own):
        self.second.wait_recv()
        self.row.wait_recv()
        i = self.image
        return own + self.got_core[i, 1].astype(F32) + self.got_row[i].astype(F32)

    def finish(self):
        self.first.wait_send()
        self.second.wait_send()
        self.row.wait_send()


class WeightGather:
    def __init__(self, cfg, place, own, full, sems, w):
        far_send, far_recv, near_send, near_recv = sems
        self.own, self.full = own, full
        block = cfg.block

        def rows(offset, near):
            return rows_at((place.far_at(offset) * NEAR + near) * block, block)

        self.here = rows(0, place.near)
        src = full.at[self.here]
        self.fars = [
            remote(src, src, far_send.at[w, o], far_recv.at[w, o], place.far_peers[o])
            for o in range(FAR - 1)
        ]
        self.nears = []
        for k in range(FAR):
            part = full.at[rows(-k, place.near)]
            self.nears.append(remote(part, part, near_send.at[w, k], near_recv.at[w, k], place.near_peer))

    def start(self):
        self.full[self.here, :] = self.own[...]
        for copy in self.fars:
            copy.start()
        self.nears[0].start()

    def forward(self, which=None):
        for o in range(FAR - 1) if which is None else which:
            self.fars[o].wait_recv()
            self.nears[o + 1].start()

    def wait(self):
        for copy in self.nears:
            copy.wait_recv()

    def finish(self):
        for copy in self.fars + self.nears:
            copy.wait_send()


class WeightScatter:
    def __init__(self, cfg, place, part, got_near, got_far, sems, w):
        far_send, far_recv, near_send, near_recv = sems
        block = cfg.block
        self.place, self.part, self.got_near, self.got_far = place, part, got_near, got_far

        def rows(offset, near):
            return rows_at((place.far_at(offset) * NEAR + near) * block, block)

        self.rows = rows
        self.nears = [
            remote(
                part.at[rows(o, 1 - place.near)],
                got_near.at[o],
                near_send.at[w, o],
                near_recv.at[w, o],
                place.near_peer,
            )
            for o in range(FAR)
        ]
        self.fars = [
            remote(
                got_near.at[o],
                got_far.at[o - 1],
                far_send.at[w, o - 1],
                far_recv.at[w, o - 1],
                place.far_peers[o - 1],
            )
            for o in range(1, FAR)
        ]

    def start(self):
        for o in list(range(1, FAR)) + [0]:
            self.nears[o].start()

    def forward(self, which=None):
        for o in range(1, FAR) if which is None else which:
            self.nears[o].wait_recv()
            mine = self.part[self.rows(o, self.place.near), :].astype(F32)
            self.got_near[o] = (mine + self.got_near[o].astype(F32)).astype(BF)
            self.fars[o - 1].start()

    def total(self):
        self.nears[0].wait_recv()
        value = self.part[self.rows(0, self.place.near), :].astype(F32) + self.got_near[0].astype(F32)
        for o in range(1, FAR):
            self.fars[o - 1].wait_recv()
            value = value + self.got_far[o - 1].astype(F32)
        return value

    def finish(self):
        for copy in self.fars + self.nears:
            copy.wait_send()


def split_heads(cfg, proj, which, out, image, at, size):
    for h in range(cfg.heads):
        start = which * cfg.head_cols + h * HEAD_DIM
        out[h, rows_at(image * cfg.tokens + at, size), :HEAD_DIM] = proj[
            :, start : start + HEAD_DIM
        ].astype(BF)


def attend_forward(cfg, image, head, q, k, v, mixed, lse):
    rows = rows_at(image * cfg.tokens, cfg.tokens)
    values = v[head, rows, :].astype(F32).T.astype(BF)[:HEAD_DIM]
    scores = dot(k[head, rows, :], q[head, rows, :], NT)
    top = jnp.max(scores, axis=0, keepdims=True)
    probs = jnp.exp2((scores - top) * SCALE_TWO)
    total = jnp.sum(probs, axis=0, keepdims=True)
    out = dot(values, probs.astype(BF), NN) * (1.0 / total)
    mixed[rows, head * HEAD_DIM : (head + 1) * HEAD_DIM] = out.T.astype(BF)
    lse[head, image : image + 1, :] = top * SCALE_TWO + jnp.log2(total)


def attend_backward(cfg, image, head, q, k, v, d_mixed, lse, d_proj, bias_sums):
    rows = rows_at(image * cfg.tokens, cfg.tokens)
    keys, query, d_out = k[head, rows, :], q[head, rows, :], d_mixed[head]
    keys_t = keys.astype(F32).T.astype(BF)[:HEAD_DIM]
    scores = dot(keys, query, NT)
    probs = jnp.exp2(scores * SCALE_TWO - lse[head, image : image + 1, :])
    d_values = dot(probs.astype(BF), d_out, NN)[:, :HEAD_DIM]
    d_probs = dot(v[head, rows, :], d_out, NT)
    delta = jnp.sum(probs * d_probs, axis=0, keepdims=True)
    d_scores = (probs * (d_probs - delta)).astype(BF)
    d_keys = dot(d_scores, query, NN)[:, :HEAD_DIM] * SCALE
    d_query = (dot(keys_t, d_scores, NN) * SCALE).T
    for which, value in ((0, d_query), (1, d_keys), (2, d_values)):
        start = which * cfg.head_cols + head * HEAD_DIM
        d_proj[rows, start : start + HEAD_DIM] = value.astype(BF)
    for row, value in ((0, d_query), (1, d_values)):
        bias_sums[row : row + 1, head * HEAD_DIM : (head + 1) * HEAD_DIM] += column_sum(value)


def keep_row_mask(cfg, place, length):
    at = lax.broadcasted_iota(jnp.int32, (cfg.seq, 1), 0) + place.t * cfg.seq
    return (at < length).astype(F32)


def key_bias(cfg, length):
    index = lax.broadcasted_iota(jnp.int32, (cfg.tokens, 1), 0)
    rank = jnp.zeros_like(index)
    for r in range(1, RANKS):
        rank = rank + (index >= r * cfg.slab).astype(jnp.int32)
    within = index - rank * cfg.slab
    at = rank * cfg.seq + within
    return jnp.where((within < cfg.seq) & (at < length), 0.0, NEG_FILL)


def forward_kernel(cfg, names, *refs):
    r = types.SimpleNamespace(**dict(zip(names, refs)))
    place = Place(cfg.extra)
    images = range(cfg.images)
    half = cfg.tokens // 2
    gather_sems = (r.wg_far_s, r.wg_far_r, r.wg_near_s, r.wg_near_r)
    scatter_sems = (r.ws_far_s, r.ws_far_r, r.ws_near_s, r.ws_near_r)
    outs = []

    def copy_out(src, dst):
        copy = pltpu.make_async_copy(src, dst, r.out_sem.at[len(outs)])
        copy.start()
        outs.append(copy)
        return copy

    place.greet()
    g_qkv = WeightGather(cfg, place, r.own_qkv, r.w_qkv, gather_sems, 0)
    g_out = WeightGather(cfg, place, r.own_out, r.w_out, gather_sems, 1)
    g_up = WeightGather(cfg, place, r.own_up, r.w_up, gather_sems, 2)
    g_down = WeightGather(cfg, place, r.own_down, r.w_down, gather_sems, 3)
    g_qkv.start()

    one = [TokenGather(cfg, place, r.h_one, r.tg_s.at[0], r.tg_r.at[0], i) for i in images]
    cot = [TokenGather(cfg, place, r.grad, r.tg_s.at[1], r.tg_r.at[1], i) for i in images]
    two = [TokenGather(cfg, place, r.h_two, r.tg_s.at[2], r.tg_r.at[2], i) for i in images]
    for i in images:
        rows, _ = standardize(r.x[i])
        value = rows * r.norm_one[0:1, :] + r.norm_one[1:2, :]
        r.h_one[slab_rows(cfg, i, place.t), :] = padded_slab(value, cfg.slab)
        one[i].start()
    bias_total = jnp.zeros((1, cfg.width), F32)
    for i in images:
        value = r.cotangent[i] * keep_row_mask(cfg, place, r.lengths[i])
        bias_total = bias_total + column_sum(value)
        r.grad[slab_rows(cfg, i, place.t), :] = padded_slab(value, cfg.slab)
    r.d_down_bias[...] = bias_total

    lane = lax.broadcasted_iota(jnp.int32, (cfg.tokens, LANES), 1)
    flag = jnp.where(lane == HEAD_DIM, 1.0, 0.0)
    for i in images:
        rows = rows_at(i * cfg.tokens, cfg.tokens)
        bias = jnp.where(lane == HEAD_DIM, key_bias(cfg, r.lengths[i]), 0.0).astype(BF)
        for h in range(cfg.heads):
            r.q[h, rows, :] = flag.astype(BF)
            r.k[h, rows, :] = bias
            r.v[h, rows, :] = jnp.zeros((cfg.tokens, LANES), BF)

    one[0].forward()
    g_qkv.forward()
    g_out.start()
    g_up.start()
    for i in images[1:]:
        one[i].forward()
    for i in images:
        cot[i].start()
    g_qkv.wait()

    def project(i):
        one[i].wait()

        @pl.loop(0, 2)
        def _(j):
            at = pl.multiple_of(j * half, 16)
            value = r.h_one[rows_at(i * cfg.tokens + at, half), :]
            proj = dot(value, r.w_qkv[...], NN)
            bias = r.qv_bias[...]
            hc = cfg.head_cols
            split_heads(cfg, proj[:, :hc] + bias[0:1, :], 0, r.q, i, at, half)
            split_heads(cfg, proj[:, hc : 2 * hc], 0, r.k, i, at, half)
            split_heads(cfg, proj[:, 2 * hc :] + bias[1:2, :], 0, r.v, i, at, half)

    sums = [
        TokenScatter(place, i, r.ts_core, r.ts_row, r.ts_row_out, (r.tsa_cs, r.tsa_cr, r.tsa_rs, r.tsa_rr))
        for i in images
    ]
    for i in images:
        project(i)
        for h in range(cfg.heads):
            attend_forward(cfg, i, h, r.q, r.k, r.v, r.mixed, r.lse)
            if i == 0 and h == 1:
                g_out.forward()
                cot[0].forward()
            if i == 0 and h == 3:
                for c in cot[1:]:
                    c.forward()
            if i == 1 and h == 1:
                g_up.forward()
                g_down.start()
        if i == 0:
            g_out.wait()
            copy_out(r.w_out, r.w_out_hbm)
        sums[i].run(
            lambda rank: dot(r.mixed[slab_rows(cfg, i, rank), :], r.w_out[...], NT), r.ts_core_out, r.keep
        )
    h_one_copy = copy_out(r.h_one, r.h_one_hbm)
    copy_out(r.w_qkv, r.w_qkv_hbm)
    copy_out(r.q, r.q_hbm)
    copy_out(r.k, r.k_hbm)
    copy_out(r.v, r.v_hbm)
    copy_out(r.mixed, r.mixed_hbm)

    for i in images:
        attn = sums[i].total(r.keep[1 + i])[: cfg.seq]
        value = r.x[i] + attn + r.out_bias[...]
        r.resid[i] = value
        rows, _ = standardize(value)
        value = rows * r.norm_two[0:1, :] + r.norm_two[1:2, :]
        r.h_two[slab_rows(cfg, i, place.t), :] = padded_slab(value, cfg.slab)
        two[i].start()
    for s in sums:
        s.finish()
    g_up.wait()

    def unit_block(i, rank):
        rows = slab_rows(cfg, i, rank)
        pre = dot(r.h_two[rows, :], r.w_up[...], NN) + r.up_bias[...]
        value, slope = gelu_pair(pre)
        r.act[rows, :] = value.astype(BF)
        r.slope[rows, :] = slope

    for i in images:
        unit_block(i, place.t)
        two[i].core.wait_recv()
        unit_block(i, place.t_core)
        two[i].forward()
        unit_block(i, place.t_row)
        two[i].relay.wait_recv()
        unit_block(i, place.t_both)
        if i == 0:
            g_down.forward()
    copy_out(r.h_two, r.h_two_hbm)

    for c in cot:
        c.wait()
        c.finish()
    third = cfg.width // 3

    @pl.loop(0, 3)
    def _(j):
        cols = pl.ds(pl.multiple_of(j * third, LANES), third)
        r.d_down_part[rows_at(j * third, third), :] = dot(r.grad[:, cols], r.act[...], TN).astype(BF)

    s_down = WeightScatter(cfg, place, r.d_down_part, r.ws_near, r.ws_far, scatter_sems, 0)
    s_down.start()
    g_down.wait()

    backs = [
        TokenScatter(place, i, r.ts_core, r.ts_row, r.ts_row_out, (r.tsb_cs, r.tsb_cr, r.tsb_rs, r.tsb_rr))
        for i in images
    ]
    r.d_up_bias[...] = jnp.zeros_like(r.d_up_bias)
    for i in images:

        @pl.loop(0, 2)
        def _(j):
            rows = rows_at(i * cfg.tokens + j * half, half)
            d_pre = dot(r.grad[rows, :], r.w_down[...], NN) * r.slope[rows, :]
            r.d_up_bias[...] += column_sum(d_pre)
            r.grad[rows, : cfg.units] = d_pre.astype(BF)

        backs[i].run(
            lambda rank: dot(r.grad[slab_rows(cfg, i, rank), : cfg.units], r.w_up[...], NT),
            r.ts_core_out,
            r.keep,
        )
        if i == 0:
            s_down.forward()
    copy_out(r.grad, r.d_pre_hbm)
    for c in one:
        c.finish()
    h_one_copy.wait()
    for i in images:

        @pl.loop(0, 2)
        def _(j):
            rows = rows_at(i * cfg.tokens + j * half, half)
            r.h_one[rows, :] = dot(r.act[rows, :], r.w_down[...], NT).astype(BF)

    copy_out(r.h_one, r.mlp_hbm)
    for i in images:
        r.d_two[i] = backs[i].total(r.keep[1 + i])[: cfg.seq]
    r.d_down[...] = s_down.total()

    for copy in outs:
        if copy is not h_one_copy:
            copy.wait()
    for item in backs + two + [g_qkv, g_out, g_up, g_down, s_down]:
        item.finish()


def spread(kernel, cfg, inputs, outputs, scratch, collective_id, cost):
    names = list(inputs) + list(outputs) + list(scratch)
    space = {"v": pltpu.VMEM, "s": pltpu.SMEM, "h": pl.ANY}
    result = pl.pallas_call(
        functools.partial(kernel, cfg, names),
        out_shape=tuple(jax.ShapeDtypeStruct(shape, dtype) for _, shape, dtype in outputs.values()),
        in_specs=[pl.BlockSpec(memory_space=space[where]) for where, _ in inputs.values()],
        out_specs=tuple(pl.BlockSpec(memory_space=space[where]) for where, _, _ in outputs.values()),
        scratch_shapes=list(scratch.values()),
        compiler_params=pltpu.CompilerParams(
            collective_id=collective_id, has_side_effects=True, vmem_limit_bytes=VMEM_BYTES
        ),
        cost_estimate=pl.CostEstimate(flops=cost, bytes_accessed=cost // 1000, transcendentals=0),
    )(*[value for _, value in inputs.values()])
    return dict(zip(outputs, result))


def dma(*shape):
    return pltpu.SemaphoreType.DMA(shape)


def call_forward(cfg, inputs):
    all_tokens = cfg.images * cfg.tokens
    w, u, hc, n = cfg.width, cfg.units, cfg.head_cols, cfg.images
    heads = (cfg.heads, all_tokens, LANES)
    local = (n, cfg.seq, w)
    outputs = dict(
        h_one_hbm=("h", (all_tokens, w), BF),
        h_two_hbm=("h", (all_tokens, w), BF),
        q_hbm=("h", heads, BF),
        k_hbm=("h", heads, BF),
        v_hbm=("h", heads, BF),
        mixed_hbm=("h", (all_tokens, hc), BF),
        w_qkv_hbm=("h", (w, 3 * hc), BF),
        w_out_hbm=("h", (w, hc), BF),
        d_pre_hbm=("h", (all_tokens, w), BF),
        mlp_hbm=("h", (all_tokens, w), BF),
        lse=("v", (cfg.heads, n, cfg.tokens), F32),
        resid=("v", local, F32),
        d_two=("v", local, F32),
        d_down=("v", (cfg.block, u), F32),
        d_up_bias=("v", (1, u), F32),
        d_down_bias=("v", (1, w), F32),
    )
    scratch = dict(
        w_qkv=pltpu.VMEM((w, 3 * hc), BF),
        w_out=pltpu.VMEM((w, hc), BF),
        w_up=pltpu.VMEM((w, u), BF),
        w_down=pltpu.VMEM((w, u), BF),
        h_one=pltpu.VMEM((all_tokens, w), BF),
        h_two=pltpu.VMEM((all_tokens, w), BF),
        grad=pltpu.VMEM((all_tokens, w), BF),
        q=pltpu.VMEM(heads, BF),
        k=pltpu.VMEM(heads, BF),
        v=pltpu.VMEM(heads, BF),
        mixed=pltpu.VMEM((all_tokens, hc), BF),
        act=pltpu.VMEM((all_tokens, u), BF),
        slope=pltpu.VMEM((all_tokens, u), F32),
        ts_core=pltpu.VMEM((n, 2, cfg.slab, w), BF),
        ts_row=pltpu.VMEM((n, cfg.slab, w), BF),
        ts_core_out=pltpu.VMEM((n, 2, cfg.slab, w), BF),
        ts_row_out=pltpu.VMEM((n, cfg.slab, w), BF),
        keep=pltpu.VMEM((1 + n, cfg.slab, w), F32),
        d_down_part=pltpu.VMEM((w, u), BF),
        ws_near=pltpu.VMEM((FAR, cfg.block, u), BF),
        ws_far=pltpu.VMEM((FAR - 1, cfg.block, u), BF),
        wg_far_s=dma(4, FAR - 1),
        wg_far_r=dma(4, FAR - 1),
        wg_near_s=dma(4, FAR),
        wg_near_r=dma(4, FAR),
        ws_far_s=dma(1, FAR - 1),
        ws_far_r=dma(1, FAR - 1),
        ws_near_s=dma(1, FAR),
        ws_near_r=dma(1, FAR),
        tg_s=dma(3, n, 3),
        tg_r=dma(3, n, 3),
        tsa_cs=dma(n, 2),
        tsa_cr=dma(n, 2),
        tsa_rs=dma(n),
        tsa_rr=dma(n),
        tsb_cs=dma(n, 2),
        tsb_cr=dma(n, 2),
        tsb_rs=dma(n),
        tsb_rr=dma(n),
        out_sem=dma(16),
    )
    return spread(forward_kernel, cfg, inputs, outputs, scratch, 0, 30 * 10**9)


class VectorSum:
    def __init__(self, place, far, near, rank, send, recv):
        self.place, self.far, self.near, self.rank = place, far, near, rank
        mine = far.at[place.far]
        self.fars = [remote(mine, mine, send.at[o], recv.at[o], place.far_peers[o]) for o in range(FAR - 1)]
        mine = near.at[place.near]
        at = FAR - 1
        self.nears = [remote(mine, mine, send.at[at], recv.at[at], place.near_peer)]
        mine = rank.at[place.t]
        self.ranks = []
        for peer in (place.core_peer, place.row_peer, place.both_peer):
            at += 1
            self.ranks.append(remote(mine, mine, send.at[at], recv.at[at], peer))

    def start(self, value):
        self.far[self.place.far] = value
        for copy in self.fars:
            copy.start()

    def step(self):
        for copy in self.fars:
            copy.wait_recv()
        self.near[self.place.near] = (self.far[0] + self.far[1]) + (self.far[2] + self.far[3])
        self.nears[0].start()

    def last(self):
        self.nears[0].wait_recv()
        self.rank[self.place.t] = self.near[0] + self.near[1]
        for copy in self.ranks:
            copy.start()

    def total(self):
        for copy in self.ranks:
            copy.wait_recv()
        whole = (self.rank[0] + self.rank[1]) + (self.rank[2] + self.rank[3])
        return whole, self.rank[self.place.t]

    def finish(self):
        for copy in self.fars + self.nears + self.ranks:
            copy.wait_send()


def backward_kernel(cfg, names, *refs):
    r = types.SimpleNamespace(**dict(zip(names, refs)))
    place = Place(cfg.extra)
    images = range(cfg.images)
    half = cfg.tokens // 2
    third = cfg.width // 3
    scatter_sems = (r.ws_far_s, r.ws_far_r, r.ws_near_s, r.ws_near_r)
    loads = {}

    def load(name, buf):
        copy = pltpu.make_async_copy(getattr(r, name + "_hbm"), buf, r.in_sem.at[len(loads)])
        copy.start()
        loads[name] = copy

    for name in ("d_pre", "h_two", "mlp", "w_out", "q", "k", "v", "mixed", "w_qkv"):
        load(name, getattr(r, name))
    place.greet(both=True)

    dres = [TokenGather(cfg, place, r.d_res, r.tg_s, r.tg_r, i) for i in images]
    gain_sum = jnp.zeros((1, cfg.width), F32)
    shift_sum = jnp.zeros((1, cfg.width), F32)
    out_bias_sum = jnp.zeros((1, cfg.width), F32)
    for i in images:
        rows, inverse = standardize(r.resid[i])
        d_normed = r.d_two[i]
        grad = r.cotangent[i] * keep_row_mask(cfg, place, r.lengths[i])
        value = grad + norm_backward(d_normed, rows, inverse, r.norm_two[0:1, :])
        r.d_stream[i] = value
        r.d_res[slab_rows(cfg, i, place.t), :] = padded_slab(value, cfg.slab)
        dres[i].start()
        gain_sum = gain_sum + column_sum(d_normed * rows)
        shift_sum = shift_sum + column_sum(d_normed)
        out_bias_sum = out_bias_sum + column_sum(value)
    early = VectorSum(place, r.early_far, r.early_near, r.early_rank, r.early_s, r.early_r)
    pad = jnp.zeros((1, cfg.width - cfg.units % cfg.width), F32) if cfg.units < cfg.width else None
    up_bias_row = r.d_up_bias[...] if pad is None else jnp.concatenate([r.d_up_bias[...], pad], axis=1)
    early.start(
        jnp.concatenate(
            [
                out_bias_sum,
                gain_sum,
                shift_sum,
                r.d_down_bias[...],
                up_bias_row,
                jnp.zeros((3, cfg.width), F32),
            ],
            axis=0,
        )
    )
    r.bias_sums[...] = jnp.zeros_like(r.bias_sums)
    r.d_mixed[...] = jnp.zeros_like(r.d_mixed)

    def weight_part(part, left, right, j):
        cols = pl.ds(pl.multiple_of(j * third, LANES), third)
        columns = part.shape[1]
        part[rows_at(j * third, third), :] = dot(left[:, cols], right[:, :columns], TN).astype(BF)

    loads["d_pre"].wait()
    loads["h_two"].wait()

    @pl.loop(0, 2)
    def _(j):
        weight_part(r.part_up, r.h_two, r.d_pre, j)

    dres[0].forward()
    weight_part(r.part_up, r.h_two, r.d_pre, 2)
    d_proj, h_one = r.h_two, r.d_pre
    load("h_one", h_one)
    s_up = WeightScatter(cfg, place, r.part_up, r.up_near, r.up_far, scatter_sems, 0)
    s_out = WeightScatter(cfg, place, r.part_out, r.out_near, r.out_far, scatter_sems, 1)
    s_qkv = WeightScatter(cfg, place, r.part_qkv, r.qkv_near, r.qkv_far, scatter_sems, 2)
    s_up.start()
    early.step()

    loads["mlp"].wait()
    feeds = [
        TokenScatter(place, i, r.tsa_core, r.tsa_row, r.tsa_row_out, (r.tsa_cs, r.tsa_cr, r.tsa_rs, r.tsa_rr))
        for i in images
    ]
    for i in images:
        feeds[i].send_parts(cfg, r.mlp)
    for c in dres[1:]:
        c.forward()
    for i in images:
        feeds[i].pass_parts(cfg, r.mlp)

    for name in ("w_out", "q", "k", "v", "mixed"):
        loads[name].wait()
    sums = [
        TokenScatter(place, i, r.tsb_core, r.tsb_row, r.tsb_row_out, (r.tsb_cs, r.tsb_cr, r.tsb_rs, r.tsb_rr))
        for i in images
    ]
    dres[0].wait()
    for i in images:

        @pl.loop(0, 2)
        def _(j):
            at = pl.multiple_of(j * half, 16)
            value = dot(r.d_res[rows_at(i * cfg.tokens + at, half), :], r.w_out[...], NN)
            split_heads(cfg, value, 0, r.d_mixed, 0, at, half)

        for h in range(cfg.heads):
            attend_backward(cfg, i, h, r.q, r.k, r.v, r.d_mixed, r.lse, d_proj, r.bias_sums)
            if i == 0 and h == 1:
                early.last()
            if i == 0 and h == 3:
                s_up.forward()
            if i == 1 and h == 1:
                r.early_all[...], r.early_dp[...] = early.total()
            if i == 1 and h == 2:
                for f in images:
                    value = feeds[f].total(r.mlp[slab_rows(cfg, f, place.t), :].astype(F32))
                    r.block_out[f] = r.resid[f] + value[: cfg.seq] + r.down_bias[...]
        if i == 0:
            loads["w_qkv"].wait()
        sums[i].run(
            lambda rank: dot(d_proj[slab_rows(cfg, i, rank), : 3 * cfg.head_cols], r.w_qkv[...], NT),
            r.tsb_core_out,
            r.keep,
        )
        if i == 0:
            for c in dres[1:]:
                c.wait()

            @pl.loop(0, 3)
            def _(j):
                weight_part(r.part_out, r.d_res, r.mixed, j)

            s_out.start()

    loads["h_one"].wait()

    @pl.loop(0, 3)
    def _(j):
        weight_part(r.part_qkv, h_one, d_proj, j)

    s_qkv.start()
    s_out.forward()

    gain_sum = jnp.zeros((1, cfg.width), F32)
    shift_sum = jnp.zeros((1, cfg.width), F32)
    for i in images:
        d_normed = sums[i].total(r.keep[1 + i])[: cfg.seq]
        rows, inverse = standardize(r.x[i])
        r.grad_input[i] = r.d_stream[i] + norm_backward(d_normed, rows, inverse, r.norm_one[0:1, :])
        gain_sum = gain_sum + column_sum(d_normed * rows)
        shift_sum = shift_sum + column_sum(d_normed)
    late = VectorSum(place, r.late_far, r.late_near, r.late_rank, r.late_s, r.late_r)
    pad = jnp.zeros((2, cfg.width - cfg.head_cols), F32)
    late.start(
        jnp.concatenate(
            [
                gain_sum,
                shift_sum,
                jnp.concatenate([r.bias_sums[...], pad], axis=1),
                jnp.zeros((4, cfg.width), F32),
            ],
            axis=0,
        )
    )
    r.d_up[...] = s_up.total()
    late.step()
    s_qkv.forward()
    late.last()
    r.d_out[...] = s_out.total()
    r.late_all[...], r.late_dp[...] = late.total()
    r.d_qkv[...] = s_qkv.total()
    for item in dres + feeds + sums + [s_up, s_out, s_qkv, early, late]:
        item.finish()


def call_backward(cfg, inputs):
    all_tokens = cfg.images * cfg.tokens
    w, u, hc, n = cfg.width, cfg.units, cfg.head_cols, cfg.images
    heads = (cfg.heads, all_tokens, LANES)
    local = (n, cfg.seq, w)
    vec = (8, w)
    outputs = dict(
        block_out=("v", local, F32),
        grad_input=("v", local, F32),
        d_up=("v", (cfg.block, u), F32),
        d_qkv=("v", (cfg.block, 3 * hc), F32),
        d_out=("v", (cfg.block, hc), F32),
        early_all=("v", vec, F32),
        early_dp=("v", vec, F32),
        late_all=("v", vec, F32),
        late_dp=("v", vec, F32),
    )
    scratch = dict(
        d_pre=pltpu.VMEM((all_tokens, w), BF),
        h_two=pltpu.VMEM((all_tokens, w), BF),
        mlp=pltpu.VMEM((all_tokens, w), BF),
        w_out=pltpu.VMEM((w, hc), BF),
        q=pltpu.VMEM(heads, BF),
        k=pltpu.VMEM(heads, BF),
        v=pltpu.VMEM(heads, BF),
        mixed=pltpu.VMEM((all_tokens, hc), BF),
        w_qkv=pltpu.VMEM((w, 3 * hc), BF),
        d_res=pltpu.VMEM((all_tokens, w), BF),
        d_stream=pltpu.VMEM(local, F32),
        d_mixed=pltpu.VMEM((cfg.heads, cfg.tokens, LANES), BF),
        bias_sums=pltpu.VMEM((2, hc), F32),
        tsa_core=pltpu.VMEM((n, 2, cfg.slab, w), BF),
        tsa_row=pltpu.VMEM((n, cfg.slab, w), BF),
        tsa_row_out=pltpu.VMEM((n, cfg.slab, w), BF),
        tsb_core=pltpu.VMEM((n, 2, cfg.slab, w), BF),
        tsb_row=pltpu.VMEM((n, cfg.slab, w), BF),
        tsb_core_out=pltpu.VMEM((n, 2, cfg.slab, w), BF),
        tsb_row_out=pltpu.VMEM((n, cfg.slab, w), BF),
        keep=pltpu.VMEM((1 + n, cfg.slab, w), F32),
        part_up=pltpu.VMEM((w, u), BF),
        part_out=pltpu.VMEM((w, hc), BF),
        part_qkv=pltpu.VMEM((w, 3 * hc), BF),
        up_near=pltpu.VMEM((FAR, cfg.block, u), BF),
        up_far=pltpu.VMEM((FAR - 1, cfg.block, u), BF),
        out_near=pltpu.VMEM((FAR, cfg.block, hc), BF),
        out_far=pltpu.VMEM((FAR - 1, cfg.block, hc), BF),
        qkv_near=pltpu.VMEM((FAR, cfg.block, 3 * hc), BF),
        qkv_far=pltpu.VMEM((FAR - 1, cfg.block, 3 * hc), BF),
        early_far=pltpu.VMEM((FAR,) + vec, F32),
        early_near=pltpu.VMEM((NEAR,) + vec, F32),
        early_rank=pltpu.VMEM((RANKS,) + vec, F32),
        late_far=pltpu.VMEM((FAR,) + vec, F32),
        late_near=pltpu.VMEM((NEAR,) + vec, F32),
        late_rank=pltpu.VMEM((RANKS,) + vec, F32),
        early_s=dma(FAR + 3),
        early_r=dma(FAR + 3),
        late_s=dma(FAR + 3),
        late_r=dma(FAR + 3),
        ws_far_s=dma(3, FAR - 1),
        ws_far_r=dma(3, FAR - 1),
        ws_near_s=dma(3, FAR),
        ws_near_r=dma(3, FAR),
        tg_s=dma(n, 3),
        tg_r=dma(n, 3),
        tsa_cs=dma(n, 2),
        tsa_cr=dma(n, 2),
        tsa_rs=dma(n),
        tsa_rr=dma(n),
        tsb_cs=dma(n, 2),
        tsb_cr=dma(n, 2),
        tsb_rs=dma(n),
        tsb_rr=dma(n),
        in_sem=dma(10),
    )
    return spread(backward_kernel, cfg, inputs, outputs, scratch, 1, 30 * 10**9)


def adamw(param, grad, mom, var, rate, decay):
    mom_new = BETA_ONE * mom + (1.0 - BETA_ONE) * grad
    var_new = BETA_TWO * var + (1.0 - BETA_TWO) * grad * grad
    mom_hat = mom_new / (1.0 - BETA_ONE**STEP)
    var_hat = var_new / (1.0 - BETA_TWO**STEP)
    change = mom_hat / (jnp.sqrt(var_hat) + ADAM_EPS)
    return (param - rate * (change + decay * param), mom_new, var_new)


def per_device(
    layer_input_stream,
    cotangent,
    valid_len,
    attention_norm_pair,
    qkv_weight,
    qv_bias,
    out_weight,
    out_bias,
    feedforward_norm_pair,
    up_weight,
    up_bias,
    down_weight,
    down_bias,
    *moments,
):
    moms, varis = moments[:10], moments[10:]
    images, seq, width = layer_input_stream.shape
    head_cols = qv_bias.shape[1]
    units = up_bias.shape[0]
    slab = -(-seq // 16) * 16
    extra = lax.axis_size("dp") // GROUPS
    cfg = types.SimpleNamespace(
        images=images,
        seq=seq,
        slab=slab,
        tokens=RANKS * slab,
        width=width,
        head_cols=head_cols,
        heads=head_cols // HEAD_DIM,
        units=units,
        block=width // GROUPS,
        extra=extra,
    )
    group = lax.axis_index("dp") // extra
    shard = width // (GROUPS * extra)

    def to_block(value):
        value = value.astype(BF)
        if extra == 1:
            return value
        full = lax.all_gather(value, "dp", axis=0, tiled=True)
        return lax.dynamic_slice_in_dim(full, group * cfg.block, cfg.block, 0)

    def from_block(value):
        if extra == 1:
            return value
        full = jnp.zeros((width,) + value.shape[1:], value.dtype)
        full = lax.dynamic_update_slice_in_dim(full, value, group * cfg.block, 0)
        return lax.psum_scatter(full, "dp", scatter_dimension=0, tiled=True)

    def over_rest(value):
        return value if extra == 1 else lax.psum(value, "dp") * (1.0 / GROUPS)

    forward = call_forward(
        cfg,
        dict(
            x=("v", layer_input_stream),
            cotangent=("v", cotangent),
            lengths=("s", valid_len),
            norm_one=("v", attention_norm_pair),
            norm_two=("v", feedforward_norm_pair),
            qv_bias=("v", qv_bias),
            out_bias=("v", out_bias[None]),
            up_bias=("v", up_bias[None]),
            own_qkv=("v", to_block(qkv_weight.reshape(shard, 3 * head_cols))),
            own_out=("v", to_block(out_weight.T)),
            own_up=("v", to_block(up_weight)),
            own_down=("v", to_block(down_weight.T)),
        ),
    )
    backward = call_backward(
        cfg,
        dict(
            x=("v", layer_input_stream),
            cotangent=("v", cotangent),
            lengths=("s", valid_len),
            norm_one=("v", attention_norm_pair),
            norm_two=("v", feedforward_norm_pair),
            down_bias=("v", down_bias[None]),
            **{
                name: ("v", forward[name])
                for name in ("resid", "d_two", "lse", "d_up_bias", "d_down_bias")
            },
            **{
                name + "_hbm": ("h", forward[name + "_hbm"])
                for name in ("d_pre", "h_two", "mlp", "w_out", "q", "k", "v", "mixed", "w_qkv", "h_one")
            },
        ),
    )
    early_all, early_dp = over_rest(backward["early_all"]), over_rest(backward["early_dp"])
    late_all, late_dp = over_rest(backward["late_all"]), over_rest(backward["late_dp"])
    params = (
        attention_norm_pair,
        qkv_weight,
        qv_bias,
        out_weight,
        out_bias,
        feedforward_norm_pair,
        up_weight,
        up_bias,
        down_weight,
        down_bias,
    )
    grads = (
        late_all[0:2],
        from_block(backward["d_qkv"]).reshape(qkv_weight.shape),
        late_dp[2:4, :head_cols],
        from_block(backward["d_out"]).T,
        early_all[0],
        early_all[1:3],
        from_block(backward["d_up"]),
        early_dp[4, :units],
        from_block(forward["d_down"]).T,
        early_all[3],
    )
    matrix_flags = (False, True, False, True, False, False, True, False, True, False)
    news, newmoms, newvars = ([], [], [])
    for param, gradient, mom, var, flag in zip(params, grads, moms, varis, matrix_flags):
        rate = RATE_MATRIX if flag else RATE_VECTOR
        decay = DECAY if flag else 0.0
        new_p, new_m, new_v = adamw(param, gradient, mom, var, rate, decay)
        news.append(new_p)
        newmoms.append(new_m)
        newvars.append(new_v)
    return (
        backward["block_out"],
        backward["grad_input"],
        *grads,
        *news,
        *newmoms,
        *newvars,
    )


def solution(mesh):
    stream = P("dp", "tensor", None)
    parameters = (
        P(),
        P("dp", None, "tensor"),
        P(None, "tensor"),
        P("tensor", "dp"),
        P(),
        P(),
        P("dp", "tensor"),
        P("tensor"),
        P("tensor", "dp"),
        P(),
    )
    return jax.shard_map(
        per_device,
        mesh=mesh,
        in_specs=(stream, stream, P("dp")) + parameters * 3,
        out_specs=(stream, stream) + parameters * 4,
        check_vma=False,
    )
```

```python
import functools
import math
import types

import jax
import jax.numpy as jnp
from jax import lax
from jax.experimental import pallas as pl
from jax.experimental.pallas import tpu as pltpu
from jax.sharding import PartitionSpec as P

HEAD_DIM = 72
STEP = 4

NORM_EPS = 1e-06
NEG_FILL = -1e30
BETA_ONE = 0.9
BETA_TWO = 0.95
ADAM_EPS = 1e-08
RATE_MATRIX = 0.01
RATE_VECTOR = 0.1
DECAY = 0.1
GELU_COEF = math.sqrt(2.0 / math.pi)
CUBIC = 0.044715

NEAR = 2
FAR = 4
GROUPS = NEAR * FAR
RANKS = 4
LANES = 128
SCALE = 1.0 / math.sqrt(HEAD_DIM)
SCALE_TWO = SCALE * math.log2(math.e)
VMEM_BYTES = 63 * 2**20

MESH = pl.DeviceIdType.MESH
BF = jnp.bfloat16
F32 = jnp.float32
NN = (((1,), (0,)), ((), ()))
NT = (((1,), (1,)), ((), ()))
TN = (((0,), (0,)), ((), ()))


def dot(left, right, dims):
    return lax.dot_general(left, right, dims, preferred_element_type=F32)


def rows_at(start, size, unit=16):
    return pl.ds(pl.multiple_of(start, unit), size)


def standardize(value):
    centered_rows = value - jnp.mean(value, axis=-1, keepdims=True)
    spread = jnp.mean(centered_rows * centered_rows, axis=-1, keepdims=True)
    inverse_deviation = lax.rsqrt(spread + NORM_EPS)
    return centered_rows * inverse_deviation, inverse_deviation


def norm_backward(normed_gradient, rows, inverse_deviation, gain):
    g = normed_gradient * gain
    first_average = jnp.mean(g, axis=-1, keepdims=True)
    second_average = jnp.mean(g * rows, axis=-1, keepdims=True)
    return inverse_deviation * (g - first_average - rows * second_average)


def column_sum(value):
    return jnp.sum(value, axis=0, keepdims=True)


def gelu_pair(value):
    inner = GELU_COEF * (value + CUBIC * value * value * value)
    tangent = jnp.tanh(inner)
    result = 0.5 * value * (1.0 + tangent)
    slope = 0.5 * (1.0 + tangent) + 0.5 * value * (1.0 - tangent * tangent) * GELU_COEF * (
        1.0 + 3.0 * CUBIC * value * value
    )
    return (result, slope)


def padded_slab(value, slab):
    rows, width = value.shape
    if slab > rows:
        value = jnp.concatenate([value, jnp.zeros((slab - rows, width), value.dtype)], axis=0)
    return value.astype(BF)


class Place:
    def __init__(self, extra):
        dp, self.t = lax.axis_index("dp"), lax.axis_index("tensor")
        t = self.t
        group = dp // extra
        sub = dp - group * extra
        self.far = group // NEAR
        self.near = group - self.far * NEAR
        row = t // 2
        core = t - 2 * row
        self.t_core = t + 1 - 2 * core
        self.t_row = t + 2 - 4 * row
        self.t_both = 3 - t
        self.core_peer = (dp, self.t_core)
        self.row_peer = (dp, self.t_row)
        self.both_peer = (dp, self.t_both)

        def at(far, near):
            return ((far * NEAR + near) * extra + sub, t)

        self.near_peer = at(self.far, 1 - self.near)
        self.far_peers = [at(self.far_at(o), self.near) for o in range(1, FAR)]

    def far_at(self, offset):
        return lax.rem(self.far + (offset + FAR), FAR)

    def greet(self, both=False):
        peers = [self.core_peer, self.row_peer, self.near_peer] + self.far_peers
        if both:
            peers.append(self.both_peer)
        barrier = pltpu.get_barrier_semaphore()
        for peer in peers:
            pl.semaphore_signal(barrier, inc=1, device_id=peer, device_id_type=MESH)
        pl.semaphore_wait(barrier, len(peers))


def remote(src, dst, send, recv, peer):
    return pltpu.make_async_remote_copy(
        src_ref=src, dst_ref=dst, send_sem=send, recv_sem=recv, device_id=peer, device_id_type=MESH
    )


def slab_rows(cfg, image, rank):
    return rows_at(image * cfg.tokens + rank * cfg.slab, cfg.slab)


class TokenGather:
    def __init__(self, cfg, place, buf, send, recv, image):
        def copy(j, rank, peer):
            part = buf.at[slab_rows(cfg, image, rank)]
            return remote(part, part, send.at[image, j], recv.at[image, j], peer)

        self.core = copy(0, place.t, place.core_peer)
        self.row = copy(1, place.t, place.row_peer)
        self.relay = copy(2, place.t_row, place.core_peer)
        self.core_here = False

    def start(self):
        self.row.start()
        self.core.start()

    def wait_core(self):
        if not self.core_here:
            self.core.wait_recv()
            self.core_here = True

    def forward(self):
        self.row.wait_recv()
        self.relay.start()

    def wait(self):
        self.wait_core()
        self.relay.wait_recv()

    def finish(self):
        self.core.wait_send()
        self.row.wait_send()
        self.relay.wait_send()


class TokenScatter:
    def __init__(self, place, image, got_core, got_row, out_row, sems):
        core_send, core_recv, row_send, row_recv = sems
        self.place, self.image = place, image
        self.got_core, self.got_row, self.out_row = got_core, got_row, out_row
        self.sems = sems

    def to_core(self, j, src):
        core_send, core_recv, _, _ = self.sems
        i = self.image
        return remote(
            src, self.got_core.at[i, j], core_send.at[i, j], core_recv.at[i, j], self.place.core_peer
        )

    def to_row(self):
        _, _, row_send, row_recv = self.sems
        i = self.image
        return remote(
            self.out_row.at[i], self.got_row.at[i], row_send.at[i], row_recv.at[i], self.place.row_peer
        )

    def run(self, calc, out_core, keep):
        place, i = self.place, self.image
        out_core[i, 0] = calc(place.t_both).astype(BF)
        self.first = self.to_core(0, out_core.at[i, 0])
        self.first.start()
        keep[0] = calc(place.t_row)
        out_core[i, 1] = calc(place.t_core).astype(BF)
        self.second = self.to_core(1, out_core.at[i, 1])
        self.second.start()
        self.first.wait_recv()
        self.out_row[i] = (keep[0] + self.got_core[i, 0].astype(F32)).astype(BF)
        self.row = self.to_row()
        self.row.start()
        keep[1 + i] = calc(place.t)

    def send_parts(self, cfg, parts):
        place, i = self.place, self.image
        self.first = self.to_core(0, parts.at[slab_rows(cfg, i, place.t_both)])
        self.second = self.to_core(1, parts.at[slab_rows(cfg, i, place.t_core)])
        self.first.start()
        self.second.start()

    def pass_parts(self, cfg, parts):
        i = self.image
        self.first.wait_recv()
        rows = slab_rows(cfg, i, self.place.t_row)
        parts[rows, :] = (parts[rows, :].astype(F32) + self.got_core[i, 0].astype(F32)).astype(BF)
        _, _, row_send, row_recv = self.sems
        self.row = remote(
            parts.at[rows], self.got_row.at[i], row_send.at[i], row_recv.at[i], self.place.row_peer
        )
        self.row.start()

    def total(self, own):
        self.second.wait_recv()
        self.row.wait_recv()
        i = self.image
        return own + self.got_core[i, 1].astype(F32) + self.got_row[i].astype(F32)

    def finish(self):
        self.first.wait_send()
        self.second.wait_send()
        self.row.wait_send()


class WeightGather:
    def __init__(self, cfg, place, full, columns, sems, w):
        far_send, far_recv, near_send, near_recv = sems
        first, last = columns

        def part(offset):
            rows = rows_at((place.far_at(offset) * NEAR + place.near) * cfg.block, cfg.block)
            return full.at[rows, first:last]

        src = part(0)
        self.fars = [
            remote(src, src, far_send.at[w, o], far_recv.at[w, o], place.far_peers[o])
            for o in range(FAR - 1)
        ]
        self.nears = [
            remote(part(-k), part(-k), near_send.at[w, k], near_recv.at[w, k], place.near_peer)
            for k in range(FAR)
        ]

    def start(self):
        for copy in self.fars:
            copy.start()
        self.nears[0].start()

    def forward(self, which=None):
        for o in range(FAR - 1) if which is None else which:
            self.fars[o].wait_recv()
            self.nears[o + 1].start()

    def wait(self):
        for copy in self.nears:
            copy.wait_recv()

    def finish(self):
        for copy in self.fars + self.nears:
            copy.wait_send()


class WeightScatter:
    def __init__(self, cfg, place, part, first, got_near, got_far, sems, w):
        far_send, far_recv, near_send, near_recv = sems
        block = cfg.block
        self.first, self.last = first, first + got_near.shape[2]
        self.place, self.part, self.got_near, self.got_far = place, part, got_near, got_far

        def rows(offset, near):
            return rows_at((place.far_at(offset) * NEAR + near) * block, block)

        self.rows = rows
        self.nears = [
            remote(
                part.at[rows(o, 1 - place.near), self.first : self.last],
                got_near.at[o],
                near_send.at[w, o],
                near_recv.at[w, o],
                place.near_peer,
            )
            for o in range(FAR)
        ]
        self.fars = [
            remote(
                got_near.at[o],
                got_far.at[o - 1],
                far_send.at[w, o - 1],
                far_recv.at[w, o - 1],
                place.far_peers[o - 1],
            )
            for o in range(1, FAR)
        ]

    def start(self):
        for o in list(range(1, FAR)) + [0]:
            self.nears[o].start()

    def forward(self, which=None):
        for o in range(1, FAR) if which is None else which:
            self.nears[o].wait_recv()
            mine = self.part[self.rows(o, self.place.near), self.first : self.last].astype(F32)
            self.got_near[o] = (mine + self.got_near[o].astype(F32)).astype(BF)
            self.fars[o - 1].start()

    def total(self):
        self.nears[0].wait_recv()
        mine = self.part[self.rows(0, self.place.near), self.first : self.last].astype(F32)
        value = mine + self.got_near[0].astype(F32)
        for o in range(1, FAR):
            self.fars[o - 1].wait_recv()
            value = value + self.got_far[o - 1].astype(F32)
        return value

    def finish(self):
        for copy in self.fars + self.nears:
            copy.wait_send()


def split_heads(cfg, value, out, image, at, size):
    for h in range(cfg.heads):
        part = value[:, h * HEAD_DIM : (h + 1) * HEAD_DIM]
        out[h][rows_at(image * cfg.tokens + at, size), :HEAD_DIM] = part.astype(BF)


def attend_forward(cfg, image, head, q, k, v, mixed, lse):
    rows = rows_at(image * cfg.tokens, cfg.tokens)
    values = v[head, rows, :].astype(F32).T.astype(BF)[:HEAD_DIM]
    scores = dot(k[head, rows, :], q[head, rows, :], NT)
    top = jnp.max(scores, axis=0, keepdims=True)
    probs = jnp.exp2((scores - top) * SCALE_TWO)
    total = jnp.sum(probs, axis=0, keepdims=True)
    out = dot(values, probs.astype(BF), NN) * (1.0 / total)
    mixed[rows, head * HEAD_DIM : (head + 1) * HEAD_DIM] = out.T.astype(BF)
    lse[head, image : image + 1, :] = top * SCALE_TWO + jnp.log2(total)


def attend_backward(cfg, image, head, q, k, v, d_mixed, lse, d_proj, bias_sums):
    rows = rows_at(image * cfg.tokens, cfg.tokens)
    keys, query, d_out = k[head, rows, :], q[head, rows, :], d_mixed[head][...]
    keys_t = keys.astype(F32).T.astype(BF)[:HEAD_DIM]
    scores = dot(keys, query, NT)
    probs = jnp.exp2(scores * SCALE_TWO - lse[head, image : image + 1, :])
    d_values = dot(probs.astype(BF), d_out, NN)[:, :HEAD_DIM]
    d_probs = dot(v[head, rows, :], d_out, NT)
    delta = jnp.sum(probs * d_probs, axis=0, keepdims=True)
    d_scores = (probs * (d_probs - delta)).astype(BF)
    d_keys = dot(d_scores, query, NN)[:, :HEAD_DIM] * SCALE
    d_query = (dot(keys_t, d_scores, NN) * SCALE).T
    for which, value in ((0, d_query), (1, d_keys), (2, d_values)):
        start = (3 * head + which) * HEAD_DIM
        d_proj[rows, start : start + HEAD_DIM] = value.astype(BF)
    for row, value in ((0, d_query), (1, d_values)):
        bias_sums[row : row + 1, head * HEAD_DIM : (head + 1) * HEAD_DIM] += column_sum(value)


def keep_row_mask(cfg, place, length):
    at = lax.broadcasted_iota(jnp.int32, (cfg.seq, 1), 0) + place.t * cfg.seq
    return (at < length).astype(F32)


def key_bias(cfg, length):
    index = lax.broadcasted_iota(jnp.int32, (cfg.tokens, 1), 0)
    rank = jnp.zeros_like(index)
    for r in range(1, RANKS):
        rank = rank + (index >= r * cfg.slab).astype(jnp.int32)
    within = index - rank * cfg.slab
    at = rank * cfg.seq + within
    return jnp.where((within < cfg.seq) & (at < length), 0.0, NEG_FILL)


def layer_kernel(cfg, names, *refs):
    r = types.SimpleNamespace(**dict(zip(names, refs)))
    place = Place(cfg.extra)
    images = range(cfg.images)
    heads, units, hc = cfg.heads, cfg.units, cfg.head_cols
    half, third = cfg.tokens // 2, cfg.width // 3
    gather_sems = (r.wg_far_s, r.wg_far_r, r.wg_near_s, r.wg_near_r)
    scatter_sems = (r.ws_far_s, r.ws_far_r, r.ws_near_s, r.ws_near_r)
    q, k, v = (r.qkv.at[pl.ds(n * heads, heads)] for n in range(3))
    own_qkv, own_out, own_up, own_down = r.d_qkv, r.d_out, r.d_up, r.d_down
    resid, cotangent = r.block_out, r.grad_input
    h_one, mlp = r.page_one, r.page_one
    h_two, d_proj = r.page_two, r.page_two
    grad, d_pre, h_one_again = r.page_three, r.page_three, r.page_three
    act = r.page_four
    part_up = r.w_up
    part_down, part_qkv = r.part, r.part
    part_out = r.w_down
    d_mixed = [r.page_four.at[pl.ds(0, cfg.tokens), pl.ds(h * LANES, LANES)] for h in range(heads)]

    def local(src, dst, n):
        copy = pltpu.make_async_copy(src, dst, r.local_sem.at[n])
        copy.start()
        return copy

    load_qkv = local(r.own_qkv_hbm, own_qkv, 0)
    load_x = local(r.x_hbm, r.x, 1)
    load_out = local(r.own_out_hbm, own_out, 2)
    load_up = local(r.own_up_hbm, own_up, 3)
    load_cot = local(r.cotangent_hbm, cotangent, 4)
    load_down = local(r.own_down_hbm, own_down, 5)

    place.greet(both=True)
    middle, most, cut = 4 * LANES, 5 * LANES, 7 * LANES
    ends = [r.w_qkv.shape[1], r.w_out.shape[1], r.w_up.shape[1], r.w_down.shape[1]]
    plan = [
        (r.w_qkv, 0, middle),
        (r.w_qkv, middle, ends[0]),
        (r.w_out, 0, ends[1]),
        (r.w_up, 0, most),
        (r.w_up, most, ends[2]),
        (r.w_down, 0, middle),
        (r.w_down, middle, cut),
        (r.w_down, cut, ends[3]),
    ]
    gathers = [
        WeightGather(cfg, place, full, (first, last), gather_sems, n)
        for n, (full, first, last) in enumerate(plan)
    ]
    g_heads, g_out, g_up, g_down = gathers[0:2], gathers[2], gathers[3:5], gathers[5:8]
    here = rows_at((place.far * NEAR + place.near) * cfg.block, cfg.block)
    load_qkv.wait()
    columns = [own_qkv[n][:, h * HEAD_DIM : (h + 1) * HEAD_DIM] for h in range(heads) for n in range(3)]
    columns.append(jnp.zeros((cfg.block, ends[0] - 3 * hc), own_qkv.dtype))
    r.w_qkv[here, :] = jnp.concatenate(columns, axis=1).astype(BF)
    g_heads[0].start()

    one = [TokenGather(cfg, place, h_one, r.tg_s.at[0], r.tg_r.at[0], i) for i in images]
    cot = [TokenGather(cfg, place, grad, r.tg_s.at[1], r.tg_r.at[1], i) for i in images]
    two = [TokenGather(cfg, place, h_two, r.tg_s.at[2], r.tg_r.at[2], i) for i in images]
    dres = [TokenGather(cfg, place, r.d_res, r.tg_s.at[3], r.tg_r.at[3], i) for i in images]
    load_x.wait()
    for i in images:
        rows, _ = standardize(r.x[i])
        value = rows * r.norm_one[0:1, :] + r.norm_one[1:2, :]
        h_one[slab_rows(cfg, i, place.t), :] = padded_slab(value, cfg.slab)
        one[i].start()

    lane = lax.broadcasted_iota(jnp.int32, (cfg.tokens, LANES), 1)
    flag = jnp.where(lane == HEAD_DIM, 1.0, 0.0)
    for i in images:
        rows = rows_at(i * cfg.tokens, cfg.tokens)
        bias = jnp.where(lane == HEAD_DIM, key_bias(cfg, r.lengths[i]), 0.0).astype(BF)
        for h in range(heads):
            q[h, rows, :] = flag.astype(BF)
            k[h, rows, :] = bias
            v[h, rows, :] = jnp.zeros((cfg.tokens, LANES), BF)

    load_cot.wait()
    down_bias_sum = jnp.zeros((1, cfg.width), F32)
    for i in images:
        value = cotangent[i] * keep_row_mask(cfg, place, r.lengths[i])
        cotangent[i] = value
        down_bias_sum = down_bias_sum + column_sum(value)
        grad[slab_rows(cfg, i, place.t), :] = padded_slab(value, cfg.slab)
    r.vector[3:4, :] = down_bias_sum

    load_out.wait()
    load_up.wait()
    load_down.wait()
    r.w_out[here, :hc] = own_out[...].astype(BF)
    r.w_up[here, :units] = own_up[...].astype(BF)
    r.w_down[here, :units] = own_down[...].astype(BF)

    def advance(n):
        gathers[n].forward([0])
        if n == 0:
            gathers[1].start()
        gathers[n].forward([1, 2])
        if n + 2 < len(gathers):
            gathers[n + 2].start()

    advance(0)
    one[0].forward()
    for i in images[1:]:
        one[i].forward()
    for i in images:
        cot[i].start()
    g_heads[0].wait()

    def project(i, pair):
        @pl.loop(0, 2)
        def _(j):
            at = pl.multiple_of(j * half, 16)
            value = h_one[rows_at(i * cfg.tokens + at, half), :]
            rows = rows_at(i * cfg.tokens + at, half)
            first = pair * 3 * LANES
            proj = dot(value, r.w_qkv[:, first : first + 4 * LANES], NN)
            for h in (2 * pair, 2 * pair + 1):
                bias = r.qv_bias[:, h * HEAD_DIM : (h + 1) * HEAD_DIM]
                for n, out in enumerate((q, k, v)):
                    start = (3 * h + n) * HEAD_DIM - first
                    part = proj[:, start : start + HEAD_DIM]
                    if n != 1:
                        part = part + bias[n // 2 : n // 2 + 1, :]
                    out[h, rows, :HEAD_DIM] = part.astype(BF)

    def scatters(core, row, sems):
        return [TokenScatter(place, i, core, row, r.ts_row_out, sems) for i in images]

    attns = scatters(r.tsa_core, r.tsa_row, (r.ts_cs.at[0], r.ts_cr.at[0], r.ts_rs.at[0], r.ts_rr.at[0]))
    backs = scatters(r.tsa_core, r.tsa_row, (r.ts_cs.at[1], r.ts_cr.at[1], r.ts_rs.at[1], r.ts_rr.at[1]))
    feeds = scatters(r.tsa_core, r.tsa_row, (r.ts_cs.at[2], r.ts_cr.at[2], r.ts_rs.at[2], r.ts_rr.at[2]))
    sums = scatters(r.tsb_core, r.tsb_row, (r.ts_cs.at[3], r.ts_cr.at[3], r.ts_rs.at[3], r.ts_rr.at[3]))
    def pump_forward(i, h):
        if i == 0 and h == 1:
            advance(1)
        if i == 1 and h == 1:
            advance(2)
            g_heads[1].wait()
        if i == 0 and h == 2:
            cot[0].forward()
        if i == 0 and h == 3:
            g_out.wait()
        if i == 1 and h == 2:
            advance(3)

    for pair in range(2):
        for i in images:
            if pair == 0:
                one[i].wait()
            project(i, pair)
            for h in (2 * pair, 2 * pair + 1):
                attend_forward(cfg, i, h, q, k, v, r.mixed, r.lse)
                pump_forward(i, h)
            if pair == 1:
                attns[i].run(
                    lambda rank: dot(r.mixed[slab_rows(cfg, i, rank), :], r.w_out[:, :hc], NT),
                    r.ts_core_out,
                    r.keep,
                )
    spill_h_one = local(h_one, r.h_one_hbm, 6)
    spill_qkv = local(r.qkv, r.qkv_hbm, 7)

    for c in cot[1:]:
        c.forward()
    for i in images:
        attn = attns[i].total(r.keep[1 + i])[: cfg.seq]
        value = r.x[i] + attn + r.out_bias[...][None]
        resid[i] = value
        rows, _ = standardize(value)
        value = rows * r.norm_two[0:1, :] + r.norm_two[1:2, :]
        h_two[slab_rows(cfg, i, place.t), :] = padded_slab(value, cfg.slab)
        two[i].start()
        if i == 0:
            advance(4)
    for item in attns:
        item.finish()
    for g in g_up:
        g.wait()
    advance(5)
    spill_qkv.wait()
    tiles = [(n, min(LANES, units - n * LANES)) for n in range(-(-units // LANES))]

    def unit_block(i, rank):
        rows = slab_rows(cfg, i, rank)
        pre = dot(h_two[rows, :], r.w_up[:, :units], NN) + r.up_bias[...][None]
        value, slope = gelu_pair(pre)
        act[rows, :units] = value.astype(BF)
        for n, size in tiles:
            r.qkv[n, rows, :size] = slope[:, n * LANES : n * LANES + size].astype(BF)

    for i in images:
        unit_block(i, place.t)
        two[i].wait_core()
        unit_block(i, place.t_core)
        two[i].forward()
        unit_block(i, place.t_row)
        two[i].wait()
        unit_block(i, place.t_both)
        advance(6 + i)

    for c in cot:
        c.wait()
        c.finish()

    def weight_part(part, left, right, first=0):
        last = first + right.shape[1]

        @pl.loop(0, 3)
        def _(j):
            cols = pl.ds(pl.multiple_of(j * third, LANES), third)
            part[rows_at(j * third, third), first:last] = dot(left[:, cols], right, TN).astype(BF)

    def weight_scatter(n, part, first, near, far):
        return WeightScatter(cfg, place, part, first, near, far, scatter_sems, n)

    s_down = weight_scatter(0, part_down, 0, r.down_near, r.down_far)
    s_up = weight_scatter(1, part_up, 0, r.up_near, r.up_far)
    s_out = weight_scatter(2, part_out, 0, r.out_near, r.out_far)
    cuts = {1: (0, 3 * LANES), 2: (3 * LANES, 5 * LANES), 3: (5 * LANES, ends[0])}
    s_qkv = {
        h: weight_scatter(2 + h, part_qkv, cuts[h][0], getattr(r, f"qkv_near_{h}"), getattr(r, f"qkv_far_{h}"))
        for h in cuts
    }

    weight_part(part_down, grad, act[:, :units])
    s_down.start()
    r.vector[4:5, :] = jnp.zeros((1, cfg.width), F32)
    parts = [part for part in tiles if part[0] < 7], [part for part in tiles if part[0] >= 7]

    def d_pre_part(i, part):
        first, last = part[0][0] * LANES, part[-1][0] * LANES + part[-1][1]

        @pl.loop(0, 2)
        def _(j):
            rows = rows_at(i * cfg.tokens + j * half, half)
            slope = jnp.concatenate([r.qkv[n, rows, :size] for n, size in part], axis=1)
            value = dot(grad[rows, :], r.w_down[:, first:last], NN) * slope.astype(F32)
            r.vector[4:5, first:last] += column_sum(value)
            for n, size in part:
                start = n * LANES - first
                r.qkv[n, rows, :size] = value[:, start : start + size].astype(BF)

    def d_pre_place(i):
        @pl.loop(0, 2)
        def _(j):
            rows = rows_at(i * cfg.tokens + j * half, half)
            for n, size in tiles:
                d_pre[rows, n * LANES : n * LANES + size] = r.qkv[n, rows, :size]

    g_down[0].wait()
    g_down[1].wait()
    for i in images:
        d_pre_part(i, parts[0])
    g_down[2].wait()
    for i in images:
        d_pre_part(i, parts[1])
        d_pre_place(i)
        backs[i].run(
            lambda rank: dot(d_pre[slab_rows(cfg, i, rank), :units], r.w_up[:, :units], NT),
            r.ts_core_out,
            r.keep,
        )
        s_down.forward([1 + i])
    fetch_qkv = local(r.qkv_hbm, r.qkv, 8)

    def feed(i):
        @pl.loop(0, 2)
        def _(j):
            rows = rows_at(i * cfg.tokens + j * half, half)
            mlp[rows, :] = dot(act[rows, :units], r.w_down[:, :units], NT).astype(BF)

    def through_norm_two(i):
        d_normed = backs[i].total(r.keep[1 + i])[: cfg.seq]
        rows, inverse = standardize(resid[i])
        value = cotangent[i] + norm_backward(d_normed, rows, inverse, r.norm_two[0:1, :])
        r.grad_input[i] = value
        r.d_res[slab_rows(cfg, i, place.t), :] = padded_slab(value, cfg.slab)
        dres[i].start()
        return column_sum(value), column_sum(d_normed * rows), column_sum(d_normed)

    for item in two + gathers:
        item.finish()
    weight_part(part_up, h_two, d_pre[:, :units])
    s_up.start()
    vectors = [through_norm_two(0)]
    s_down.forward([3])
    for c in one:
        c.finish()
    spill_h_one.wait()
    fetch_h_one = local(r.h_one_hbm, h_one_again, 9)
    for i in images:
        feed(i)
    for i in images[1:]:
        vectors.append(through_norm_two(i))
    for item in backs:
        item.finish()
    s_up.forward([1])
    for n in range(3):
        r.vector[n : n + 1, :] = sum(entry[n] for entry in vectors)
    early = VectorSum(place, r.early_far, r.early_near, r.early_rank, r.early_s, r.early_r)
    r.vector[5:8, :] = jnp.zeros((3, cfg.width), F32)
    early.start(r.vector[...])
    r.bias_sums[...] = jnp.zeros_like(r.bias_sums)
    for part in d_mixed:
        part[...] = jnp.zeros((cfg.tokens, LANES), BF)
    for i in images:
        dres[i].wait_core()
        feeds[i].send_parts(cfg, mlp)
    dres[0].forward()
    feeds[0].pass_parts(cfg, mlp)
    fetch_qkv.wait()
    dres[0].wait()

    def qkv_part(h):
        first, last = cuts[h]
        weight_part(part_qkv, h_one_again, d_proj[:, first:last], first)
        s_qkv[h].start()

    for i in images:
        @pl.loop(0, 2)
        def _(j):
            at = pl.multiple_of(j * half, 16)
            value = dot(r.d_res[rows_at(i * cfg.tokens + at, half), :], r.w_out[:, :hc], NN)
            split_heads(cfg, value, d_mixed, 0, at, half)

        for h in range(heads):
            attend_backward(cfg, i, h, q, k, v, d_mixed, r.lse, d_proj, r.bias_sums)
            if i == 0 and h == 0:
                s_up.forward([2])
            if i == 0 and h == 1:
                s_up.forward([3])
            if i == 0 and h == 3:
                dres[1].forward()
            if i == 1 and h == 0:
                r.d_down[...] = s_down.total()[:, :units]
                s_down.finish()
                fetch_h_one.wait()
            if i == 1 and h in (1, 2):
                qkv_part(h)
            if i == 1 and h == 1:
                s_out.forward([1, 2])
            if i == 1 and h == 2:
                s_out.forward([3])
            if i == 1 and h == 3:
                s_qkv[1].forward()
                early.step()
        sums[i].run(
            lambda rank: dot(d_proj[slab_rows(cfg, i, rank), : 3 * hc], r.w_qkv[:, : 3 * hc], NT),
            r.ts_core_out,
            r.keep,
        )
        if i == 0:
            dres[1].wait()
            weight_part(part_out, r.d_res, r.mixed[...])
            s_out.start()
    qkv_part(3)
    early.last()
    feeds[1].pass_parts(cfg, mlp)
    s_qkv[2].forward()

    def finish_block(i):
        value = feeds[i].total(mlp[slab_rows(cfg, i, place.t), :].astype(F32))
        r.block_out[i] = resid[i] + value[: cfg.seq] + r.down_bias[...][None]
        feeds[i].finish()

    finish_block(0)
    r.early_all[...], r.early_dp[...] = early.total()

    gain_sum = jnp.zeros((1, cfg.width), F32)
    shift_sum = jnp.zeros((1, cfg.width), F32)
    for i in images:
        d_normed = sums[i].total(r.keep[1 + i])[: cfg.seq]
        rows, inverse = standardize(r.x[i])
        r.grad_input[i] = r.grad_input[i] + norm_backward(d_normed, rows, inverse, r.norm_one[0:1, :])
        gain_sum = gain_sum + column_sum(d_normed * rows)
        shift_sum = shift_sum + column_sum(d_normed)
    late = VectorSum(place, r.late_far, r.late_near, r.late_rank, r.late_s, r.late_r)
    pad = jnp.zeros((2, cfg.width - hc), F32)
    late.start(
        jnp.concatenate(
            [
                gain_sum,
                shift_sum,
                jnp.concatenate([r.bias_sums[...], pad], axis=1),
                jnp.zeros((4, cfg.width), F32),
            ],
            axis=0,
        )
    )
    s_qkv[3].forward()
    r.d_up[...] = s_up.total()[:, :units]
    r.d_out[...] = s_out.total()[:, :hc]
    late.step()
    late.last()
    finish_block(1)
    r.late_all[...], r.late_dp[...] = late.total()
    value = jnp.concatenate([s_qkv[h].total() for h in cuts], axis=1)
    for h in range(heads):
        for n in range(3):
            start = (3 * h + n) * HEAD_DIM
            r.d_qkv[n, :, h * HEAD_DIM : (h + 1) * HEAD_DIM] = value[:, start : start + HEAD_DIM]
    for item in dres + sums + [s_up, s_out, early, late] + list(s_qkv.values()):
        item.finish()


def spread(kernel, cfg, inputs, outputs, scratch, collective_id, cost):
    names = list(inputs) + list(outputs) + list(scratch)
    space = {"v": pltpu.VMEM, "s": pltpu.SMEM, "h": pl.ANY}
    result = pl.pallas_call(
        functools.partial(kernel, cfg, names),
        out_shape=tuple(jax.ShapeDtypeStruct(shape, dtype) for _, shape, dtype in outputs.values()),
        in_specs=[pl.BlockSpec(memory_space=space[where]) for where, _ in inputs.values()],
        out_specs=tuple(pl.BlockSpec(memory_space=space[where]) for where, _, _ in outputs.values()),
        scratch_shapes=list(scratch.values()),
        compiler_params=pltpu.CompilerParams(
            collective_id=collective_id, has_side_effects=True, vmem_limit_bytes=VMEM_BYTES
        ),
        cost_estimate=pl.CostEstimate(flops=cost, bytes_accessed=cost // 1000, transcendentals=0),
    )(*[value for _, value in inputs.values()])
    return dict(zip(outputs, result))


def dma(*shape):
    return pltpu.SemaphoreType.DMA(shape)


class VectorSum:
    def __init__(self, place, far, near, rank, send, recv):
        self.place, self.far, self.near, self.rank = place, far, near, rank
        mine = far.at[place.far]
        self.fars = [remote(mine, mine, send.at[o], recv.at[o], place.far_peers[o]) for o in range(FAR - 1)]
        mine = near.at[place.near]
        at = FAR - 1
        self.nears = [remote(mine, mine, send.at[at], recv.at[at], place.near_peer)]
        mine = rank.at[place.t]
        self.ranks = []
        for peer in (place.core_peer, place.row_peer, place.both_peer):
            at += 1
            self.ranks.append(remote(mine, mine, send.at[at], recv.at[at], peer))

    def start(self, value):
        self.far[self.place.far] = value
        for copy in self.fars:
            copy.start()

    def step(self):
        for copy in self.fars:
            copy.wait_recv()
        self.near[self.place.near] = (self.far[0] + self.far[1]) + (self.far[2] + self.far[3])
        self.nears[0].start()

    def last(self):
        self.nears[0].wait_recv()
        self.rank[self.place.t] = self.near[0] + self.near[1]
        for copy in self.ranks:
            copy.start()

    def total(self):
        for copy in self.ranks:
            copy.wait_recv()
        whole = (self.rank[0] + self.rank[1]) + (self.rank[2] + self.rank[3])
        return whole, self.rank[self.place.t]

    def finish(self):
        for copy in self.fars + self.nears + self.ranks:
            copy.wait_send()


def call_layer(cfg, inputs):
    all_tokens = cfg.images * cfg.tokens
    w, hc, n = cfg.width, cfg.head_cols, cfg.images
    units_p, hc_p, three_p = (-(-size // LANES) * LANES for size in (cfg.units, hc, 3 * hc))
    qkv = (3 * cfg.heads, all_tokens, LANES)
    local = (n, cfg.seq, w)
    page = (all_tokens, w)
    slabs = (n, cfg.slab, w)
    vec = (8, w)
    outputs = dict(
        block_out=("v", local, F32),
        grad_input=("v", local, F32),
        d_qkv=("v", (3, cfg.block, hc), F32),
        d_out=("v", (cfg.block, hc), F32),
        d_up=("v", (cfg.block, cfg.units), F32),
        d_down=("v", (cfg.block, cfg.units), F32),
        early_all=("v", vec, F32),
        early_dp=("v", vec, F32),
        late_all=("v", vec, F32),
        late_dp=("v", vec, F32),
        h_one_hbm=("h", page, BF),
        qkv_hbm=("h", qkv, BF),
    )
    scratch = dict(
        w_qkv=pltpu.VMEM((w, three_p), BF),
        w_out=pltpu.VMEM((w, hc_p), BF),
        w_up=pltpu.VMEM((w, units_p), BF),
        w_down=pltpu.VMEM((w, units_p), BF),
        x=pltpu.VMEM(local, F32),
        page_one=pltpu.VMEM(page, BF),
        page_two=pltpu.VMEM(page, BF),
        page_three=pltpu.VMEM(page, BF),
        page_four=pltpu.VMEM(page, BF),
        d_res=pltpu.VMEM(page, BF),
        qkv=pltpu.VMEM(qkv, BF),
        mixed=pltpu.VMEM((all_tokens, hc), BF),
        lse=pltpu.VMEM((cfg.heads, n, cfg.tokens), F32),
        bias_sums=pltpu.VMEM((2, hc), F32),
        vector=pltpu.VMEM(vec, F32),
        tsa_core=pltpu.VMEM((n, 2) + slabs[1:], BF),
        tsa_row=pltpu.VMEM(slabs, BF),
        tsb_core=pltpu.VMEM((n, 2) + slabs[1:], BF),
        tsb_row=pltpu.VMEM(slabs, BF),
        ts_core_out=pltpu.VMEM((n, 2) + slabs[1:], BF),
        ts_row_out=pltpu.VMEM(slabs, BF),
        keep=pltpu.VMEM((1 + n,) + slabs[1:], F32),
        part=pltpu.VMEM((w, w), BF),
        down_near=pltpu.VMEM((FAR, cfg.block, units_p), BF),
        down_far=pltpu.VMEM((FAR - 1, cfg.block, units_p), BF),
        up_near=pltpu.VMEM((FAR, cfg.block, units_p), BF),
        up_far=pltpu.VMEM((FAR - 1, cfg.block, units_p), BF),
        out_near=pltpu.VMEM((FAR, cfg.block, hc_p), BF),
        out_far=pltpu.VMEM((FAR - 1, cfg.block, hc_p), BF),
        **{
            f"qkv_{side}_{h}": pltpu.VMEM((count, cfg.block, size), BF)
            for h, size in ((1, 3 * LANES), (2, 2 * LANES), (3, three_p - 5 * LANES))
            for side, count in (("near", FAR), ("far", FAR - 1))
        },
        early_far=pltpu.VMEM((FAR,) + vec, F32),
        early_near=pltpu.VMEM((NEAR,) + vec, F32),
        early_rank=pltpu.VMEM((RANKS,) + vec, F32),
        late_far=pltpu.VMEM((FAR,) + vec, F32),
        late_near=pltpu.VMEM((NEAR,) + vec, F32),
        late_rank=pltpu.VMEM((RANKS,) + vec, F32),
        early_s=dma(FAR + 3),
        early_r=dma(FAR + 3),
        late_s=dma(FAR + 3),
        late_r=dma(FAR + 3),
        wg_far_s=dma(8, FAR - 1),
        wg_far_r=dma(8, FAR - 1),
        wg_near_s=dma(8, FAR),
        wg_near_r=dma(8, FAR),
        ws_far_s=dma(6, FAR - 1),
        ws_far_r=dma(6, FAR - 1),
        ws_near_s=dma(6, FAR),
        ws_near_r=dma(6, FAR),
        tg_s=dma(4, n, 3),
        tg_r=dma(4, n, 3),
        ts_cs=dma(4, n, 2),
        ts_cr=dma(4, n, 2),
        ts_rs=dma(4, n),
        ts_rr=dma(4, n),
        local_sem=dma(10),
    )
    return spread(layer_kernel, cfg, inputs, outputs, scratch, 0, 60 * 10**9)


def adamw(param, grad, mom, var, rate, decay):
    mom_new = BETA_ONE * mom + (1.0 - BETA_ONE) * grad
    var_new = BETA_TWO * var + (1.0 - BETA_TWO) * grad * grad
    mom_hat = mom_new / (1.0 - BETA_ONE**STEP)
    var_hat = var_new / (1.0 - BETA_TWO**STEP)
    change = mom_hat / (jnp.sqrt(var_hat) + ADAM_EPS)
    return (param - rate * (change + decay * param), mom_new, var_new)


MATRICES = {1: "qkv", 3: "out", 6: "up", 8: "down"}


def update_kernel(cfg, *refs):
    params, moms, varis = refs[0:10], refs[10:20], refs[20:30]
    grads = dict(zip(("qkv", "out", "up", "down", "early_all", "early_dp", "late_all", "late_dp"), refs[30:38]))
    streams, outs = refs[38:40], refs[40:]
    for source, target in zip(streams, outs[:2]):
        target[...] = source[...]
    outs = outs[2:]

    def step(n, grad, rate, decay):
        new = adamw(params[n][...], grad, moms[n][...], varis[n][...], rate, decay)
        for kind, value in enumerate((grad,) + new):
            outs[10 * kind + n][...] = value

    for n, name in MATRICES.items():
        step(n, grads[name][...], RATE_MATRIX, DECAY)
    vectors = {
        0: grads["late_all"][0:2, :],
        2: grads["late_dp"][2:4, : cfg.head_cols],
        4: grads["early_all"][0, :],
        5: grads["early_all"][1:3, :],
        7: grads["early_dp"][4, : cfg.units],
        9: grads["early_all"][3, :],
    }
    for n, grad in vectors.items():
        step(n, grad, RATE_VECTOR, 0.0)


def call_update(cfg, shard, params, moms, varis, grads, block_out, grad_input):
    steps = 3 if shard % 24 == 0 and cfg.width % (3 * LANES) == 0 else 1
    rows = shard // steps

    def spec(value, n=None):
        shape = value.shape
        if n == "stream":
            return pl.BlockSpec(shape[:2] + (cfg.width // steps,), lambda i: (0, 0, i))
        if n not in MATRICES:
            zeros = (0,) * len(shape)
            return pl.BlockSpec(shape, lambda i: zeros)
        if len(shape) == 3:
            return pl.BlockSpec((shape[0], rows, shape[2]), lambda i: (0, i, 0))
        return pl.BlockSpec((rows, shape[1]), lambda i: (i, 0))

    order = ("qkv", "out", "up", "down", "early_all", "early_dp", "late_all", "late_dp")
    number = {name: n for n, name in MATRICES.items()}
    values = [*params, *moms, *varis, *(grads[name] for name in order), block_out, grad_input]
    ten = [spec(value, n) for n, value in enumerate(params)]
    in_specs = ten * 3 + [spec(grads[name], number.get(name)) for name in order]
    two = [spec(block_out, "stream"), spec(grad_input, "stream")]
    shapes = [block_out, grad_input] + list(params) * 4
    return pl.pallas_call(
        functools.partial(update_kernel, cfg),
        grid=(steps,),
        out_shape=tuple(jax.ShapeDtypeStruct(value.shape, F32) for value in shapes),
        in_specs=in_specs + two,
        out_specs=tuple(two + ten * 4),
        compiler_params=pltpu.CompilerParams(vmem_limit_bytes=VMEM_BYTES),
    )(*values)


def per_device(
    layer_input_stream,
    cotangent,
    valid_len,
    attention_norm_pair,
    qkv_weight,
    qv_bias,
    out_weight,
    out_bias,
    feedforward_norm_pair,
    up_weight,
    up_bias,
    down_weight,
    down_bias,
    *moments,
):
    moms, varis = moments[:10], moments[10:]
    images, seq, width = layer_input_stream.shape
    head_cols = qv_bias.shape[1]
    units = up_bias.shape[0]
    slab = -(-seq // 16) * 16
    extra = lax.axis_size("dp") // GROUPS
    cfg = types.SimpleNamespace(
        images=images,
        seq=seq,
        slab=slab,
        tokens=RANKS * slab,
        width=width,
        head_cols=head_cols,
        heads=head_cols // HEAD_DIM,
        units=units,
        block=width // GROUPS,
        extra=extra,
    )
    group = lax.axis_index("dp") // extra
    shard = width // (GROUPS * extra)

    def to_block(value, axis=0):
        if extra == 1:
            return value
        full = lax.all_gather(value, "dp", axis=axis, tiled=True)
        return lax.dynamic_slice_in_dim(full, group * cfg.block, cfg.block, axis)

    def from_block(value, axis=0):
        if extra == 1:
            return value
        shape = value.shape[:axis] + (width,) + value.shape[axis + 1 :]
        full = jnp.zeros(shape, value.dtype)
        full = lax.dynamic_update_slice_in_dim(full, value, group * cfg.block, axis)
        return lax.psum_scatter(full, "dp", scatter_dimension=axis, tiled=True)

    def over_rest(value):
        return value if extra == 1 else lax.psum(value, "dp") * (1.0 / GROUPS)

    def turned(values):
        attn, qkv, qv, out, out_b, mlp, up, up_b, down, down_b = values
        return (attn, qkv.transpose(1, 0, 2), qv, out.T, out_b, mlp, up, up_b, down.T, down_b)

    params = turned(
        (
            attention_norm_pair,
            qkv_weight,
            qv_bias,
            out_weight,
            out_bias,
            feedforward_norm_pair,
            up_weight,
            up_bias,
            down_weight,
            down_bias,
        )
    )
    moms, varis = turned(moms), turned(varis)
    layer = call_layer(
        cfg,
        dict(
            x_hbm=("h", layer_input_stream),
            cotangent_hbm=("h", cotangent),
            lengths=("s", valid_len),
            norm_one=("v", attention_norm_pair),
            norm_two=("v", feedforward_norm_pair),
            qv_bias=("v", qv_bias),
            out_bias=("v", out_bias),
            up_bias=("v", up_bias),
            down_bias=("v", down_bias),
            own_qkv_hbm=("h", to_block(params[1], 1)),
            own_out_hbm=("h", to_block(params[3])),
            own_up_hbm=("h", to_block(params[6])),
            own_down_hbm=("h", to_block(params[8])),
        ),
    )
    updated = call_update(
        cfg,
        shard,
        params,
        moms,
        varis,
        dict(
            qkv=from_block(layer["d_qkv"], 1),
            out=from_block(layer["d_out"]),
            up=from_block(layer["d_up"]),
            down=from_block(layer["d_down"]),
            **{
                name: over_rest(layer[name])
                for name in ("early_all", "early_dp", "late_all", "late_dp")
            },
        ),
        layer["block_out"],
        layer["grad_input"],
    )
    streams, rest = updated[:2], updated[2:]
    results = []
    for kind in range(4):
        results.extend(turned(rest[10 * kind : 10 * kind + 10]))
    return (*streams, *results)


def solution(mesh):
    stream = P("dp", "tensor", None)
    parameters = (
        P(),
        P("dp", None, "tensor"),
        P(None, "tensor"),
        P("tensor", "dp"),
        P(),
        P(),
        P("dp", "tensor"),
        P("tensor"),
        P("tensor", "dp"),
        P(),
    )
    return jax.shard_map(
        per_device,
        mesh=mesh,
        in_specs=(stream, stream, P("dp")) + parameters * 3,
        out_specs=(stream, stream) + parameters * 4,
        check_vma=False,
    )
```

```python
import functools
import math
import types

import jax
import jax.numpy as jnp
from jax import lax
from jax.experimental import pallas as pl
from jax.experimental.pallas import tpu as pltpu
from jax.sharding import PartitionSpec as P

HEAD_DIM = 72
STEP = 4

NORM_EPS = 1e-06
NEG_FILL = -1e30
BETA_ONE = 0.9
BETA_TWO = 0.95
ADAM_EPS = 1e-08
RATE_MATRIX = 0.01
RATE_VECTOR = 0.1
DECAY = 0.1
GELU_COEF = math.sqrt(2.0 / math.pi)
CUBIC = 0.044715

NEAR = 2
FAR = 4
GROUPS = NEAR * FAR
RANKS = 4
LANES = 128
SCALE = 1.0 / math.sqrt(HEAD_DIM)
SCALE_TWO = SCALE * math.log2(math.e)
VMEM_BYTES = 63 * 2**20

MESH = pl.DeviceIdType.MESH
BF = jnp.bfloat16
F32 = jnp.float32
NN = (((1,), (0,)), ((), ()))
NT = (((1,), (1,)), ((), ()))
TN = (((0,), (0,)), ((), ()))


def dot(left, right, dims):
    return lax.dot_general(left, right, dims, preferred_element_type=F32)


def rows_at(start, size, unit=16):
    return pl.ds(pl.multiple_of(start, unit), size)


def standardize(value):
    centered_rows = value - jnp.mean(value, axis=-1, keepdims=True)
    spread = jnp.mean(centered_rows * centered_rows, axis=-1, keepdims=True)
    inverse_deviation = lax.rsqrt(spread + NORM_EPS)
    return centered_rows * inverse_deviation, inverse_deviation


def norm_backward(normed_gradient, rows, inverse_deviation, gain):
    g = normed_gradient * gain
    first_average = jnp.mean(g, axis=-1, keepdims=True)
    second_average = jnp.mean(g * rows, axis=-1, keepdims=True)
    return inverse_deviation * (g - first_average - rows * second_average)


def column_sum(value):
    return jnp.sum(value, axis=0, keepdims=True)


def gelu_pair(value):
    inner = GELU_COEF * (value + CUBIC * value * value * value)
    tangent = jnp.tanh(inner)
    result = 0.5 * value * (1.0 + tangent)
    slope = 0.5 * (1.0 + tangent) + 0.5 * value * (1.0 - tangent * tangent) * GELU_COEF * (
        1.0 + 3.0 * CUBIC * value * value
    )
    return (result, slope)


def padded_slab(value, slab):
    rows, width = value.shape
    if slab > rows:
        value = jnp.concatenate([value, jnp.zeros((slab - rows, width), value.dtype)], axis=0)
    return value.astype(BF)


class Place:
    def __init__(self, extra):
        dp, self.t = lax.axis_index("dp"), lax.axis_index("tensor")
        t = self.t
        group = dp // extra
        sub = dp - group * extra
        self.far = group // NEAR
        self.near = group - self.far * NEAR
        row = t // 2
        core = t - 2 * row
        self.t_core = t + 1 - 2 * core
        self.t_row = t + 2 - 4 * row
        self.t_both = 3 - t
        self.core_peer = (dp, self.t_core)
        self.row_peer = (dp, self.t_row)
        self.both_peer = (dp, self.t_both)

        def at(far, near):
            return ((far * NEAR + near) * extra + sub, t)

        self.near_peer = at(self.far, 1 - self.near)
        self.far_peers = [at(self.far_at(o), self.near) for o in range(1, FAR)]

    def far_at(self, offset):
        return lax.rem(self.far + (offset + FAR), FAR)

    def greet(self, both=False):
        peers = [self.core_peer, self.row_peer, self.near_peer] + self.far_peers
        if both:
            peers.append(self.both_peer)
        barrier = pltpu.get_barrier_semaphore()
        for peer in peers:
            pl.semaphore_signal(barrier, inc=1, device_id=peer, device_id_type=MESH)
        pl.semaphore_wait(barrier, len(peers))


def remote(src, dst, send, recv, peer):
    return pltpu.make_async_remote_copy(
        src_ref=src, dst_ref=dst, send_sem=send, recv_sem=recv, device_id=peer, device_id_type=MESH
    )


def slab_rows(cfg, image, rank):
    return rows_at(image * cfg.tokens + rank * cfg.slab, cfg.slab)


class TokenGather:
    def __init__(self, cfg, place, buf, send, recv, image):
        def copy(j, rank, peer):
            part = buf.at[slab_rows(cfg, image, rank)]
            return remote(part, part, send.at[image, j], recv.at[image, j], peer)

        self.core = copy(0, place.t, place.core_peer)
        self.row = copy(1, place.t, place.row_peer)
        self.relay = copy(2, place.t_row, place.core_peer)
        self.core_here = False

    def start(self):
        self.row.start()
        self.core.start()

    def wait_core(self):
        if not self.core_here:
            self.core.wait_recv()
            self.core_here = True

    def forward(self):
        self.row.wait_recv()
        self.relay.start()

    def wait(self):
        self.wait_core()
        self.relay.wait_recv()

    def finish(self):
        self.core.wait_send()
        self.row.wait_send()
        self.relay.wait_send()


class TokenScatter:
    def __init__(self, place, image, got_core, got_row, out_row, sems):
        core_send, core_recv, row_send, row_recv = sems
        self.place, self.image = place, image
        self.got_core, self.got_row, self.out_row = got_core, got_row, out_row
        self.sems = sems

    def to_core(self, j, src):
        core_send, core_recv, _, _ = self.sems
        i = self.image
        return remote(
            src, self.got_core.at[i, j], core_send.at[i, j], core_recv.at[i, j], self.place.core_peer
        )

    def to_row(self):
        _, _, row_send, row_recv = self.sems
        i = self.image
        return remote(
            self.out_row.at[i], self.got_row.at[i], row_send.at[i], row_recv.at[i], self.place.row_peer
        )

    def run(self, calc, out_core, keep):
        place, i = self.place, self.image
        out_core[i, 0] = calc(place.t_both).astype(BF)
        self.first = self.to_core(0, out_core.at[i, 0])
        self.first.start()
        keep[0] = calc(place.t_row)
        out_core[i, 1] = calc(place.t_core).astype(BF)
        self.second = self.to_core(1, out_core.at[i, 1])
        self.second.start()
        self.first.wait_recv()
        self.out_row[i] = (keep[0] + self.got_core[i, 0].astype(F32)).astype(BF)
        self.row = self.to_row()
        self.row.start()
        keep[1 + i] = calc(place.t)

    def send_parts(self, cfg, parts):
        place, i = self.place, self.image
        self.first = self.to_core(0, parts.at[slab_rows(cfg, i, place.t_both)])
        self.second = self.to_core(1, parts.at[slab_rows(cfg, i, place.t_core)])
        self.first.start()
        self.second.start()

    def pass_parts(self, cfg, parts):
        i = self.image
        self.first.wait_recv()
        rows = slab_rows(cfg, i, self.place.t_row)
        parts[rows, :] = (parts[rows, :].astype(F32) + self.got_core[i, 0].astype(F32)).astype(BF)
        _, _, row_send, row_recv = self.sems
        self.row = remote(
            parts.at[rows], self.got_row.at[i], row_send.at[i], row_recv.at[i], self.place.row_peer
        )
        self.row.start()

    def total(self, own):
        self.second.wait_recv()
        self.row.wait_recv()
        i = self.image
        return own + self.got_core[i, 1].astype(F32) + self.got_row[i].astype(F32)

    def finish(self):
        self.first.wait_send()
        self.second.wait_send()
        self.row.wait_send()


class WeightGather:
    def __init__(self, cfg, place, full, columns, sems, w):
        far_send, far_recv, near_send, near_recv = sems
        first, last = columns

        def part(offset):
            rows = rows_at((place.far_at(offset) * NEAR + place.near) * cfg.block, cfg.block)
            return full.at[rows, first:last]

        src = part(0)
        self.fars = [
            remote(src, src, far_send.at[w, o], far_recv.at[w, o], place.far_peers[o])
            for o in range(FAR - 1)
        ]
        self.nears = [
            remote(part(-k), part(-k), near_send.at[w, k], near_recv.at[w, k], place.near_peer)
            for k in range(FAR)
        ]

    def start(self):
        for copy in self.fars:
            copy.start()
        self.nears[0].start()

    def forward(self, which=None):
        for o in range(FAR - 1) if which is None else which:
            self.fars[o].wait_recv()
            self.nears[o + 1].start()

    def wait(self):
        for copy in self.nears:
            copy.wait_recv()

    def finish(self):
        for copy in self.fars + self.nears:
            copy.wait_send()


class WeightScatter:
    def __init__(self, cfg, place, part, first, got_near, got_far, sems, w):
        far_send, far_recv, near_send, near_recv = sems
        block = cfg.block
        self.first, self.last = first, first + got_near.shape[2]
        self.place, self.part, self.got_near, self.got_far = place, part, got_near, got_far

        def rows(offset, near):
            return rows_at((place.far_at(offset) * NEAR + near) * block, block)

        self.rows = rows
        self.nears = [
            remote(
                part.at[rows(o, 1 - place.near), self.first : self.last],
                got_near.at[o],
                near_send.at[w, o],
                near_recv.at[w, o],
                place.near_peer,
            )
            for o in range(FAR)
        ]
        self.fars = [
            remote(
                got_near.at[o],
                got_far.at[o - 1],
                far_send.at[w, o - 1],
                far_recv.at[w, o - 1],
                place.far_peers[o - 1],
            )
            for o in range(1, FAR)
        ]

    def start(self):
        for o in list(range(1, FAR)) + [0]:
            self.nears[o].start()

    def forward(self, which=None):
        for o in range(1, FAR) if which is None else which:
            self.nears[o].wait_recv()
            mine = self.part[self.rows(o, self.place.near), self.first : self.last].astype(F32)
            self.got_near[o] = (mine + self.got_near[o].astype(F32)).astype(BF)
            self.fars[o - 1].start()

    def total(self):
        self.nears[0].wait_recv()
        mine = self.part[self.rows(0, self.place.near), self.first : self.last].astype(F32)
        value = mine + self.got_near[0].astype(F32)
        for o in range(1, FAR):
            self.fars[o - 1].wait_recv()
            value = value + self.got_far[o - 1].astype(F32)
        return value

    def finish(self):
        for copy in self.fars + self.nears:
            copy.wait_send()


def split_heads(cfg, value, shift, out, image, at, size):
    for h in range(cfg.heads):
        part = value[:, shift + h * HEAD_DIM : shift + (h + 1) * HEAD_DIM]
        out[h][rows_at(image * cfg.tokens + at, size), :HEAD_DIM] = part.astype(BF)


def attend_forward(cfg, image, head, q, k, v, mixed, shift, lse):
    rows = rows_at(image * cfg.tokens, cfg.tokens)
    values = v[head, rows, :].astype(F32).T.astype(BF)[:HEAD_DIM]
    scores = dot(k[head, rows, :], q[head, rows, :], NT)
    top = jnp.max(scores, axis=0, keepdims=True)
    probs = jnp.exp2((scores - top) * SCALE_TWO)
    total = jnp.sum(probs, axis=0, keepdims=True)
    out = dot(values, probs.astype(BF), NN) * (1.0 / total)
    start = shift + head * HEAD_DIM
    mixed[rows, start : start + HEAD_DIM] = out.T.astype(BF)
    lse[head, image : image + 1, :] = top * SCALE_TWO + jnp.log2(total)


def attend_backward(cfg, image, head, q, k, v, d_mixed, lse, d_proj, bias_sums):
    rows = rows_at(image * cfg.tokens, cfg.tokens)
    keys, query, d_out = k[head, rows, :], q[head, rows, :], d_mixed[head][...]
    keys_t = keys.astype(F32).T.astype(BF)[:HEAD_DIM]
    scores = dot(keys, query, NT)
    probs = jnp.exp2(scores * SCALE_TWO - lse[head, image : image + 1, :])
    d_values = dot(probs.astype(BF), d_out, NN)[:, :HEAD_DIM]
    d_probs = dot(v[head, rows, :], d_out, NT)
    delta = jnp.sum(probs * d_probs, axis=0, keepdims=True)
    d_scores = (probs * (d_probs - delta)).astype(BF)
    d_keys = dot(d_scores, query, NN)[:, :HEAD_DIM] * SCALE
    d_query = (dot(keys_t, d_scores, NN) * SCALE).T
    for which, value in ((0, d_query), (1, d_keys), (2, d_values)):
        start = (3 * head + which) * HEAD_DIM
        d_proj[rows, start : start + HEAD_DIM] = value.astype(BF)
    for row, value in ((0, d_query), (1, d_values)):
        bias_sums[row : row + 1, head * HEAD_DIM : (head + 1) * HEAD_DIM] += column_sum(value)


def keep_row_mask(cfg, place, length):
    at = lax.broadcasted_iota(jnp.int32, (cfg.seq, 1), 0) + place.t * cfg.seq
    return (at < length).astype(F32)


def key_bias(cfg, length):
    index = lax.broadcasted_iota(jnp.int32, (cfg.tokens, 1), 0)
    rank = jnp.zeros_like(index)
    for r in range(1, RANKS):
        rank = rank + (index >= r * cfg.slab).astype(jnp.int32)
    within = index - rank * cfg.slab
    at = rank * cfg.seq + within
    return jnp.where((within < cfg.seq) & (at < length), 0.0, NEG_FILL)


def layer_kernel(cfg, names, *refs):
    r = types.SimpleNamespace(**dict(zip(names, refs)))
    place = Place(cfg.extra)
    images = range(cfg.images)
    heads, units, hc = cfg.heads, cfg.units, cfg.head_cols
    half, third = cfg.tokens // 2, cfg.width // 3
    gather_sems = (r.wg_far_s, r.wg_far_r, r.wg_near_s, r.wg_near_r)
    scatter_sems = (r.ws_far_s, r.ws_far_r, r.ws_near_s, r.ws_near_r)
    q, k, v = (r.qkv.at[pl.ds(n * heads, heads)] for n in range(3))
    own_qkv, own_out, own_up, own_down = r.d_qkv, r.d_out, r.d_up, r.d_down
    resid, cotangent = r.block, r.gradient
    w = r.w
    out_at, up_at, wide = 3 * hc, 4 * hc, -(-units // LANES) * LANES
    edge = units % LANES
    out_first = out_at // LANES * LANES
    out_shift = out_at - out_first
    down_first = up_at + wide - LANES
    out_window, up_window = slice(out_first, up_at), slice(up_at, up_at + wide)
    tiles = range(wide // LANES)

    def lanes(value):
        return lax.broadcasted_iota(jnp.int32, value.shape, 1)

    def to_window(value):
        first, last = value[0], value[-1]
        moved = jnp.where(lanes(last) < 2 * edge, pltpu.roll(first, edge, 1), 0.0)
        head = jnp.where(lanes(first) < edge, 0.0, first)
        return [head, *value[1:-1], jnp.where(lanes(last) < edge, last, moved)]

    def from_window(value):
        first, last = value[0], value[-1]
        moved = pltpu.roll(last, LANES - edge, 1)
        head = jnp.where(lanes(first) < edge, moved, first)
        return [head, *value[1:-1], jnp.where(lanes(last) < edge, last, 0.0)]
    h_one, mlp = r.page_one, r.page_one
    h_two, d_proj = r.page_two, r.page_two
    grad, d_pre, h_one_again = r.page_three, r.page_three, r.page_three
    act = r.page_four
    part_down, part_qkv = r.part, r.part
    d_mixed = [r.page_four.at[pl.ds(0, cfg.tokens), pl.ds(h * LANES, LANES)] for h in range(heads)]

    def local(src, dst, n):
        copy = pltpu.make_async_copy(src, dst, r.local_sem.at[n])
        copy.start()
        return copy

    load_qkv = local(r.own_qkv_hbm, own_qkv, 0)
    load_x = local(r.x_hbm, r.x, 1)
    load_out = local(r.own_out_hbm, own_out, 2)
    load_up = local(r.own_up_hbm, own_up, 3)
    load_cot = local(r.cotangent_hbm, cotangent, 4)
    load_down = local(r.own_down_hbm, own_down, 5)

    place.greet(both=True)
    bounds = [n * LANES for n in (0, 4, 7, 9, 14, 18, 22, 24)] + [w.shape[1]]
    gathers = [
        WeightGather(cfg, place, w, (first, last), gather_sems, n)
        for n, (first, last) in enumerate(zip(bounds[:-1], bounds[1:]))
    ]
    g_heads, g_out, g_up, g_down = gathers[0:2], gathers[2], gathers[3:5], gathers[5:8]
    here = rows_at((place.far * NEAR + place.near) * cfg.block, cfg.block)
    load_qkv.wait()
    load_out.wait()
    columns = [own_qkv[n][:, h * HEAD_DIM : (h + 1) * HEAD_DIM] for h in range(heads) for n in range(3)]
    w[here, :up_at] = jnp.concatenate(columns + [own_out[...]], axis=1).astype(BF)
    g_heads[0].start()

    one = [TokenGather(cfg, place, h_one, r.tg_s.at[0], r.tg_r.at[0], i) for i in images]
    cot = [TokenGather(cfg, place, grad, r.tg_s.at[1], r.tg_r.at[1], i) for i in images]
    two = [TokenGather(cfg, place, h_two, r.tg_s.at[2], r.tg_r.at[2], i) for i in images]
    dres = [TokenGather(cfg, place, r.d_res, r.tg_s.at[3], r.tg_r.at[3], i) for i in images]
    load_x.wait()
    for i in images:
        rows, _ = standardize(r.x[i])
        value = rows * r.norm_one[0:1, :] + r.norm_one[1:2, :]
        h_one[slab_rows(cfg, i, place.t), :] = padded_slab(value, cfg.slab)
        one[i].start()

    lane = lax.broadcasted_iota(jnp.int32, (cfg.tokens, LANES), 1)
    flag = jnp.where(lane == HEAD_DIM, 1.0, 0.0)
    r.mixed[:, :out_shift] = jnp.zeros((cfg.images * cfg.tokens, out_shift), BF)
    for i in images:
        rows = rows_at(i * cfg.tokens, cfg.tokens)
        bias = jnp.where(lane == HEAD_DIM, key_bias(cfg, r.lengths[i]), 0.0).astype(BF)
        for h in range(heads):
            q[h, rows, :] = flag.astype(BF)
            k[h, rows, :] = bias
            v[h, rows, :] = jnp.zeros((cfg.tokens, LANES), BF)

    load_cot.wait()
    down_bias_sum = jnp.zeros((1, cfg.width), F32)
    for i in images:
        value = cotangent[i] * keep_row_mask(cfg, place, r.lengths[i])
        cotangent[i] = value
        down_bias_sum = down_bias_sum + column_sum(value)
        grad[slab_rows(cfg, i, place.t), :] = padded_slab(value, cfg.slab)
    r.vector[3:4, :] = down_bias_sum

    load_up.wait()
    load_down.wait()
    rest = jnp.zeros((cfg.block, w.shape[1] - up_at - 2 * units), own_up.dtype)
    columns = [own_up[...], own_down[:, edge:], own_down[:, :edge], rest]
    w[here, up_at:] = jnp.concatenate(columns, axis=1).astype(BF)

    def advance(n):
        gathers[n].forward([0])
        if n == 0:
            gathers[1].start()
        gathers[n].forward([1, 2])
        if n + 2 < len(gathers):
            gathers[n + 2].start()

    advance(0)
    one[0].forward()
    for i in images[1:]:
        one[i].forward()
    for i in images:
        cot[i].start()
    g_heads[0].wait()

    def project(i, pair):
        @pl.loop(0, 2)
        def _(j):
            at = pl.multiple_of(j * half, 16)
            value = h_one[rows_at(i * cfg.tokens + at, half), :]
            rows = rows_at(i * cfg.tokens + at, half)
            first = pair * 3 * LANES
            proj = dot(value, w[:, first : first + 4 * LANES], NN)
            for h in (2 * pair, 2 * pair + 1):
                bias = r.qv_bias[:, h * HEAD_DIM : (h + 1) * HEAD_DIM]
                for n, out in enumerate((q, k, v)):
                    start = (3 * h + n) * HEAD_DIM - first
                    part = proj[:, start : start + HEAD_DIM]
                    if n != 1:
                        part = part + bias[n // 2 : n // 2 + 1, :]
                    out[h, rows, :HEAD_DIM] = part.astype(BF)

    def scatters(core, row, sems):
        return [TokenScatter(place, i, core, row, r.ts_row_out, sems) for i in images]

    attns = scatters(r.tsa_core, r.tsa_row, (r.ts_cs.at[0], r.ts_cr.at[0], r.ts_rs.at[0], r.ts_rr.at[0]))
    backs = scatters(r.tsa_core, r.tsa_row, (r.ts_cs.at[1], r.ts_cr.at[1], r.ts_rs.at[1], r.ts_rr.at[1]))
    feeds = scatters(r.tsa_core, r.tsa_row, (r.ts_cs.at[2], r.ts_cr.at[2], r.ts_rs.at[2], r.ts_rr.at[2]))
    sums = scatters(r.tsb_core, r.tsb_row, (r.ts_cs.at[3], r.ts_cr.at[3], r.ts_rs.at[3], r.ts_rr.at[3]))
    def pump_forward(i, h):
        if i == 0 and h == 1:
            advance(1)
        if i == 1 and h == 1:
            advance(2)
            g_heads[1].wait()
        if i == 0 and h == 2:
            cot[0].forward()
        if i == 0 and h == 3:
            g_out.wait()
        if i == 1 and h == 2:
            advance(3)

    for pair in range(2):
        for i in images:
            if pair == 0:
                one[i].wait()
            project(i, pair)
            for h in (2 * pair, 2 * pair + 1):
                attend_forward(cfg, i, h, q, k, v, r.mixed, out_shift, r.lse)
                pump_forward(i, h)
            if pair == 1:
                attns[i].run(
                    lambda rank: dot(r.mixed[slab_rows(cfg, i, rank), :], w[:, out_window], NT),
                    r.ts_core_out,
                    r.keep,
                )
    spill_h_one = local(h_one, r.h_one_hbm, 6)
    spill_qkv = local(r.qkv, r.qkv_hbm, 7)

    for c in cot[1:]:
        c.forward()
    for i in images:
        attn = attns[i].total(r.keep[1 + i])[: cfg.seq]
        value = r.x[i] + attn + r.out_bias[...][None]
        resid[i] = value
        rows, _ = standardize(value)
        value = rows * r.norm_two[0:1, :] + r.norm_two[1:2, :]
        h_two[slab_rows(cfg, i, place.t), :] = padded_slab(value, cfg.slab)
        two[i].start()
        if i == 0:
            advance(4)
    for item in attns:
        item.finish()
    for g in g_up:
        g.wait()
    advance(5)
    spill_qkv.wait()
    up_bias = jnp.concatenate([r.up_bias[...][None], jnp.zeros((1, wide - units), F32)], axis=1)

    def split(value):
        return [value[:, n * LANES : (n + 1) * LANES] for n in range(value.shape[1] // LANES)]

    def unit_block(i, rank):
        rows = slab_rows(cfg, i, rank)
        pre = dot(h_two[rows, :], w[:, up_window], NN) + up_bias
        value, slope = gelu_pair(pre)
        for n, part in enumerate(to_window(split(value))):
            act[rows, n * LANES : (n + 1) * LANES] = part.astype(BF)
        for n, part in enumerate(to_window(split(slope))):
            r.qkv[n, rows, :] = part.astype(BF)

    for i in images:
        unit_block(i, place.t)
        two[i].wait_core()
        unit_block(i, place.t_core)
        two[i].forward()
        unit_block(i, place.t_row)
        two[i].wait()
        unit_block(i, place.t_both)
        advance(6 + i)

    for c in cot:
        c.wait()
        c.finish()

    def weight_part(part, left, right, first=0):
        last = first + right.shape[1]

        @pl.loop(0, 3)
        def _(j):
            cols = pl.ds(pl.multiple_of(j * third, LANES), third)
            part[rows_at(j * third, third), first:last] = dot(left[:, cols], right, TN).astype(BF)

    def weight_scatter(n, part, first, near, far):
        return WeightScatter(cfg, place, part, first, near, far, scatter_sems, n)

    spare = down_first + LANES
    down_half = (wide + LANES) // 2 // LANES * LANES
    s_down = [
        weight_scatter(0, part_down, LANES, r.down_near_0, r.down_far_0),
        weight_scatter(6, part_down, down_half, r.down_near_1, r.down_far_1),
    ]
    s_up = weight_scatter(1, w, up_at, r.up_near, r.up_far)
    s_out = weight_scatter(2, w, spare + LANES, r.out_near, r.out_far)
    cuts = {1: (0, 3 * LANES), 2: (3 * LANES, 5 * LANES), 3: (5 * LANES, out_first + LANES)}
    s_qkv = {
        h: weight_scatter(2 + h, part_qkv, cuts[h][0], getattr(r, f"qkv_near_{h}"), getattr(r, f"qkv_far_{h}"))
        for h in cuts
    }

    weight_part(part_down, grad, act[:, :down_half])
    s_down[0].start()
    weight_part(part_down, grad, act[:, down_half:], down_half)
    s_down[1].start()
    s_down[0].forward([1])
    r.vector[4:5, :] = jnp.zeros((1, cfg.width), F32)

    def d_pre_part(i, part):
        first = part[0] * LANES

        @pl.loop(0, 2)
        def _(j):
            rows = rows_at(i * cfg.tokens + j * half, half)
            slope = jnp.concatenate([r.qkv[n, rows, :] for n in part], axis=1)
            value = dot(grad[rows, :], w[:, down_first + first : down_first + first + slope.shape[1]], NN)
            value = value * slope.astype(F32)
            r.vector[4:5, first : first + slope.shape[1]] += column_sum(value)
            for n, column in zip(part, split(value)):
                r.qkv[n, rows, :] = column.astype(BF)

    def d_pre_place(i):
        @pl.loop(0, 2)
        def _(j):
            rows = rows_at(i * cfg.tokens + j * half, half)
            ends = from_window([r.qkv[0, rows, :].astype(F32), r.qkv[tiles[-1], rows, :].astype(F32)])
            for n in tiles[1:-1]:
                d_pre[rows, n * LANES : (n + 1) * LANES] = r.qkv[n, rows, :]
            d_pre[rows, :LANES] = ends[0].astype(BF)
            d_pre[rows, wide - LANES :] = ends[1].astype(BF)

    g_down[0].wait()
    g_down[1].wait()
    for i in images:
        d_pre_part(i, tiles[:7])
        if i == 0:
            g_down[2].wait()
            s_down[0].forward([2])
        d_pre_part(i, tiles[7:])
        d_pre_place(i)
        if i == 1:
            s_down[1].forward([1])
        backs[i].run(
            lambda rank: dot(d_pre[slab_rows(cfg, i, rank), :], w[:, up_window], NT),
            r.ts_core_out,
            r.keep,
        )
        s_down[i].forward([3 - i])
    fetch_qkv = local(r.qkv_hbm, r.qkv, 8)

    def feed(i):
        @pl.loop(0, 2)
        def _(j):
            rows = rows_at(i * cfg.tokens + j * half, half)
            value = dot(act[rows, :LANES], r.edge[...], NT)
            value = value + dot(act[rows, LANES:], w[:, down_first + LANES :], NT)
            mlp[rows, :] = value.astype(BF)

    def through_norm_two(i):
        d_normed = backs[i].total(r.keep[1 + i])[: cfg.seq]
        rows, inverse = standardize(resid[i])
        value = cotangent[i] + norm_backward(d_normed, rows, inverse, r.norm_two[0:1, :])
        r.gradient[i] = value
        r.d_res[slab_rows(cfg, i, place.t), :] = padded_slab(value, cfg.slab)
        dres[i].start()
        return column_sum(value), column_sum(d_normed * rows), column_sum(d_normed)

    for item in two + gathers:
        item.finish()
    r.edge[...] = w[:, down_first : down_first + LANES]
    weight_part(w, h_two, d_pre[...], up_at)
    w[:, down_first : down_first + LANES] = (
        w[:, down_first : down_first + LANES].astype(F32) + part_down[:, :LANES].astype(F32)
    ).astype(BF)
    s_up.start()
    s_down[1].forward([3])
    vectors = [through_norm_two(0)]
    for c in one:
        c.finish()
    spill_h_one.wait()
    fetch_h_one = local(r.h_one_hbm, h_one_again, 9)
    for i in images:
        feed(i)
    for i in images[1:]:
        vectors.append(through_norm_two(i))
    for item in backs:
        item.finish()
    s_up.forward([1])
    for n in range(3):
        r.vector[n : n + 1, :] = sum(entry[n] for entry in vectors)
    row = r.vector[4:5, :]
    r.vector[4:5, :] = jnp.concatenate(from_window(split(row)), axis=1)
    early = VectorSum(place, r.early_far, r.early_near, r.early_rank, r.early_s, r.early_r)
    r.vector[5:8, :] = jnp.zeros((3, cfg.width), F32)
    early.start(r.vector[...])
    r.bias_sums[...] = jnp.zeros_like(r.bias_sums)
    for part in d_mixed:
        part[...] = jnp.zeros((cfg.tokens, LANES), BF)
    d_proj[:, out_at : out_first + LANES] = jnp.zeros((cfg.images * cfg.tokens, LANES - out_shift), BF)
    for i in images:
        dres[i].wait_core()
        feeds[i].send_parts(cfg, mlp)
    dres[0].forward()
    feeds[0].pass_parts(cfg, mlp)
    fetch_qkv.wait()
    dres[0].wait()

    def qkv_part(h):
        first, last = cuts[h]
        weight_part(part_qkv, h_one_again, d_proj[:, first:last], first)
        if last > out_first:
            part_qkv[:, out_first:last] = (
                part_qkv[:, out_first:last].astype(F32) + w[:, spare : spare + LANES].astype(F32)
            ).astype(BF)
        s_qkv[h].start()

    for i in images:
        @pl.loop(0, 2)
        def _(j):
            at = pl.multiple_of(j * half, 16)
            value = dot(r.d_res[rows_at(i * cfg.tokens + at, half), :], w[:, out_window], NN)
            split_heads(cfg, value, out_shift, d_mixed, 0, at, half)

        for h in range(heads):
            attend_backward(cfg, i, h, q, k, v, d_mixed, r.lse, d_proj, r.bias_sums)
            if i == 0 and h == 0:
                s_up.forward([2])
            if i == 0 and h == 2:
                s_up.forward([3])
            if i == 0 and h == 3:
                dres[1].forward()
            if i == 1 and h == 0:
                value = jnp.concatenate([part.total() for part in s_down], axis=1)
                r.d_down[:, LANES:] = value[:, : units - LANES]
                r.d_down[:, :edge] = value[:, units - LANES : units - LANES + edge]
                for part in s_down:
                    part.finish()
                early.step()
                fetch_h_one.wait()
            if i == 1 and h in (1, 2):
                qkv_part(h)
            if i == 1 and h == 1:
                s_out.forward([1, 2])
            if i == 1 and h == 2:
                s_out.forward([3])
                early.last()
            if i == 1 and h == 3:
                s_qkv[1].forward()
        sums[i].run(
            lambda rank: dot(
                d_proj[slab_rows(cfg, i, rank), : out_first + LANES], w[:, : out_first + LANES], NT
            ),
            r.ts_core_out,
            r.keep,
        )
        if i == 0:
            dres[1].wait()
            weight_part(w, r.d_res, r.mixed[...], spare)
            s_out.start()
    qkv_part(3)
    feeds[1].pass_parts(cfg, mlp)
    s_qkv[2].forward()
    results = []

    def finish_block(i):
        value = feeds[i].total(mlp[slab_rows(cfg, i, place.t), :].astype(F32))
        r.block[i] = resid[i] + value[: cfg.seq] + r.down_bias[...][None]
        feeds[i].finish()
        results.append(local(r.block.at[i], r.block_out.at[i], 10 + i))

    finish_block(0)
    gain_sum = jnp.zeros((1, cfg.width), F32)
    shift_sum = jnp.zeros((1, cfg.width), F32)
    for i in images:
        if i == 1:
            s_qkv[3].forward()
        d_normed = sums[i].total(r.keep[1 + i])[: cfg.seq]
        rows, inverse = standardize(r.x[i])
        r.gradient[i] = r.gradient[i] + norm_backward(d_normed, rows, inverse, r.norm_one[0:1, :])
        results.append(local(r.gradient.at[i], r.grad_input.at[i], 12 + i))
        gain_sum = gain_sum + column_sum(d_normed * rows)
        shift_sum = shift_sum + column_sum(d_normed)
    late = VectorSum(place, r.late_far, r.late_near, r.late_rank, r.late_s, r.late_r)
    pad = jnp.zeros((2, cfg.width - hc), F32)
    late.start(
        jnp.concatenate(
            [
                gain_sum,
                shift_sum,
                jnp.concatenate([r.bias_sums[...], pad], axis=1),
                jnp.zeros((4, cfg.width), F32),
            ],
            axis=0,
        )
    )
    value = s_up.total()
    r.d_up[...] = value[:, :units]
    r.d_down[:, edge:LANES] = value[:, units:]
    r.d_out[:, LANES - out_shift :] = s_out.total()
    r.early_all[...], r.early_dp[...] = early.total()
    late.step()
    finish_block(1)

    def place_heads(value, first, some):
        for h in some:
            for n in range(3):
                start = (3 * h + n) * HEAD_DIM - first
                r.d_qkv[n, :, h * HEAD_DIM : (h + 1) * HEAD_DIM] = value[:, start : start + HEAD_DIM]

    begun = jnp.concatenate([s_qkv[1].total(), s_qkv[2].total()], axis=1)
    place_heads(begun, 0, range(2))
    late.last()
    value = jnp.concatenate([begun[:, cuts[2][0] :], s_qkv[3].total()], axis=1)
    place_heads(value, cuts[2][0], range(2, heads))
    r.d_out[:, : LANES - out_shift] = value[:, out_at - cuts[2][0] :]
    r.late_all[...], r.late_dp[...] = late.total()
    for copy in results:
        copy.wait()
    for item in dres + sums + [s_up, s_out, early, late] + list(s_qkv.values()):
        item.finish()


def spread(kernel, cfg, inputs, outputs, scratch, collective_id, cost):
    names = list(inputs) + list(outputs) + list(scratch)
    space = {"v": pltpu.VMEM, "s": pltpu.SMEM, "h": pl.ANY}
    result = pl.pallas_call(
        functools.partial(kernel, cfg, names),
        out_shape=tuple(jax.ShapeDtypeStruct(shape, dtype) for _, shape, dtype in outputs.values()),
        in_specs=[pl.BlockSpec(memory_space=space[where]) for where, _ in inputs.values()],
        out_specs=tuple(pl.BlockSpec(memory_space=space[where]) for where, _, _ in outputs.values()),
        scratch_shapes=list(scratch.values()),
        compiler_params=pltpu.CompilerParams(
            collective_id=collective_id, has_side_effects=True, vmem_limit_bytes=VMEM_BYTES
        ),
        cost_estimate=pl.CostEstimate(flops=cost, bytes_accessed=cost // 1000, transcendentals=0),
    )(*[value for _, value in inputs.values()])
    return dict(zip(outputs, result))


def dma(*shape):
    return pltpu.SemaphoreType.DMA(shape)


class VectorSum:
    def __init__(self, place, far, near, rank, send, recv):
        self.place, self.far, self.near, self.rank = place, far, near, rank
        mine = far.at[place.far]
        self.fars = [remote(mine, mine, send.at[o], recv.at[o], place.far_peers[o]) for o in range(FAR - 1)]
        mine = near.at[place.near]
        at = FAR - 1
        self.nears = [remote(mine, mine, send.at[at], recv.at[at], place.near_peer)]
        mine = rank.at[place.t]
        self.ranks = []
        for peer in (place.core_peer, place.row_peer, place.both_peer):
            at += 1
            self.ranks.append(remote(mine, mine, send.at[at], recv.at[at], peer))

    def start(self, value):
        self.far[self.place.far] = value
        for copy in self.fars:
            copy.start()

    def step(self):
        for copy in self.fars:
            copy.wait_recv()
        self.near[self.place.near] = (self.far[0] + self.far[1]) + (self.far[2] + self.far[3])
        self.nears[0].start()

    def last(self):
        self.nears[0].wait_recv()
        self.rank[self.place.t] = self.near[0] + self.near[1]
        for copy in self.ranks:
            copy.start()

    def total(self):
        for copy in self.ranks:
            copy.wait_recv()
        whole = (self.rank[0] + self.rank[1]) + (self.rank[2] + self.rank[3])
        return whole, self.rank[self.place.t]

    def finish(self):
        for copy in self.fars + self.nears + self.ranks:
            copy.wait_send()


def call_layer(cfg, inputs):
    all_tokens = cfg.images * cfg.tokens
    w, hc, n = cfg.width, cfg.head_cols, cfg.images
    units_p, hc_p, three_p = (-(-size // LANES) * LANES for size in (cfg.units, hc, 3 * hc))
    qkv = (3 * cfg.heads, all_tokens, LANES)
    local = (n, cfg.seq, w)
    page = (all_tokens, w)
    slabs = (n, cfg.slab, w)
    vec = (8, w)
    outputs = dict(
        block_out=("h", local, F32),
        grad_input=("h", local, F32),
        d_qkv=("v", (3, cfg.block, hc), F32),
        d_out=("v", (cfg.block, hc), F32),
        d_up=("v", (cfg.block, cfg.units), F32),
        d_down=("v", (cfg.block, cfg.units), F32),
        early_all=("v", vec, F32),
        early_dp=("v", vec, F32),
        late_all=("v", vec, F32),
        late_dp=("v", vec, F32),
        h_one_hbm=("h", page, BF),
        qkv_hbm=("h", qkv, BF),
    )
    scratch = dict(
        w=pltpu.VMEM((w, 4 * hc - LANES + 2 * units_p), BF),
        edge=pltpu.VMEM((w, LANES), BF),
        block=pltpu.VMEM(local, F32),
        gradient=pltpu.VMEM(local, F32),
        x=pltpu.VMEM(local, F32),
        page_one=pltpu.VMEM(page, BF),
        page_two=pltpu.VMEM(page, BF),
        page_three=pltpu.VMEM(page, BF),
        page_four=pltpu.VMEM(page, BF),
        d_res=pltpu.VMEM(page, BF),
        qkv=pltpu.VMEM(qkv, BF),
        mixed=pltpu.VMEM((all_tokens, hc_p), BF),
        lse=pltpu.VMEM((cfg.heads, n, cfg.tokens), F32),
        bias_sums=pltpu.VMEM((2, hc), F32),
        vector=pltpu.VMEM(vec, F32),
        tsa_core=pltpu.VMEM((n, 2) + slabs[1:], BF),
        tsa_row=pltpu.VMEM(slabs, BF),
        tsb_core=pltpu.VMEM((n, 2) + slabs[1:], BF),
        tsb_row=pltpu.VMEM(slabs, BF),
        ts_core_out=pltpu.VMEM((n, 2) + slabs[1:], BF),
        ts_row_out=pltpu.VMEM(slabs, BF),
        keep=pltpu.VMEM((1 + n,) + slabs[1:], F32),
        part=pltpu.VMEM((w, w), BF),
        **{
            f"down_{side}_{n}": pltpu.VMEM((count, cfg.block, (units_p - LANES) // 2), BF)
            for n in range(2)
            for side, count in (("near", FAR), ("far", FAR - 1))
        },
        up_near=pltpu.VMEM((FAR, cfg.block, units_p), BF),
        up_far=pltpu.VMEM((FAR - 1, cfg.block, units_p), BF),
        out_near=pltpu.VMEM((FAR, cfg.block, hc_p - LANES), BF),
        out_far=pltpu.VMEM((FAR - 1, cfg.block, hc_p - LANES), BF),
        **{
            f"qkv_{side}_{h}": pltpu.VMEM((count, cfg.block, size), BF)
            for h, size in ((1, 3 * LANES), (2, 2 * LANES), (3, three_p - 5 * LANES))
            for side, count in (("near", FAR), ("far", FAR - 1))
        },
        early_far=pltpu.VMEM((FAR,) + vec, F32),
        early_near=pltpu.VMEM((NEAR,) + vec, F32),
        early_rank=pltpu.VMEM((RANKS,) + vec, F32),
        late_far=pltpu.VMEM((FAR,) + vec, F32),
        late_near=pltpu.VMEM((NEAR,) + vec, F32),
        late_rank=pltpu.VMEM((RANKS,) + vec, F32),
        early_s=dma(FAR + 3),
        early_r=dma(FAR + 3),
        late_s=dma(FAR + 3),
        late_r=dma(FAR + 3),
        wg_far_s=dma(8, FAR - 1),
        wg_far_r=dma(8, FAR - 1),
        wg_near_s=dma(8, FAR),
        wg_near_r=dma(8, FAR),
        ws_far_s=dma(7, FAR - 1),
        ws_far_r=dma(7, FAR - 1),
        ws_near_s=dma(7, FAR),
        ws_near_r=dma(7, FAR),
        tg_s=dma(4, n, 3),
        tg_r=dma(4, n, 3),
        ts_cs=dma(4, n, 2),
        ts_cr=dma(4, n, 2),
        ts_rs=dma(4, n),
        ts_rr=dma(4, n),
        local_sem=dma(14),
    )
    return spread(layer_kernel, cfg, inputs, outputs, scratch, 0, 60 * 10**9)


def adamw(param, grad, mom, var, rate, decay):
    mom_new = BETA_ONE * mom + (1.0 - BETA_ONE) * grad
    var_new = BETA_TWO * var + (1.0 - BETA_TWO) * grad * grad
    mom_hat = mom_new / (1.0 - BETA_ONE**STEP)
    var_hat = var_new / (1.0 - BETA_TWO**STEP)
    change = mom_hat / (jnp.sqrt(var_hat) + ADAM_EPS)
    return (param - rate * (change + decay * param), mom_new, var_new)


MATRICES = {1: "qkv", 3: "out", 6: "up", 8: "down"}


def update_kernel(cfg, *refs):
    params, moms, varis = refs[0:10], refs[10:20], refs[20:30]
    grads = dict(zip(("qkv", "out", "up", "down", "early_all", "early_dp", "late_all", "late_dp"), refs[30:38]))
    streams, outs = refs[38:40], refs[40:]
    for source, target in zip(streams, outs[:2]):
        target[...] = source[...]
    outs = outs[2:]

    def step(n, grad, rate, decay):
        new = adamw(params[n][...], grad, moms[n][...], varis[n][...], rate, decay)
        for kind, value in enumerate((grad,) + new):
            outs[10 * kind + n][...] = value

    for n, name in MATRICES.items():
        step(n, grads[name][...], RATE_MATRIX, DECAY)
    vectors = {
        0: grads["late_all"][0:2, :],
        2: grads["late_dp"][2:4, : cfg.head_cols],
        4: grads["early_all"][0, :],
        5: grads["early_all"][1:3, :],
        7: grads["early_dp"][4, : cfg.units],
        9: grads["early_all"][3, :],
    }
    for n, grad in vectors.items():
        step(n, grad, RATE_VECTOR, 0.0)


def call_update(cfg, shard, params, moms, varis, grads, block_out, grad_input):
    steps = 3 if shard % 24 == 0 and cfg.width % (3 * LANES) == 0 else 1
    rows = shard // steps

    def spec(value, n=None):
        shape = value.shape
        if n == "stream":
            return pl.BlockSpec(shape[:2] + (cfg.width // steps,), lambda i: (0, 0, i))
        if n not in MATRICES:
            zeros = (0,) * len(shape)
            return pl.BlockSpec(shape, lambda i: zeros)
        if len(shape) == 3:
            return pl.BlockSpec((shape[0], rows, shape[2]), lambda i: (0, i, 0))
        return pl.BlockSpec((rows, shape[1]), lambda i: (i, 0))

    order = ("qkv", "out", "up", "down", "early_all", "early_dp", "late_all", "late_dp")
    number = {name: n for n, name in MATRICES.items()}
    values = [*params, *moms, *varis, *(grads[name] for name in order), block_out, grad_input]
    ten = [spec(value, n) for n, value in enumerate(params)]
    in_specs = ten * 3 + [spec(grads[name], number.get(name)) for name in order]
    two = [spec(block_out, "stream"), spec(grad_input, "stream")]
    shapes = [block_out, grad_input] + list(params) * 4
    return pl.pallas_call(
        functools.partial(update_kernel, cfg),
        grid=(steps,),
        out_shape=tuple(jax.ShapeDtypeStruct(value.shape, F32) for value in shapes),
        in_specs=in_specs + two,
        out_specs=tuple(two + ten * 4),
        compiler_params=pltpu.CompilerParams(vmem_limit_bytes=VMEM_BYTES),
    )(*values)


def per_device(
    layer_input_stream,
    cotangent,
    valid_len,
    attention_norm_pair,
    qkv_weight,
    qv_bias,
    out_weight,
    out_bias,
    feedforward_norm_pair,
    up_weight,
    up_bias,
    down_weight,
    down_bias,
    *moments,
):
    moms, varis = moments[:10], moments[10:]
    images, seq, width = layer_input_stream.shape
    head_cols = qv_bias.shape[1]
    units = up_bias.shape[0]
    slab = -(-seq // 16) * 16
    extra = lax.axis_size("dp") // GROUPS
    cfg = types.SimpleNamespace(
        images=images,
        seq=seq,
        slab=slab,
        tokens=RANKS * slab,
        width=width,
        head_cols=head_cols,
        heads=head_cols // HEAD_DIM,
        units=units,
        block=width // GROUPS,
        extra=extra,
    )
    group = lax.axis_index("dp") // extra
    shard = width // (GROUPS * extra)

    def to_block(value, axis=0):
        if extra == 1:
            return value
        full = lax.all_gather(value, "dp", axis=axis, tiled=True)
        return lax.dynamic_slice_in_dim(full, group * cfg.block, cfg.block, axis)

    def from_block(value, axis=0):
        if extra == 1:
            return value
        shape = value.shape[:axis] + (width,) + value.shape[axis + 1 :]
        full = jnp.zeros(shape, value.dtype)
        full = lax.dynamic_update_slice_in_dim(full, value, group * cfg.block, axis)
        return lax.psum_scatter(full, "dp", scatter_dimension=axis, tiled=True)

    def over_rest(value):
        return value if extra == 1 else lax.psum(value, "dp") * (1.0 / GROUPS)

    def turned(values):
        attn, qkv, qv, out, out_b, mlp, up, up_b, down, down_b = values
        return (attn, qkv.transpose(1, 0, 2), qv, out.T, out_b, mlp, up, up_b, down.T, down_b)

    params = turned(
        (
            attention_norm_pair,
            qkv_weight,
            qv_bias,
            out_weight,
            out_bias,
            feedforward_norm_pair,
            up_weight,
            up_bias,
            down_weight,
            down_bias,
        )
    )
    moms, varis = turned(moms), turned(varis)
    layer = call_layer(
        cfg,
        dict(
            x_hbm=("h", layer_input_stream),
            cotangent_hbm=("h", cotangent),
            lengths=("s", valid_len),
            norm_one=("v", attention_norm_pair),
            norm_two=("v", feedforward_norm_pair),
            qv_bias=("v", qv_bias),
            out_bias=("v", out_bias),
            up_bias=("v", up_bias),
            down_bias=("v", down_bias),
            own_qkv_hbm=("h", to_block(params[1], 1)),
            own_out_hbm=("h", to_block(params[3])),
            own_up_hbm=("h", to_block(params[6])),
            own_down_hbm=("h", to_block(params[8])),
        ),
    )
    updated = call_update(
        cfg,
        shard,
        params,
        moms,
        varis,
        dict(
            qkv=from_block(layer["d_qkv"], 1),
            out=from_block(layer["d_out"]),
            up=from_block(layer["d_up"]),
            down=from_block(layer["d_down"]),
            **{
                name: over_rest(layer[name])
                for name in ("early_all", "early_dp", "late_all", "late_dp")
            },
        ),
        layer["block_out"],
        layer["grad_input"],
    )
    streams, rest = updated[:2], updated[2:]
    results = []
    for kind in range(4):
        results.extend(turned(rest[10 * kind : 10 * kind + 10]))
    return (*streams, *results)


def solution(mesh):
    stream = P("dp", "tensor", None)
    parameters = (
        P(),
        P("dp", None, "tensor"),
        P(None, "tensor"),
        P("tensor", "dp"),
        P(),
        P(),
        P("dp", "tensor"),
        P("tensor"),
        P("tensor", "dp"),
        P(),
    )
    return jax.shard_map(
        per_device,
        mesh=mesh,
        in_specs=(stream, stream, P("dp")) + parameters * 3,
        out_specs=(stream, stream) + parameters * 4,
        check_vma=False,
    )
```

```python
import functools
import math
import types

import jax
import jax.numpy as jnp
from jax import lax
from jax.experimental import pallas as pl
from jax.experimental.pallas import tpu as pltpu
from jax.sharding import PartitionSpec as P

HEAD_DIM = 72
STEP = 4

NORM_EPS = 1e-06
NEG_FILL = -1e30
BETA_ONE = 0.9
BETA_TWO = 0.95
ADAM_EPS = 1e-08
RATE_MATRIX = 0.01
RATE_VECTOR = 0.1
DECAY = 0.1
GELU_COEF = math.sqrt(2.0 / math.pi)
CUBIC = 0.044715

NEAR = 2
FAR = 4
GROUPS = NEAR * FAR
RANKS = 4
LANES = 128
SCALE = 1.0 / math.sqrt(HEAD_DIM)
SCALE_TWO = SCALE * math.log2(math.e)
VMEM_BYTES = 63 * 2**20

MESH = pl.DeviceIdType.MESH
BF = jnp.bfloat16
F32 = jnp.float32
NN = (((1,), (0,)), ((), ()))
NT = (((1,), (1,)), ((), ()))
TN = (((0,), (0,)), ((), ()))


def dot(left, right, dims):
    return lax.dot_general(left, right, dims, preferred_element_type=F32)


def rows_at(start, size, unit=16):
    return pl.ds(pl.multiple_of(start, unit), size)


def standardize(value):
    centered_rows = value - jnp.mean(value, axis=-1, keepdims=True)
    spread = jnp.mean(centered_rows * centered_rows, axis=-1, keepdims=True)
    inverse_deviation = lax.rsqrt(spread + NORM_EPS)
    return centered_rows * inverse_deviation, inverse_deviation


def norm_backward(normed_gradient, rows, inverse_deviation, gain):
    g = normed_gradient * gain
    first_average = jnp.mean(g, axis=-1, keepdims=True)
    second_average = jnp.mean(g * rows, axis=-1, keepdims=True)
    return inverse_deviation * (g - first_average - rows * second_average)


def column_sum(value):
    return jnp.sum(value, axis=0, keepdims=True)


def gelu_pair(value):
    inner = GELU_COEF * (value + CUBIC * value * value * value)
    tangent = jnp.tanh(inner)
    result = 0.5 * value * (1.0 + tangent)
    slope = 0.5 * (1.0 + tangent) + 0.5 * value * (1.0 - tangent * tangent) * GELU_COEF * (
        1.0 + 3.0 * CUBIC * value * value
    )
    return (result, slope)


def padded_slab(value, slab):
    rows, width = value.shape
    if slab > rows:
        value = jnp.concatenate([value, jnp.zeros((slab - rows, width), value.dtype)], axis=0)
    return value.astype(BF)


class Place:
    def __init__(self, extra):
        dp, self.t = lax.axis_index("dp"), lax.axis_index("tensor")
        t = self.t
        group = dp // extra
        sub = dp - group * extra
        self.far = group // NEAR
        self.near = group - self.far * NEAR
        row = t // 2
        core = t - 2 * row
        self.t_core = t + 1 - 2 * core
        self.t_row = t + 2 - 4 * row
        self.t_both = 3 - t
        self.core_peer = (dp, self.t_core)
        self.row_peer = (dp, self.t_row)
        self.both_peer = (dp, self.t_both)

        def at(far, near):
            return ((far * NEAR + near) * extra + sub, t)

        self.near_peer = at(self.far, 1 - self.near)
        self.far_peers = [at(self.far_at(o), self.near) for o in range(1, FAR)]

    def far_at(self, offset):
        return lax.rem(self.far + (offset + FAR), FAR)

    def greet(self, both=False):
        peers = [self.core_peer, self.row_peer, self.near_peer] + self.far_peers
        if both:
            peers.append(self.both_peer)
        barrier = pltpu.get_barrier_semaphore()
        for peer in peers:
            pl.semaphore_signal(barrier, inc=1, device_id=peer, device_id_type=MESH)
        pl.semaphore_wait(barrier, len(peers))


def remote(src, dst, send, recv, peer):
    return pltpu.make_async_remote_copy(
        src_ref=src, dst_ref=dst, send_sem=send, recv_sem=recv, device_id=peer, device_id_type=MESH
    )


def slab_rows(cfg, image, rank):
    return rows_at(image * cfg.tokens + rank * cfg.slab, cfg.slab)


class TokenGather:
    def __init__(self, cfg, place, buf, send, recv, image):
        def copy(j, rank, peer):
            part = buf.at[slab_rows(cfg, image, rank)]
            return remote(part, part, send.at[image, j], recv.at[image, j], peer)

        self.core = copy(0, place.t, place.core_peer)
        self.row = copy(1, place.t, place.row_peer)
        self.relay = copy(2, place.t_row, place.core_peer)
        self.core_here = False

    def start(self):
        self.row.start()
        self.core.start()

    def wait_core(self):
        if not self.core_here:
            self.core.wait_recv()
            self.core_here = True

    def forward(self):
        self.row.wait_recv()
        self.relay.start()

    def wait(self):
        self.wait_core()
        self.relay.wait_recv()

    def finish(self):
        self.core.wait_send()
        self.row.wait_send()
        self.relay.wait_send()


class TokenScatter:
    def __init__(self, place, image, got_core, got_row, out_row, sems):
        core_send, core_recv, row_send, row_recv = sems
        self.place, self.image = place, image
        self.got_core, self.got_row, self.out_row = got_core, got_row, out_row
        self.sems = sems

    def to_core(self, j, src):
        core_send, core_recv, _, _ = self.sems
        i = self.image
        return remote(
            src, self.got_core.at[i, j], core_send.at[i, j], core_recv.at[i, j], self.place.core_peer
        )

    def to_row(self):
        _, _, row_send, row_recv = self.sems
        i = self.image
        return remote(
            self.out_row.at[i], self.got_row.at[i], row_send.at[i], row_recv.at[i], self.place.row_peer
        )

    def run(self, calc, out_core, keep, between=None):
        place, i = self.place, self.image
        out_core[i, 0] = calc(place.t_both).astype(BF)
        self.first = self.to_core(0, out_core.at[i, 0])
        self.first.start()
        keep[0] = calc(place.t_row)
        if between is not None:
            between(0)
        out_core[i, 1] = calc(place.t_core).astype(BF)
        self.second = self.to_core(1, out_core.at[i, 1])
        self.second.start()
        self.first.wait_recv()
        self.out_row[i] = (keep[0] + self.got_core[i, 0].astype(F32)).astype(BF)
        self.row = self.to_row()
        self.row.start()
        if between is not None:
            between(1)
        keep[1 + i] = calc(place.t)

    def send_parts(self, cfg, parts):
        place, i = self.place, self.image
        self.first = self.to_core(0, parts.at[slab_rows(cfg, i, place.t_both)])
        self.second = self.to_core(1, parts.at[slab_rows(cfg, i, place.t_core)])
        self.first.start()
        self.second.start()

    def pass_parts(self, cfg, parts):
        i = self.image
        self.first.wait_recv()
        rows = slab_rows(cfg, i, self.place.t_row)
        parts[rows, :] = (parts[rows, :].astype(F32) + self.got_core[i, 0].astype(F32)).astype(BF)
        _, _, row_send, row_recv = self.sems
        self.row = remote(
            parts.at[rows], self.got_row.at[i], row_send.at[i], row_recv.at[i], self.place.row_peer
        )
        self.row.start()

    def total(self, own):
        self.second.wait_recv()
        self.row.wait_recv()
        i = self.image
        return own + self.got_core[i, 1].astype(F32) + self.got_row[i].astype(F32)

    def finish(self):
        self.first.wait_send()
        self.second.wait_send()
        self.row.wait_send()


class WeightGather:
    def __init__(self, cfg, place, full, columns, sems, w):
        far_send, far_recv, near_send, near_recv = sems
        first, last = columns

        def part(offset):
            rows = rows_at((place.far_at(offset) * NEAR + place.near) * cfg.block, cfg.block)
            return full.at[rows, first:last]

        src = part(0)
        self.fars = [
            remote(src, src, far_send.at[w, o], far_recv.at[w, o], place.far_peers[o])
            for o in range(FAR - 1)
        ]
        self.nears = [
            remote(part(-k), part(-k), near_send.at[w, k], near_recv.at[w, k], place.near_peer)
            for k in range(FAR)
        ]

    def start(self):
        for copy in self.fars:
            copy.start()

    def start_near(self):
        self.nears[0].start()

    def forward(self, which=None):
        for o in range(FAR - 1) if which is None else which:
            self.fars[o].wait_recv()
            self.nears[o + 1].start()

    def wait(self):
        for copy in self.nears:
            copy.wait_recv()

    def finish(self):
        for copy in self.fars + self.nears:
            copy.wait_send()


class WeightScatter:
    def __init__(self, cfg, place, part, first, got_near, got_far, sems, w):
        far_send, far_recv, near_send, near_recv = sems
        block = cfg.block
        self.first, self.last = first, first + got_near.shape[2]
        self.place, self.part, self.got_near, self.got_far = place, part, got_near, got_far

        def rows(offset, near):
            return rows_at((place.far_at(offset) * NEAR + near) * block, block)

        self.rows = rows
        self.nears = [
            remote(
                part.at[rows(o, 1 - place.near), self.first : self.last],
                got_near.at[o],
                near_send.at[w, o],
                near_recv.at[w, o],
                place.near_peer,
            )
            for o in range(FAR)
        ]
        self.fars = [
            remote(
                got_near.at[o],
                got_far.at[o - 1],
                far_send.at[w, o - 1],
                far_recv.at[w, o - 1],
                place.far_peers[o - 1],
            )
            for o in range(1, FAR)
        ]

    def start(self):
        for o in list(range(1, FAR)) + [0]:
            self.nears[o].start()

    def forward(self, which=None):
        for o in range(1, FAR) if which is None else which:
            self.nears[o].wait_recv()
            mine = self.part[self.rows(o, self.place.near), self.first : self.last].astype(F32)
            self.got_near[o] = (mine + self.got_near[o].astype(F32)).astype(BF)
            self.fars[o - 1].start()

    def total(self):
        self.nears[0].wait_recv()
        mine = self.part[self.rows(0, self.place.near), self.first : self.last].astype(F32)
        value = mine + self.got_near[0].astype(F32)
        for o in range(1, FAR):
            self.fars[o - 1].wait_recv()
            value = value + self.got_far[o - 1].astype(F32)
        return value

    def finish(self):
        for copy in self.fars + self.nears:
            copy.wait_send()


def split_heads(cfg, value, shift, out, image, at, size):
    for h in range(cfg.heads):
        part = value[:, shift + h * HEAD_DIM : shift + (h + 1) * HEAD_DIM]
        out[h][rows_at(image * cfg.tokens + at, size), :HEAD_DIM] = part.astype(BF)


def attend_forward(cfg, image, head, q, k, v, mixed, shift, lse):
    rows = rows_at(image * cfg.tokens, cfg.tokens)
    values = v[head, rows, :].astype(F32).T.astype(BF)[:HEAD_DIM]
    scores = dot(k[head, rows, :], q[head, rows, :], NT)
    top = jnp.max(scores, axis=0, keepdims=True)
    probs = jnp.exp2((scores - top) * SCALE_TWO)
    total = jnp.sum(probs, axis=0, keepdims=True)
    out = dot(values, probs.astype(BF), NN) * (1.0 / total)
    start = shift + head * HEAD_DIM
    mixed[rows, start : start + HEAD_DIM] = out.T.astype(BF)
    lse[head, image : image + 1, :] = top * SCALE_TWO + jnp.log2(total)


def attend_backward(cfg, image, head, q, k, v, d_mixed, lse, d_proj, bias_sums):
    rows = rows_at(image * cfg.tokens, cfg.tokens)
    keys, query, d_out = k[head, rows, :], q[head, rows, :], d_mixed[head][...]
    keys_t = keys.astype(F32).T.astype(BF)[:HEAD_DIM]
    scores = dot(keys, query, NT)
    probs = jnp.exp2(scores * SCALE_TWO - lse[head, image : image + 1, :])
    d_values = dot(probs.astype(BF), d_out, NN)[:, :HEAD_DIM]
    d_probs = dot(v[head, rows, :], d_out, NT)
    delta = jnp.sum(probs * d_probs, axis=0, keepdims=True)
    d_scores = (probs * (d_probs - delta)).astype(BF)
    d_keys = dot(d_scores, query, NN)[:, :HEAD_DIM] * SCALE
    d_query = (dot(keys_t, d_scores, NN) * SCALE).T
    for which, value in ((0, d_query), (1, d_keys), (2, d_values)):
        start = (3 * head + which) * HEAD_DIM
        d_proj[rows, start : start + HEAD_DIM] = value.astype(BF)
    for row, value in ((0, d_query), (1, d_values)):
        bias_sums[row : row + 1, head * HEAD_DIM : (head + 1) * HEAD_DIM] += column_sum(value)


def keep_row_mask(cfg, place, length):
    at = lax.broadcasted_iota(jnp.int32, (cfg.seq, 1), 0) + place.t * cfg.seq
    return (at < length).astype(F32)


def key_bias(cfg, length):
    index = lax.broadcasted_iota(jnp.int32, (cfg.tokens, 1), 0)
    rank = jnp.zeros_like(index)
    for r in range(1, RANKS):
        rank = rank + (index >= r * cfg.slab).astype(jnp.int32)
    within = index - rank * cfg.slab
    at = rank * cfg.seq + within
    return jnp.where((within < cfg.seq) & (at < length), 0.0, NEG_FILL)


def layer_kernel(cfg, names, *refs):
    r = types.SimpleNamespace(**dict(zip(names, refs)))
    place = Place(cfg.extra)
    images = range(cfg.images)
    heads, units, hc = cfg.heads, cfg.units, cfg.head_cols
    half, third = cfg.tokens // 2, cfg.width // 3
    gather_sems = (r.wg_far_s, r.wg_far_r, r.wg_near_s, r.wg_near_r)
    scatter_sems = (r.ws_far_s, r.ws_far_r, r.ws_near_s, r.ws_near_r)
    q, k, v = (r.qkv.at[pl.ds(n * heads, heads)] for n in range(3))
    own_qkv, own_out, own_up, own_down = r.d_qkv, r.d_out, r.d_up, r.d_down
    resid, cotangent = r.block, r.gradient
    w = r.w
    out_at, up_at, wide = 3 * hc, 4 * hc, -(-units // LANES) * LANES
    edge = units % LANES
    out_first = out_at // LANES * LANES
    out_shift = out_at - out_first
    down_first = up_at + wide - LANES
    out_window, up_window = slice(out_first, up_at), slice(up_at, up_at + wide)
    tiles = range(wide // LANES)

    def lanes(value):
        return lax.broadcasted_iota(jnp.int32, value.shape, 1)

    def to_window(value):
        first, last = value[0], value[-1]
        moved = jnp.where(lanes(last) < 2 * edge, pltpu.roll(first, edge, 1), 0.0)
        head = jnp.where(lanes(first) < edge, 0.0, first)
        return [head, *value[1:-1], jnp.where(lanes(last) < edge, last, moved)]

    def from_window(value):
        first, last = value[0], value[-1]
        moved = pltpu.roll(last, LANES - edge, 1)
        head = jnp.where(lanes(first) < edge, moved, first)
        return [head, *value[1:-1], jnp.where(lanes(last) < edge, last, 0.0)]
    h_one, mlp = r.page_one, r.page_one
    h_two, d_proj = r.page_two, r.page_two
    grad, d_pre, h_one_again = r.page_three, r.page_three, r.page_three
    act = r.page_four
    part_down, part_qkv = r.part, r.part
    d_mixed = [r.page_four.at[pl.ds(0, cfg.tokens), pl.ds(h * LANES, LANES)] for h in range(heads)]

    def local(src, dst, n):
        copy = pltpu.make_async_copy(src, dst, r.local_sem.at[n])
        copy.start()
        return copy

    load_qkv = local(r.own_qkv_hbm, own_qkv, 0)
    load_x = local(r.x_hbm, r.x, 1)
    load_out = local(r.own_out_hbm, own_out, 2)
    load_up = local(r.own_up_hbm, own_up, 3)
    load_cot = local(r.cotangent_hbm, cotangent, 4)
    load_down = local(r.own_down_hbm, own_down, 5)

    place.greet(both=True)
    bounds = [n * LANES for n in (0, 4, 7, 9, 14, 16, 18, 22, 24)] + [w.shape[1]]
    gathers = [
        WeightGather(cfg, place, w, (first, last), gather_sems, n)
        for n, (first, last) in enumerate(zip(bounds[:-1], bounds[1:]))
    ]
    g_heads, g_out, g_up, g_down = gathers[0:2], gathers[2], gathers[3:6], gathers[6:9]
    here = rows_at((place.far * NEAR + place.near) * cfg.block, cfg.block)
    load_qkv.wait()
    load_out.wait()
    columns = [own_qkv[n][:, h * HEAD_DIM : (h + 1) * HEAD_DIM] for h in range(heads) for n in range(3)]
    w[here, :up_at] = jnp.concatenate(columns + [own_out[...]], axis=1).astype(BF)
    g_heads[0].start()
    g_heads[0].start_near()

    one = [TokenGather(cfg, place, h_one, r.tg_s.at[0], r.tg_r.at[0], i) for i in images]
    cot = [TokenGather(cfg, place, grad, r.tg_s.at[1], r.tg_r.at[1], i) for i in images]
    two = [TokenGather(cfg, place, h_two, r.tg_s.at[2], r.tg_r.at[2], i) for i in images]
    dres = [TokenGather(cfg, place, r.d_res, r.tg_s.at[3], r.tg_r.at[3], i) for i in images]
    load_x.wait()
    for i in images:
        rows, _ = standardize(r.x[i])
        value = rows * r.norm_one[0:1, :] + r.norm_one[1:2, :]
        h_one[slab_rows(cfg, i, place.t), :] = padded_slab(value, cfg.slab)
        one[i].start()

    lane = lax.broadcasted_iota(jnp.int32, (cfg.tokens, LANES), 1)
    flag = jnp.where(lane == HEAD_DIM, 1.0, 0.0)
    r.mixed[:, :out_shift] = jnp.zeros((cfg.images * cfg.tokens, out_shift), BF)
    for i in images:
        rows = rows_at(i * cfg.tokens, cfg.tokens)
        bias = jnp.where(lane == HEAD_DIM, key_bias(cfg, r.lengths[i]), 0.0).astype(BF)
        for h in range(heads):
            q[h, rows, :] = flag.astype(BF)
            k[h, rows, :] = bias
            v[h, rows, :] = jnp.zeros((cfg.tokens, LANES), BF)

    load_cot.wait()
    down_bias_sum = jnp.zeros((1, cfg.width), F32)
    for i in images:
        value = cotangent[i] * keep_row_mask(cfg, place, r.lengths[i])
        cotangent[i] = value
        down_bias_sum = down_bias_sum + column_sum(value)
        grad[slab_rows(cfg, i, place.t), :] = padded_slab(value, cfg.slab)
    r.vector[3:4, :] = down_bias_sum

    load_up.wait()
    load_down.wait()
    rest = jnp.zeros((cfg.block, w.shape[1] - up_at - 2 * units), own_up.dtype)
    columns = [own_up[...], own_down[:, edge:], own_down[:, :edge], rest]
    w[here, up_at:] = jnp.concatenate(columns, axis=1).astype(BF)

    def advance(n):
        gathers[n].forward([0])
        if n == 0:
            gathers[1].start()
        gathers[n].forward([1, 2])
        if n + 2 < len(gathers):
            gathers[n + 2].start()
        if n + 1 < len(gathers):
            gathers[n + 1].start_near()

    advance(0)
    one[0].forward()
    for i in images[1:]:
        one[i].forward()
    for i in images:
        cot[i].start()
    g_heads[0].wait()

    def project(i, pair):
        @pl.loop(0, 2)
        def _(j):
            at = pl.multiple_of(j * half, 16)
            value = h_one[rows_at(i * cfg.tokens + at, half), :]
            rows = rows_at(i * cfg.tokens + at, half)
            first = pair * 3 * LANES
            proj = dot(value, w[:, first : first + 4 * LANES], NN)
            for h in (2 * pair, 2 * pair + 1):
                bias = r.qv_bias[:, h * HEAD_DIM : (h + 1) * HEAD_DIM]
                for n, out in enumerate((q, k, v)):
                    start = (3 * h + n) * HEAD_DIM - first
                    part = proj[:, start : start + HEAD_DIM]
                    if n != 1:
                        part = part + bias[n // 2 : n // 2 + 1, :]
                    out[h, rows, :HEAD_DIM] = part.astype(BF)

    def scatters(core, row, sems):
        return [TokenScatter(place, i, core, row, r.ts_row_out, sems) for i in images]

    attns = scatters(r.tsa_core, r.tsa_row, (r.ts_cs.at[0], r.ts_cr.at[0], r.ts_rs.at[0], r.ts_rr.at[0]))
    backs = scatters(r.tsa_core, r.tsa_row, (r.ts_cs.at[1], r.ts_cr.at[1], r.ts_rs.at[1], r.ts_rr.at[1]))
    feeds = scatters(r.tsa_core, r.tsa_row, (r.ts_cs.at[2], r.ts_cr.at[2], r.ts_rs.at[2], r.ts_rr.at[2]))
    sums = scatters(r.tsb_core, r.tsb_row, (r.ts_cs.at[3], r.ts_cr.at[3], r.ts_rs.at[3], r.ts_rr.at[3]))
    def pump_forward(i, h):
        if i == 0 and h == 1:
            advance(1)
        if i == 1 and h == 1:
            advance(2)
            g_heads[1].wait()
        if i == 0 and h == 2:
            cot[0].forward()
        if i == 0 and h == 3:
            g_out.wait()
        if i == 1 and h == 2:
            advance(3)

    for pair in range(2):
        for i in images:
            if pair == 0:
                one[i].wait()
            project(i, pair)
            for h in (2 * pair, 2 * pair + 1):
                attend_forward(cfg, i, h, q, k, v, r.mixed, out_shift, r.lse)
                pump_forward(i, h)
            if pair == 1:
                attns[i].run(
                    lambda rank: dot(r.mixed[slab_rows(cfg, i, rank), :], w[:, out_window], NT),
                    r.ts_core_out,
                    r.keep,
                )
    spill_h_one = local(h_one, r.h_one_hbm, 6)
    spill_qkv = local(r.qkv, r.qkv_hbm, 7)

    for c in cot[1:]:
        c.forward()
    advance(4)
    for i in images:
        attn = attns[i].total(r.keep[1 + i])[: cfg.seq]
        value = r.x[i] + attn + r.out_bias[...][None]
        resid[i] = value
        rows, _ = standardize(value)
        value = rows * r.norm_two[0:1, :] + r.norm_two[1:2, :]
        h_two[slab_rows(cfg, i, place.t), :] = padded_slab(value, cfg.slab)
        two[i].start()
        if i == 0:
            advance(5)
    for item in attns:
        item.finish()
    for g in g_up:
        g.wait()
    advance(6)
    spill_qkv.wait()
    up_bias = jnp.concatenate([r.up_bias[...][None], jnp.zeros((1, wide - units), F32)], axis=1)

    def split(value):
        return [value[:, n * LANES : (n + 1) * LANES] for n in range(value.shape[1] // LANES)]

    def unit_block(i, rank):
        rows = slab_rows(cfg, i, rank)
        pre = dot(h_two[rows, :], w[:, up_window], NN) + up_bias
        value, slope = gelu_pair(pre)
        for n, part in enumerate(to_window(split(value))):
            act[rows, n * LANES : (n + 1) * LANES] = part.astype(BF)
        for n, part in enumerate(to_window(split(slope))):
            r.qkv[n, rows, :] = part.astype(BF)

    for i in images:
        unit_block(i, place.t)
        two[i].wait_core()
        unit_block(i, place.t_core)
        if i == 0:
            advance(7)
        two[i].forward()
        unit_block(i, place.t_row)
        two[i].wait()
        unit_block(i, place.t_both)
        if i == 0:
            advance(8)

    for c in cot:
        c.wait()
        c.finish()

    def weight_part(part, left, right, first=0):
        last = first + right.shape[1]

        @pl.loop(0, 3)
        def _(j):
            cols = pl.ds(pl.multiple_of(j * third, LANES), third)
            part[rows_at(j * third, third), first:last] = dot(left[:, cols], right, TN).astype(BF)

    def weight_scatter(n, part, first, near, far):
        return WeightScatter(cfg, place, part, first, near, far, scatter_sems, n)

    spare = down_first + LANES
    down_half = (wide + LANES) // 2 // LANES * LANES
    s_down = [
        weight_scatter(0, part_down, LANES, r.down_near_0, r.down_far_0),
        weight_scatter(6, part_down, down_half, r.down_near_1, r.down_far_1),
    ]
    s_up = weight_scatter(1, w, up_at, r.up_near, r.up_far)
    s_out = weight_scatter(2, w, spare + LANES, r.out_near, r.out_far)
    cuts = {1: (0, 3 * LANES), 2: (3 * LANES, 5 * LANES), 3: (5 * LANES, out_first + LANES)}
    s_qkv = {
        h: weight_scatter(2 + h, part_qkv, cuts[h][0], getattr(r, f"qkv_near_{h}"), getattr(r, f"qkv_far_{h}"))
        for h in cuts
    }

    weight_part(part_down, grad, act[:, :down_half])
    s_down[0].start()
    weight_part(part_down, grad, act[:, down_half:], down_half)
    s_down[1].start()
    r.vector[4:5, :] = jnp.zeros((1, cfg.width), F32)

    def d_pre_part(i, part):
        first = part[0] * LANES

        @pl.loop(0, 2)
        def _(j):
            rows = rows_at(i * cfg.tokens + j * half, half)
            slope = jnp.concatenate([r.qkv[n, rows, :] for n in part], axis=1)
            value = dot(grad[rows, :], w[:, down_first + first : down_first + first + slope.shape[1]], NN)
            value = value * slope.astype(F32)
            r.vector[4:5, first : first + slope.shape[1]] += column_sum(value)
            for n, column in zip(part, split(value)):
                r.qkv[n, rows, :] = column.astype(BF)

    def d_pre_place(i):
        @pl.loop(0, 2)
        def _(j):
            rows = rows_at(i * cfg.tokens + j * half, half)
            ends = from_window([r.qkv[0, rows, :].astype(F32), r.qkv[tiles[-1], rows, :].astype(F32)])
            for n in tiles[1:-1]:
                d_pre[rows, n * LANES : (n + 1) * LANES] = r.qkv[n, rows, :]
            d_pre[rows, :LANES] = ends[0].astype(BF)
            d_pre[rows, wide - LANES :] = ends[1].astype(BF)

    g_down[0].wait()
    g_down[1].wait()
    for i in images:
        d_pre_part(i, tiles[:7])
        if i == 0:
            g_down[2].wait()
            s_down[0].forward([1])
        d_pre_part(i, tiles[7:])
        d_pre_place(i)
        if i == 0:
            s_down[0].forward([2])
        if i == 1:
            s_down[1].forward([1])
        backs[i].run(
            lambda rank: dot(d_pre[slab_rows(cfg, i, rank), :], w[:, up_window], NT),
            r.ts_core_out,
            r.keep,
        )
        s_down[i].forward([3 - i])
    fetch_qkv = local(r.qkv_hbm, r.qkv, 8)

    def feed(i):
        @pl.loop(0, 2)
        def _(j):
            rows = rows_at(i * cfg.tokens + j * half, half)
            value = dot(act[rows, :LANES], r.edge[...], NT)
            value = value + dot(act[rows, LANES:], w[:, down_first + LANES :], NT)
            mlp[rows, :] = value.astype(BF)

    def through_norm_two(i):
        d_normed = backs[i].total(r.keep[1 + i])[: cfg.seq]
        rows, inverse = standardize(resid[i])
        value = cotangent[i] + norm_backward(d_normed, rows, inverse, r.norm_two[0:1, :])
        r.gradient[i] = value
        r.d_res[slab_rows(cfg, i, place.t), :] = padded_slab(value, cfg.slab)
        dres[i].start()
        return column_sum(value), column_sum(d_normed * rows), column_sum(d_normed)

    for item in two + gathers:
        item.finish()
    r.edge[...] = w[:, down_first : down_first + LANES]
    weight_part(w, h_two, d_pre[...], up_at)
    w[:, down_first : down_first + LANES] = (
        w[:, down_first : down_first + LANES].astype(F32) + part_down[:, :LANES].astype(F32)
    ).astype(BF)
    s_up.start()
    s_down[1].forward([3])
    vectors = [through_norm_two(0)]
    for c in one:
        c.finish()
    spill_h_one.wait()
    fetch_h_one = local(r.h_one_hbm, h_one_again, 9)
    for i in images:
        feed(i)
    for i in images[1:]:
        vectors.append(through_norm_two(i))
    for item in backs:
        item.finish()
    s_up.forward([1])
    for n in range(3):
        r.vector[n : n + 1, :] = sum(entry[n] for entry in vectors)
    row = r.vector[4:5, :]
    r.vector[4:5, :] = jnp.concatenate(from_window(split(row)), axis=1)
    early = VectorSum(place, r.early_far, r.early_near, r.early_rank, r.early_s, r.early_r)
    r.vector[5:8, :] = jnp.zeros((3, cfg.width), F32)
    early.start(r.vector[...])
    r.bias_sums[...] = jnp.zeros_like(r.bias_sums)
    for part in d_mixed:
        part[...] = jnp.zeros((cfg.tokens, LANES), BF)
    d_proj[:, out_at : out_first + LANES] = jnp.zeros((cfg.images * cfg.tokens, LANES - out_shift), BF)
    for i in images:
        dres[i].wait_core()
        feeds[i].send_parts(cfg, mlp)
    dres[0].forward()
    feeds[0].pass_parts(cfg, mlp)
    fetch_qkv.wait()
    dres[0].wait()

    def qkv_part(h):
        first, last = cuts[h]
        weight_part(part_qkv, h_one_again, d_proj[:, first:last], first)
        if last > out_first:
            part_qkv[:, out_first:last] = (
                part_qkv[:, out_first:last].astype(F32) + w[:, spare : spare + LANES].astype(F32)
            ).astype(BF)
        s_qkv[h].start()

    for i in images:
        @pl.loop(0, 2)
        def _(j):
            at = pl.multiple_of(j * half, 16)
            value = dot(r.d_res[rows_at(i * cfg.tokens + at, half), :], w[:, out_window], NN)
            split_heads(cfg, value, out_shift, d_mixed, 0, at, half)

        for h in range(heads):
            attend_backward(cfg, i, h, q, k, v, d_mixed, r.lse, d_proj, r.bias_sums)
            if i == 0 and h == 0:
                s_up.forward([2])
            if i == 0 and h == 2:
                s_up.forward([3])
            if i == 0 and h == 3:
                dres[1].forward()
            if i == 1 and h == 0:
                value = jnp.concatenate([part.total() for part in s_down], axis=1)
                r.d_down[:, LANES:] = value[:, : units - LANES]
                r.d_down[:, :edge] = value[:, units - LANES : units - LANES + edge]
                for part in s_down:
                    part.finish()
                fetch_h_one.wait()
            if i == 1 and h == 1:
                early.step()
            if i == 1 and h in (1, 2):
                qkv_part(h)
            if i == 1 and h == 1:
                s_out.forward([1, 2])
            if i == 1 and h == 2:
                s_out.forward([3])
                early.last()
        sums[i].run(
            lambda rank: dot(
                d_proj[slab_rows(cfg, i, rank), : out_first + LANES], w[:, : out_first + LANES], NT
            ),
            r.ts_core_out,
            r.keep,
            None if i == 0 else lambda n: s_qkv[1].forward([1 + n]),
        )
        if i == 0:
            dres[1].wait()
            weight_part(w, r.d_res, r.mixed[...], spare)
            s_out.start()
    s_qkv[1].forward([3])
    qkv_part(3)
    feeds[1].pass_parts(cfg, mlp)
    s_qkv[2].forward()
    results = []

    def finish_block(i):
        value = feeds[i].total(mlp[slab_rows(cfg, i, place.t), :].astype(F32))
        r.block[i] = resid[i] + value[: cfg.seq] + r.down_bias[...][None]
        feeds[i].finish()
        results.append(local(r.block.at[i], r.block_out.at[i], 10 + i))

    finish_block(0)
    gain_sum = jnp.zeros((1, cfg.width), F32)
    shift_sum = jnp.zeros((1, cfg.width), F32)
    for i in images:
        d_normed = sums[i].total(r.keep[1 + i])[: cfg.seq]
        rows, inverse = standardize(r.x[i])
        r.gradient[i] = r.gradient[i] + norm_backward(d_normed, rows, inverse, r.norm_one[0:1, :])
        results.append(local(r.gradient.at[i], r.grad_input.at[i], 12 + i))
        gain_sum = gain_sum + column_sum(d_normed * rows)
        shift_sum = shift_sum + column_sum(d_normed)
    late = VectorSum(place, r.late_far, r.late_near, r.late_rank, r.late_s, r.late_r)
    pad = jnp.zeros((2, cfg.width - hc), F32)
    late.start(
        jnp.concatenate(
            [
                gain_sum,
                shift_sum,
                jnp.concatenate([r.bias_sums[...], pad], axis=1),
            ],
            axis=0,
        )
    )
    s_qkv[3].forward()
    value = s_up.total()
    r.d_up[...] = value[:, :units]
    r.d_down[:, edge:LANES] = value[:, units:]
    r.d_out[:, LANES - out_shift :] = s_out.total()
    r.early_all[...], r.early_dp[...] = early.total()
    late.step()
    finish_block(1)

    def place_heads(value, first, some):
        for h in some:
            for n in range(3):
                start = (3 * h + n) * HEAD_DIM - first
                r.d_qkv[n, :, h * HEAD_DIM : (h + 1) * HEAD_DIM] = value[:, start : start + HEAD_DIM]

    begun = jnp.concatenate([s_qkv[1].total(), s_qkv[2].total()], axis=1)
    place_heads(begun, 0, range(2))
    late.last()
    value = jnp.concatenate([begun[:, cuts[2][0] :], s_qkv[3].total()], axis=1)
    place_heads(value, cuts[2][0], range(2, heads))
    r.d_out[:, : LANES - out_shift] = value[:, out_at - cuts[2][0] :]
    r.late_all[...], r.late_dp[...] = late.total()
    for copy in results:
        copy.wait()
    for item in dres + sums + [s_up, s_out, early, late] + list(s_qkv.values()):
        item.finish()


def spread(kernel, cfg, inputs, outputs, scratch, collective_id, cost):
    names = list(inputs) + list(outputs) + list(scratch)
    space = {"v": pltpu.VMEM, "s": pltpu.SMEM, "h": pl.ANY}
    result = pl.pallas_call(
        functools.partial(kernel, cfg, names),
        out_shape=tuple(jax.ShapeDtypeStruct(shape, dtype) for _, shape, dtype in outputs.values()),
        in_specs=[pl.BlockSpec(memory_space=space[where]) for where, _ in inputs.values()],
        out_specs=tuple(pl.BlockSpec(memory_space=space[where]) for where, _, _ in outputs.values()),
        scratch_shapes=list(scratch.values()),
        compiler_params=pltpu.CompilerParams(
            collective_id=collective_id, has_side_effects=True, vmem_limit_bytes=VMEM_BYTES
        ),
        cost_estimate=pl.CostEstimate(flops=cost, bytes_accessed=cost // 1000, transcendentals=0),
    )(*[value for _, value in inputs.values()])
    return dict(zip(outputs, result))


def dma(*shape):
    return pltpu.SemaphoreType.DMA(shape)


class VectorSum:
    def __init__(self, place, far, near, rank, send, recv):
        self.place, self.far, self.near, self.rank = place, far, near, rank
        mine = far.at[place.far]
        self.fars = [remote(mine, mine, send.at[o], recv.at[o], place.far_peers[o]) for o in range(FAR - 1)]
        mine = near.at[place.near]
        at = FAR - 1
        self.nears = [remote(mine, mine, send.at[at], recv.at[at], place.near_peer)]
        mine = rank.at[place.t]
        self.ranks = []
        for peer in (place.core_peer, place.row_peer, place.both_peer):
            at += 1
            self.ranks.append(remote(mine, mine, send.at[at], recv.at[at], peer))

    def start(self, value):
        self.far[self.place.far] = value
        for copy in self.fars:
            copy.start()

    def step(self):
        for copy in self.fars:
            copy.wait_recv()
        self.near[self.place.near] = (self.far[0] + self.far[1]) + (self.far[2] + self.far[3])
        self.nears[0].start()

    def last(self):
        self.nears[0].wait_recv()
        self.rank[self.place.t] = self.near[0] + self.near[1]
        for copy in self.ranks:
            copy.start()

    def total(self):
        for copy in self.ranks:
            copy.wait_recv()
        whole = (self.rank[0] + self.rank[1]) + (self.rank[2] + self.rank[3])
        return whole, self.rank[self.place.t]

    def finish(self):
        for copy in self.fars + self.nears + self.ranks:
            copy.wait_send()


def call_layer(cfg, inputs):
    all_tokens = cfg.images * cfg.tokens
    w, hc, n = cfg.width, cfg.head_cols, cfg.images
    units_p, hc_p, three_p = (-(-size // LANES) * LANES for size in (cfg.units, hc, 3 * hc))
    qkv = (3 * cfg.heads, all_tokens, LANES)
    local = (n, cfg.seq, w)
    page = (all_tokens, w)
    slabs = (n, cfg.slab, w)
    vec = (8, w)
    outputs = dict(
        block_out=("h", local, F32),
        grad_input=("h", local, F32),
        d_qkv=("v", (3, cfg.block, hc), F32),
        d_out=("v", (cfg.block, hc), F32),
        d_up=("v", (cfg.block, cfg.units), F32),
        d_down=("v", (cfg.block, cfg.units), F32),
        early_all=("v", vec, F32),
        early_dp=("v", vec, F32),
        late_all=("v", (4, w), F32),
        late_dp=("v", (4, w), F32),
        h_one_hbm=("h", page, BF),
        qkv_hbm=("h", qkv, BF),
    )
    scratch = dict(
        w=pltpu.VMEM((w, 4 * hc - LANES + 2 * units_p), BF),
        edge=pltpu.VMEM((w, LANES), BF),
        block=pltpu.VMEM(local, F32),
        gradient=pltpu.VMEM(local, F32),
        x=pltpu.VMEM(local, F32),
        page_one=pltpu.VMEM(page, BF),
        page_two=pltpu.VMEM(page, BF),
        page_three=pltpu.VMEM(page, BF),
        page_four=pltpu.VMEM(page, BF),
        d_res=pltpu.VMEM(page, BF),
        qkv=pltpu.VMEM(qkv, BF),
        mixed=pltpu.VMEM((all_tokens, hc_p), BF),
        lse=pltpu.VMEM((cfg.heads, n, cfg.tokens), F32),
        bias_sums=pltpu.VMEM((2, hc), F32),
        vector=pltpu.VMEM(vec, F32),
        tsa_core=pltpu.VMEM((n, 2) + slabs[1:], BF),
        tsa_row=pltpu.VMEM(slabs, BF),
        tsb_core=pltpu.VMEM((n, 2) + slabs[1:], BF),
        tsb_row=pltpu.VMEM(slabs, BF),
        ts_core_out=pltpu.VMEM((n, 2) + slabs[1:], BF),
        ts_row_out=pltpu.VMEM(slabs, BF),
        keep=pltpu.VMEM((1 + n,) + slabs[1:], F32),
        part=pltpu.VMEM((w, w), BF),
        **{
            f"down_{side}_{n}": pltpu.VMEM((count, cfg.block, (units_p - LANES) // 2), BF)
            for n in range(2)
            for side, count in (("near", FAR), ("far", FAR - 1))
        },
        up_near=pltpu.VMEM((FAR, cfg.block, units_p), BF),
        up_far=pltpu.VMEM((FAR - 1, cfg.block, units_p), BF),
        out_near=pltpu.VMEM((FAR, cfg.block, hc_p - LANES), BF),
        out_far=pltpu.VMEM((FAR - 1, cfg.block, hc_p - LANES), BF),
        **{
            f"qkv_{side}_{h}": pltpu.VMEM((count, cfg.block, size), BF)
            for h, size in ((1, 3 * LANES), (2, 2 * LANES), (3, three_p - 5 * LANES))
            for side, count in (("near", FAR), ("far", FAR - 1))
        },
        early_far=pltpu.VMEM((FAR,) + vec, F32),
        early_near=pltpu.VMEM((NEAR,) + vec, F32),
        early_rank=pltpu.VMEM((RANKS,) + vec, F32),
        late_far=pltpu.VMEM((FAR, 4, w), F32),
        late_near=pltpu.VMEM((NEAR, 4, w), F32),
        late_rank=pltpu.VMEM((RANKS, 4, w), F32),
        early_s=dma(FAR + 3),
        early_r=dma(FAR + 3),
        late_s=dma(FAR + 3),
        late_r=dma(FAR + 3),
        wg_far_s=dma(9, FAR - 1),
        wg_far_r=dma(9, FAR - 1),
        wg_near_s=dma(9, FAR),
        wg_near_r=dma(9, FAR),
        ws_far_s=dma(7, FAR - 1),
        ws_far_r=dma(7, FAR - 1),
        ws_near_s=dma(7, FAR),
        ws_near_r=dma(7, FAR),
        tg_s=dma(4, n, 3),
        tg_r=dma(4, n, 3),
        ts_cs=dma(4, n, 2),
        ts_cr=dma(4, n, 2),
        ts_rs=dma(4, n),
        ts_rr=dma(4, n),
        local_sem=dma(14),
    )
    return spread(layer_kernel, cfg, inputs, outputs, scratch, 0, 60 * 10**9)


def adamw(param, grad, mom, var, rate, decay):
    mom_new = BETA_ONE * mom + (1.0 - BETA_ONE) * grad
    var_new = BETA_TWO * var + (1.0 - BETA_TWO) * grad * grad
    mom_hat = mom_new / (1.0 - BETA_ONE**STEP)
    var_hat = var_new / (1.0 - BETA_TWO**STEP)
    change = mom_hat / (jnp.sqrt(var_hat) + ADAM_EPS)
    return (param - rate * (change + decay * param), mom_new, var_new)


MATRICES = {1: "qkv", 3: "out", 6: "up", 8: "down"}


def update_kernel(cfg, *refs):
    params, moms, varis = refs[0:10], refs[10:20], refs[20:30]
    grads = dict(zip(("qkv", "out", "up", "down", "early_all", "early_dp", "late_all", "late_dp"), refs[30:38]))
    streams, outs = refs[38:40], refs[40:]
    for source, target in zip(streams, outs[:2]):
        target[...] = source[...]
    outs = outs[2:]

    def step(n, grad, rate, decay):
        new = adamw(params[n][...], grad, moms[n][...], varis[n][...], rate, decay)
        for kind, value in enumerate((grad,) + new):
            outs[10 * kind + n][...] = value

    for n, name in MATRICES.items():
        step(n, grads[name][...], RATE_MATRIX, DECAY)
    vectors = {
        0: grads["late_all"][0:2, :],
        2: grads["late_dp"][2:4, : cfg.head_cols],
        4: grads["early_all"][0, :],
        5: grads["early_all"][1:3, :],
        7: grads["early_dp"][4, : cfg.units],
        9: grads["early_all"][3, :],
    }
    for n, grad in vectors.items():
        step(n, grad, RATE_VECTOR, 0.0)


def call_update(cfg, shard, params, moms, varis, grads, block_out, grad_input):
    steps = 3 if shard % 24 == 0 and cfg.width % (3 * LANES) == 0 else 1
    rows = shard // steps

    def spec(value, n=None):
        shape = value.shape
        if n == "stream":
            return pl.BlockSpec(shape[:2] + (cfg.width // steps,), lambda i: (0, 0, i))
        if n not in MATRICES:
            zeros = (0,) * len(shape)
            return pl.BlockSpec(shape, lambda i: zeros)
        if len(shape) == 3:
            return pl.BlockSpec((shape[0], rows, shape[2]), lambda i: (0, i, 0))
        return pl.BlockSpec((rows, shape[1]), lambda i: (i, 0))

    order = ("qkv", "out", "up", "down", "early_all", "early_dp", "late_all", "late_dp")
    number = {name: n for n, name in MATRICES.items()}
    values = [*params, *moms, *varis, *(grads[name] for name in order), block_out, grad_input]
    ten = [spec(value, n) for n, value in enumerate(params)]
    in_specs = ten * 3 + [spec(grads[name], number.get(name)) for name in order]
    two = [spec(block_out, "stream"), spec(grad_input, "stream")]
    shapes = [block_out, grad_input] + list(params) * 4
    return pl.pallas_call(
        functools.partial(update_kernel, cfg),
        grid=(steps,),
        out_shape=tuple(jax.ShapeDtypeStruct(value.shape, F32) for value in shapes),
        in_specs=in_specs + two,
        out_specs=tuple(two + ten * 4),
        compiler_params=pltpu.CompilerParams(vmem_limit_bytes=VMEM_BYTES),
    )(*values)


def per_device(
    layer_input_stream,
    cotangent,
    valid_len,
    attention_norm_pair,
    qkv_weight,
    qv_bias,
    out_weight,
    out_bias,
    feedforward_norm_pair,
    up_weight,
    up_bias,
    down_weight,
    down_bias,
    *moments,
):
    moms, varis = moments[:10], moments[10:]
    images, seq, width = layer_input_stream.shape
    head_cols = qv_bias.shape[1]
    units = up_bias.shape[0]
    slab = -(-seq // 16) * 16
    extra = lax.axis_size("dp") // GROUPS
    cfg = types.SimpleNamespace(
        images=images,
        seq=seq,
        slab=slab,
        tokens=RANKS * slab,
        width=width,
        head_cols=head_cols,
        heads=head_cols // HEAD_DIM,
        units=units,
        block=width // GROUPS,
        extra=extra,
    )
    group = lax.axis_index("dp") // extra
    shard = width // (GROUPS * extra)

    def to_block(value, axis=0):
        if extra == 1:
            return value
        full = lax.all_gather(value, "dp", axis=axis, tiled=True)
        return lax.dynamic_slice_in_dim(full, group * cfg.block, cfg.block, axis)

    def from_block(value, axis=0):
        if extra == 1:
            return value
        shape = value.shape[:axis] + (width,) + value.shape[axis + 1 :]
        full = jnp.zeros(shape, value.dtype)
        full = lax.dynamic_update_slice_in_dim(full, value, group * cfg.block, axis)
        return lax.psum_scatter(full, "dp", scatter_dimension=axis, tiled=True)

    def over_rest(value):
        return value if extra == 1 else lax.psum(value, "dp") * (1.0 / GROUPS)

    def turned(values):
        attn, qkv, qv, out, out_b, mlp, up, up_b, down, down_b = values
        return (attn, qkv.transpose(1, 0, 2), qv, out.T, out_b, mlp, up, up_b, down.T, down_b)

    params = turned(
        (
            attention_norm_pair,
            qkv_weight,
            qv_bias,
            out_weight,
            out_bias,
            feedforward_norm_pair,
            up_weight,
            up_bias,
            down_weight,
            down_bias,
        )
    )
    moms, varis = turned(moms), turned(varis)
    layer = call_layer(
        cfg,
        dict(
            x_hbm=("h", layer_input_stream),
            cotangent_hbm=("h", cotangent),
            lengths=("s", valid_len),
            norm_one=("v", attention_norm_pair),
            norm_two=("v", feedforward_norm_pair),
            qv_bias=("v", qv_bias),
            out_bias=("v", out_bias),
            up_bias=("v", up_bias),
            down_bias=("v", down_bias),
            own_qkv_hbm=("h", to_block(params[1], 1)),
            own_out_hbm=("h", to_block(params[3])),
            own_up_hbm=("h", to_block(params[6])),
            own_down_hbm=("h", to_block(params[8])),
        ),
    )
    updated = call_update(
        cfg,
        shard,
        params,
        moms,
        varis,
        dict(
            qkv=from_block(layer["d_qkv"], 1),
            out=from_block(layer["d_out"]),
            up=from_block(layer["d_up"]),
            down=from_block(layer["d_down"]),
            **{
                name: over_rest(layer[name])
                for name in ("early_all", "early_dp", "late_all", "late_dp")
            },
        ),
        layer["block_out"],
        layer["grad_input"],
    )
    streams, rest = updated[:2], updated[2:]
    results = []
    for kind in range(4):
        results.extend(turned(rest[10 * kind : 10 * kind + 10]))
    return (*streams, *results)


def solution(mesh):
    stream = P("dp", "tensor", None)
    parameters = (
        P(),
        P("dp", None, "tensor"),
        P(None, "tensor"),
        P("tensor", "dp"),
        P(),
        P(),
        P("dp", "tensor"),
        P("tensor"),
        P("tensor", "dp"),
        P(),
    )
    return jax.shard_map(
        per_device,
        mesh=mesh,
        in_specs=(stream, stream, P("dp")) + parameters * 3,
        out_specs=(stream, stream) + parameters * 4,
        check_vma=False,
    )
```
